32 devices in a mesh: dp: 8 (over y, x, core), mp: 4 (over z).
Axes of the slice: x: 2, y: 2, z: 4, core: 2. Of those that a mesh axis runs over, the one named last changes fastest.
Arguments:
- frames: bfloat16 [8, 1536, 768], P('dp', 'mp'), may hold values from -6 to 6
- cotangent: bfloat16 [8, 1536, 768], P('dp', 'mp'), may hold values from -6 to 6
- segments: int32 [8, 1536], P('dp'), may hold values from 0 to 3, as said below
- padding: int32 [8, 1536], P('dp'), may hold values from 0 to 1, as said below
- skip_flag: int32 [8], P('dp'), may hold values from 0 to 1, as said below
- w_query: bfloat16 [768, 768], P(None, 'mp'), may hold values from -0.21875 to 0.21875
- b_query: float32 [768], P('mp'), may hold values from -3 to 3
- w_key: bfloat16 [768, 768], P(None, 'mp'), may hold values from -0.21875 to 0.21875
- w_value: bfloat16 [768, 768], P(None, 'mp'), may hold values from -0.21875 to 0.21875
- b_value: float32 [768], P('mp'), may hold values from -3 to 3
- w_out: bfloat16 [768, 768], P('mp'), may hold values from -3.5 to 3.5
- b_out: float32 [768], replicated, may hold values from -3 to 3
- gain_one: float32 [768], replicated, may hold values from 0.5 to 1.5
- shift_one: float32 [768], replicated, may hold values from -2 to 2
- w_up: bfloat16 [768, 3072], P(None, 'mp'), may hold values from -0.21875 to 0.21875
- b_up: float32 [3072], P('mp'), may hold values from -3 to 3
- w_down: bfloat16 [3072, 768], P('mp'), may hold values from -0.21875 to 0.21875
- b_down: float32 [768], replicated, may hold values from -3 to 3
- gain_two: float32 [768], replicated, may hold values from 0.5 to 1.5
- shift_two: float32 [768], replicated, may hold values from -2 to 2
Outputs:
- layer_out: bfloat16 [8, 1536, 768], P('dp', 'mp')
- frames_grad: bfloat16 [8, 1536, 768], P('dp', 'mp')
- w_query_grad: float32 [768, 768], P(None, 'mp')
- b_query_grad: float32 [768], P('mp')
- w_key_grad: float32 [768, 768], P(None, 'mp')
- w_value_grad: float32 [768, 768], P(None, 'mp')
- b_value_grad: float32 [768], P('mp')
- w_out_grad: float32 [768, 768], P('mp')
- b_out_grad: float32 [768], replicated
- gain_one_grad: float32 [768], replicated
- shift_one_grad: float32 [768], replicated
- w_up_grad: float32 [768, 3072], P(None, 'mp')
- b_up_grad: float32 [3072], P('mp')
- w_down_grad: float32 [3072, 768], P('mp')
- b_down_grad: float32 [768], replicated
- gain_two_grad: float32 [768], replicated
- shift_two_grad: float32 [768], replicated
The draws below stay inside these ranges and needn't reach their ends.
Inputs may be any that keep to these rules, and one draw needn't show every extreme that they name: `segments`: along each row the ids start at 0 and never fall; padded frames carry the id of the row's last utterance, which also has frames that are not padding. `padding`: in each row the frames marked 0 form its tail, fewer than 96 of them. `skip_flag`: one row is always marked 1; each other row is marked 1 with chance one in twenty.
All inputs are finite; a program needn't handle non-finite values.
Results may differ from the reference program's by a relative error of at most 0.02.
Values may be sent and summed in bfloat16 or wider, within the bound.
A program may use at most 128 MiB of HBM per device.

```python
import jax
import jax.numpy as jnp
from jax import lax

D = 768
HEADS = 12
HEAD_DIM = 64
FF = 3072
L = 1536
ROWS = 8


def segment_layout(key):
    base = jax.random.fold_in(key, 11)
    first_key, second_key, third_key = jax.random.split(base, 3)
    pad_counts = jax.random.randint(first_key, (ROWS,), 0, L // 16)
    short_lengths = jax.random.randint(second_key, (ROWS, 3), L // 48, L // 16)
    long_index = jax.random.randint(third_key, (ROWS,), 0, 4)
    valid_counts = L - pad_counts
    long_length = valid_counts - jnp.sum(short_lengths, 1)
    slots = jnp.arange(4)[None, :]
    before = jnp.clip(slots, 0, 2)
    after = jnp.clip(slots - 1, 0, 2)
    from_before = jnp.take_along_axis(short_lengths, jnp.broadcast_to(before, (ROWS, 4)), 1)
    from_after = jnp.take_along_axis(short_lengths, jnp.broadcast_to(after, (ROWS, 4)), 1)
    lengths_all = jnp.where(slots < long_index[:, None], from_before, jnp.where(slots == long_index[:, None], long_length[:, None], from_after))
    bounds = jnp.cumsum(lengths_all[:, :3], 1)
    positions = jnp.arange(L)
    seg_ids = jnp.sum((positions[None, :, None] >= bounds[:, None, :]).astype(jnp.int32), -1)
    pad_mask = (positions[None, :] < valid_counts[:, None]).astype(jnp.int32)
    return (seg_ids.astype(jnp.int32), pad_mask)


def draw_segments(key, part):
    return segment_layout(key)[0]


def draw_padding(key, part):
    return segment_layout(key)[1]


def draw_skip_flag(key, part):
    base = jax.random.fold_in(key, 23)
    rate_key, pick_key = jax.random.split(base, 2)
    chance = jax.random.randint(rate_key, (ROWS,), 0, 20)
    picked = jax.random.randint(pick_key, (), 0, ROWS)
    marked = (chance == 0) | (jnp.arange(ROWS) == picked)
    return marked.astype(jnp.int32)


def levels(key, dims, cuts, low, high):
    def one(dim, parts):
        steps = jax.random.uniform(jax.random.fold_in(jax.random.fold_in(key, 6), dim), (parts,), jnp.float32, low / len(cuts), high / len(cuts))
        return jnp.repeat(jnp.exp(steps), dims[dim] // parts).reshape((-1,) + (1,) * (len(dims) - dim - 1))

    loudness = one(*cuts[0])
    for cut in cuts[1:]:
        loudness = loudness * one(*cut)
    return loudness


def noise(rng, dims, scale, limit, cuts=(), held_as=jnp.bfloat16):
    loudness = levels(rng, dims, cuts, -0.22, 0.18) if cuts else 1.0
    drawn = jax.random.normal(rng, dims, jnp.float32) * scale * loudness
    return jnp.minimum(jnp.maximum(drawn, -limit), limit).astype(held_as)


def setup_inputs(seed: int = 0) -> dict:
    streams_of = jax.random.split(jax.random.key(seed), 21)
    return {
        "frames": noise(streams_of[0], (ROWS, L, D), 1.0, 6.0, ((0, 8), (1, 4))),
        "cotangent": noise(streams_of[1], (ROWS, L, D), 1.0, 6.0, ((0, 8), (1, 4))),
        "segments": draw_segments(jax.random.fold_in(streams_of[20], 71), 0),
        "padding": draw_padding(jax.random.fold_in(streams_of[20], 71), 0),
        "skip_flag": draw_skip_flag(jax.random.fold_in(streams_of[20], 71), 0),
        "w_query": noise(streams_of[5], (D, D), D ** -0.5, 0.21875, ((1, 4),)),
        "b_query": noise(streams_of[6], (D,), 0.5, 3.0, ((0, 4),), jnp.float32),
        "w_key": noise(streams_of[7], (D, D), D ** -0.5, 0.21875, ((1, 4),)),
        "w_value": noise(streams_of[8], (D, D), D ** -0.5, 0.21875, ((1, 4),)),
        "b_value": noise(streams_of[9], (D,), 0.5, 3.0, ((0, 4),), jnp.float32),
        "w_out": noise(streams_of[10], (D, D), (max(1, D // 256)) ** -0.5, 3.5, ((0, 4),)),
        "b_out": noise(streams_of[11], (D,), 0.5, 3.0, (), jnp.float32),
        "gain_one": jnp.clip(1.0 + 0.1 * jax.random.normal(streams_of[12], (D,), jnp.float32), 0.5, 1.5),
        "shift_one": noise(streams_of[13], (D,), 0.3, 2.0, (), jnp.float32),
        "w_up": noise(streams_of[14], (D, FF), D ** -0.5, 0.21875, ((1, 4),)),
        "b_up": noise(streams_of[15], (FF,), 0.5, 3.0, ((0, 4),), jnp.float32),
        "w_down": noise(streams_of[16], (FF, D), (FF // 4) ** -0.5, 0.21875, ((0, 4),)),
        "b_down": noise(streams_of[17], (D,), 0.5, 3.0, (), jnp.float32),
        "gain_two": jnp.clip(1.0 + 0.1 * jax.random.normal(streams_of[18], (D,), jnp.float32), 0.5, 1.5),
        "shift_two": noise(streams_of[19], (D,), 0.3, 2.0, (), jnp.float32),
    }


@jax.custom_vjp
def low(v):
    return lax.optimization_barrier(v.astype(jnp.bfloat16)).astype(jnp.float32)

@jax.custom_vjp
def low_back(v):
    return v

def low_keep(v):
    return (low(v), None)

def low_pass(kept, grad):
    return (grad,)

def back_keep(v):
    return (v, None)

def back_low(kept, grad):
    return (low(grad),)
low.defvjp(low_keep, low_pass)
low_back.defvjp(back_keep, back_low)

def both_round(values):
    return low(low_back(values))

def layer_norm(values, gain, shift):
    centered = values - lax.optimization_barrier(jnp.mean(values, -1, keepdims=True))
    spread = lax.optimization_barrier(jnp.mean(centered * centered, -1, keepdims=True))
    return centered * lax.rsqrt(spread + 1e-05) * gain + shift

def encoder_layer(params, frames_row, seg_row, pad_row, skip_row):
    w_query, b_query, w_key, w_value, b_value, w_out, b_out, gain_one, shift_one, w_up, b_up, w_down, b_down, gain_two, shift_two = params
    highest = lax.Precision.HIGHEST
    scale_factor = HEAD_DIM ** (-0.5)
    query_rows = both_round((jnp.dot(frames_row, w_query, precision=highest) + b_query) * scale_factor)
    key_rows = both_round(jnp.dot(frames_row, w_key, precision=highest))
    value_rows = both_round(jnp.dot(frames_row, w_value, precision=highest) + b_value)
    key_heads = key_rows.reshape(L, HEADS, HEAD_DIM)
    value_heads = value_rows.reshape(L, HEADS, HEAD_DIM)
    block_rows = min(512, L)
    block_count = L // block_rows
    query_blocks = query_rows.reshape(block_count, block_rows, HEADS, HEAD_DIM)
    seg_blocks = seg_row.reshape(block_count, block_rows)

    def attend_block(pieces):
        query_block, seg_block = pieces
        scores = low_back(jnp.einsum('qhd,khd->hqk', query_block, key_heads, precision=highest))
        allowed = (seg_block[:, None] == seg_row[None, :]) & (pad_row[None, :] == 1)
        scores = jnp.where(allowed[None], scores, -1e+30)
        weights = low(jax.nn.softmax(scores, axis=-1))
        return jnp.einsum('hqk,khd->qhd', weights, value_heads, precision=highest)
    mixed_rows = lax.map(jax.checkpoint(attend_block), (query_blocks, seg_blocks))
    mixed_rows = both_round(mixed_rows.reshape(L, D))
    attended = low_back(jnp.dot(mixed_rows, w_out, precision=highest) + b_out)
    normed = layer_norm(frames_row + attended, gain_one, shift_one)
    inner_rows = low_back(jnp.dot(low(normed), w_up, precision=highest) + b_up)
    activated = low(jax.nn.gelu(inner_rows, approximate=False))
    branch = low_back(jnp.dot(activated, w_down, precision=highest) + b_down)
    result = layer_norm(normed + branch, gain_two, shift_two)
    return jnp.where(skip_row == 1, frames_row, result)

def reference(frames, cotangent, segments, padding, skip_flag, w_query, b_query, w_key, w_value, b_value, w_out, b_out, gain_one, shift_one, w_up, b_up, w_down, b_down, gain_two, shift_two):
    params = tuple((param_entry.astype(jnp.float32) for param_entry in (w_query, b_query, w_key, w_value, b_value, w_out, b_out, gain_one, shift_one, w_up, b_up, w_down, b_down, gain_two, shift_two)))
    zero_grads = jax.tree.map(jnp.zeros_like, params)

    def one_row(grad_totals, row_items):
        frames_row, cot_row, seg_row, pad_row, skip_row = row_items
        result, pullback = jax.vjp(lambda param_set, frame_set: encoder_layer(param_set, frame_set, seg_row, pad_row, skip_row), params, frames_row.astype(jnp.float32))
        grad_params, grad_frames = pullback(cot_row.astype(jnp.float32))
        grad_totals = jax.tree.map(jnp.add, grad_totals, grad_params)
        return (grad_totals, (result.astype(jnp.bfloat16), grad_frames.astype(jnp.bfloat16)))
    grad_totals, outputs = lax.scan(one_row, zero_grads, (frames, cotangent, segments, padding, skip_flag))
    layer_out, frames_grad = outputs
    return (layer_out, frames_grad, grad_totals[0], grad_totals[1], grad_totals[2], grad_totals[3], grad_totals[4], grad_totals[5], grad_totals[6], grad_totals[7], grad_totals[8], grad_totals[9], grad_totals[10], grad_totals[11], grad_totals[12], grad_totals[13], grad_totals[14])
```

```python
import functools

import jax
import jax.numpy as jnp
from jax import lax
from jax.experimental import pallas as pl
from jax.experimental.pallas import tpu as pltpu
from jax.sharding import PartitionSpec as P

HEAD_DIM = 64
F32, BF16 = jnp.float32, jnp.bfloat16
VMEM = pl.BlockSpec(memory_space=pltpu.VMEM)
SMEM = pl.BlockSpec(memory_space=pltpu.SMEM)
LIMIT = 60 << 20


def mm(a, b, ca=1, cb=0):
    return lax.dot_general(a, b, (((ca,), (cb,)), ((), ())), preferred_element_type=F32)


def split3(v):
    hi = v.astype(BF16)
    rest = v - hi.astype(F32)
    mid = rest.astype(BF16)
    low = (rest - mid.astype(F32)).astype(BF16)
    return hi, mid, low


def pad_rows(parts, rows, width):
    parts = [p.astype(F32) for p in parts]
    have = sum(p.shape[0] for p in parts)
    return jnp.concatenate(parts + [jnp.zeros((rows - have, width), F32)], 0).astype(BF16)


def project(x, w_t, w_pad, bias_col, v_row, k_mask, one_hot, rows, q_aug, k_aug, v_aug, k_t, v_t):
    width = w_t.shape[0] // 3
    heads = width // HEAD_DIM
    every = mm(w_t, x, 1, 1) + bias_col
    every = jnp.concatenate([every[:width] * HEAD_DIM**-0.5, every[width:]], 0).astype(BF16)
    for h in range(heads):
        q_aug[h, 0:HEAD_DIM, rows] = every[h * HEAD_DIM : (h + 1) * HEAD_DIM]
        q_aug[h, HEAD_DIM : HEAD_DIM + 16, rows] = one_hot
        q_aug[h, HEAD_DIM + 16 :, rows] = jnp.zeros((48, x.shape[0]), BF16)
        k_t[h, :, rows] = every[width + h * HEAD_DIM : width + (h + 1) * HEAD_DIM]
        v_t[h, :, rows] = every[2 * width + h * HEAD_DIM : 2 * width + (h + 1) * HEAD_DIM]
    both = mm(x, w_pad, 1, 1)
    for h in range(heads):
        k_aug[h, rows, :] = both[:, h * 128 : (h + 1) * 128].astype(BF16) + k_mask
        at = (heads + h) * 128
        v_aug[h, rows, :] = (both[:, at : at + 128] + v_row[:, h * 128 : (h + 1) * 128]).astype(BF16)


def attend(h, cols, q_aug, k_aug, v_t, stats):
    scores = mm(k_aug[h], q_aug[h, :, cols])
    peak = jnp.max(scores, 0, keepdims=True)
    raised = jnp.exp(scores - peak)
    summed = jnp.sum(raised, 0, keepdims=True)
    mixed = mm(v_t[h], raised.astype(BF16)) / summed
    stats[h, :, cols] = jnp.broadcast_to(peak + jnp.log(summed), (8, mixed.shape[1]))
    return mixed.astype(BF16)


def local_forward_kernel(
    x_ref, w_ref, bias_ref, vrow_ref, kmask_ref, hot_ref,
    mixed_ref, q_aug, k_aug, v_aug, k_t, v_t, stats, w_pad
):
    heads = q_aug.shape[0]
    width = heads * HEAD_DIM
    w_pad[...] = jnp.zeros_like(w_pad)
    for i in range(2):
        for h in range(heads):
            w_pad[(i * heads + h) * 128 : (i * heads + h) * 128 + HEAD_DIM] = w_ref[
                (i + 1) * width + h * HEAD_DIM : (i + 1) * width + (h + 1) * HEAD_DIM
            ]
    length = x_ref.shape[0]
    block = 384

    def step(i, _):
        rows = pl.ds(pl.multiple_of(i * block, block), block)
        project(
            x_ref[rows, :], w_ref[...], w_pad[...], bias_ref[...], vrow_ref[...], kmask_ref[rows, :],
            hot_ref[:, rows], rows, q_aug, k_aug, v_aug, k_t, v_t,
        )
        return 0

    lax.fori_loop(0, length // block, step, 0)

    def attend_step(i, _):
        cols = pl.ds(pl.multiple_of(i * block, block), block)
        for h in range(heads):
            mixed_ref[i, h * HEAD_DIM : (h + 1) * HEAD_DIM, :] = attend(h, cols, q_aug, k_aug, v_t, stats)
        return 0

    lax.fori_loop(0, length // block, attend_step, 0)


MESH = pl.DeviceIdType.MESH
CHUNKS = 3


class Place:
    def __init__(self):
        self.d, self.z = lax.axis_index("dp"), lax.axis_index("mp")
        d, z = self.d, self.z
        self.b = d % 2
        self.p = z + self.b * (3 - 2 * z)
        self.sib = d + 1 - 2 * self.b
        self.q = (d // 2) % 4
        self.base = d - d % 8
        self.primary = self.p < 2
        self.rb = z // 2
        self.row = d - self.b + self.rb
        self.pp = z + self.rb * (3 - 2 * z)
        self.far = (z + 2) % 4
        self.group = jnp.where(self.primary, z, self.far)

    def own_line(self, place):
        return place + self.b * (3 - 2 * place)

    def line(self, place):
        return place + self.rb * (3 - 2 * place)

    def chip(self, k):
        return self.base + 2 * ((self.q + k) % 4) + self.b

    def barrier(self):
        sem = pltpu.get_barrier_semaphore()
        others = [((self.d), (self.z + k) % 4) for k in (1, 2, 3)]
        others += [(self.sib, (self.z + k) % 4) for k in range(4)]
        others += [(self.chip(k), self.z) for k in (1, 2, 3)]
        others += [(self.base + 2 * ((self.q + k) % 4) + 1 - self.b, self.z) for k in (1, 2, 3)]
        for dp, mp in others:
            pl.semaphore_signal(sem, inc=1, device_id=(dp, mp), device_id_type=MESH)
        pl.semaphore_wait(sem, len(others))

    def send(self, src, dst, send_sem, recv_sem, dp, mp):
        pltpu.make_async_remote_copy(
            src_ref=src, dst_ref=dst, send_sem=send_sem, recv_sem=recv_sem, device_id=(dp, mp), device_id_type=MESH
        ).start()

    def sent(self, src, send_sem):
        pltpu.make_async_remote_copy(
            src_ref=src, dst_ref=src, send_sem=send_sem, recv_sem=send_sem, device_id=(self.sib, self.z), device_id_type=MESH
        ).wait_send()

    def got(self, dst, recv_sem):
        pltpu.make_async_remote_copy(
            src_ref=dst, dst_ref=dst, send_sem=recv_sem, recv_sem=recv_sem, device_id=(self.sib, self.z), device_id_type=MESH
        ).wait_recv()


def forward_kernel(
    frames, w_own, small_own, kmask_own, hot_own, w_up, w_down, w_out,
    x_all, w_t, mixed_heads, mixed_own, q_aug, k_aug, v_aug, k_t, stats, small_all, up_all, down_all, out_all,
    relay, v_t, w_pad, kmask, hot,
    small_s, small_r, mask_s, mask_r, wq_s, wq_r, x_s, x_r, relay_r, on_s, fwd_s, mix_s, mix_r, local,
    p1_s, p2_s, p3_s, w_r,
):
    at = Place()
    heads = q_aug.shape[0]
    width = heads * HEAD_DIM
    share = frames.shape[0]
    step_rows = share // CHUNKS
    quarter = w_own.shape[0] // 4
    at.barrier()
    primary = at.primary
    secondary = jnp.logical_not(primary)
    z = at.z

    def rows(ch):
        return pl.ds(ch * step_rows, step_rows)

    def piece(m, chip, core):
        if m == 2:
            n = w_out.shape[0] // 4
            half = w_out.shape[1] // 2
            return (pl.ds(pl.multiple_of(chip * n, 16), n), pl.ds(pl.multiple_of(core * half, 128), half))
        n = w_up.shape[0] // 8
        return (pl.ds(pl.multiple_of((2 * chip + core) * n, 16), n), slice(None))

    mats = ((w_up, up_all), (w_down, down_all), (w_out, out_all))

    wq_rows = pl.ds(pl.multiple_of(at.q * quarter, 16), quarter)
    first = jnp.where(at.p == 0, 1, at.p - 1)

    @pl.when(primary)
    def _():
        at.send(w_own.at[wq_rows], w_t.at[wq_rows], wq_s.at[0], wq_r.at[at.q], at.d, at.far)

    for ch in range(CHUNKS):
        @pl.when(at.p < 3)
        def _():
            at.send(frames.at[rows(ch)], x_all.at[z, rows(ch)], on_s.at[z, ch], x_r.at[z, ch], at.d, at.own_line(first))

        @pl.when(at.p == 3)
        def _():
            at.send(frames.at[rows(ch)], relay.at[rows(ch)], on_s.at[z, ch], relay_r.at[ch], at.d, at.own_line(2))

    @pl.when(primary)
    def _():
        at.send(kmask_own, kmask, mask_s.at[0], mask_r.at[0], at.sib, z)
        at.send(hot_own, hot, mask_s.at[1], mask_r.at[1], at.sib, z)
        pltpu.make_async_copy(kmask_own, kmask, local.at[0]).start()
        pltpu.make_async_copy(hot_own, hot, local.at[1]).start()
        pltpu.make_async_copy(w_own, w_t, local.at[2]).start()
        pltpu.make_async_copy(frames, x_all.at[z], local.at[3]).start()
        for ch in range(CHUNKS):
            at.send(frames.at[rows(ch)], x_all.at[z, rows(ch)], fwd_s.at[z, ch], x_r.at[z, ch], at.sib, z)

    for k in (1, 2, 3):
        to = (z + k) % 4
        at.send(small_own, small_all.at[z], small_s.at[k - 1], small_r.at[z], at.d, to)
    pltpu.make_async_copy(small_own, small_all.at[z], local.at[4]).start()
    for m, (src, dst) in enumerate(mats):
        pltpu.make_async_copy(src, dst.at[z], local.at[5 + m]).start()

    @pl.when(at.p == 2)
    def _():
        for ch in range(CHUNKS):
            at.got(relay.at[rows(ch)], relay_r.at[ch])
            at.send(relay.at[rows(ch)], x_all.at[at.own_line(3), rows(ch)], x_s.at[ch], x_r.at[at.own_line(3), ch], at.d, at.own_line(1))

    @pl.when(secondary)
    def _():
        at.got(w_t.at[wq_rows], wq_r.at[at.q])
        for k in (1, 2, 3):
            at.send(w_t.at[wq_rows], w_t.at[wq_rows], wq_s.at[k], wq_r.at[at.q], at.chip(k), z)
        at.got(kmask, mask_r.at[0])
        at.got(hot, mask_r.at[1])

    @pl.when(primary)
    def _():
        pltpu.make_async_copy(kmask_own, kmask, local.at[0]).wait()
        pltpu.make_async_copy(hot_own, hot, local.at[1]).wait()
        pltpu.make_async_copy(w_own, w_t, local.at[2]).wait()
        pltpu.make_async_copy(frames, x_all.at[z], local.at[3]).wait()

    pltpu.make_async_copy(small_own, small_all.at[z], local.at[4]).wait()
    for k in (1, 2, 3):
        at.got(small_all.at[(z + k) % 4], small_r.at[(z + k) % 4])

    @pl.when(secondary)
    def _():
        for k in (1, 2, 3):
            other = (at.q + k) % 4
            at.got(w_t.at[pl.ds(pl.multiple_of(other * quarter, 16), quarter)], wq_r.at[other])

    w_pad[...] = jnp.zeros_like(w_pad)
    for i in range(2):
        for h in range(heads):
            w_pad[(i * heads + h) * 128 : (i * heads + h) * 128 + HEAD_DIM] = w_t[
                (i + 1) * width + h * HEAD_DIM : (i + 1) * width + (h + 1) * HEAD_DIM
            ]

    def shard_of(k):
        place = jnp.where(at.pp == 0, k, jnp.where(k == 0, 1, jnp.where(k == 1, 2, jnp.where(k == 2, 0, 3))))
        return place, at.line(place)

    def gather_step(k, _):
        place, s = shard_of(k)
        for ch in range(CHUNKS):
            block = x_all.at[s, rows(ch)]

            @pl.when(jnp.logical_or(k > 0, secondary))
            def _():
                at.got(block, x_r.at[s, ch])

            @pl.when(jnp.logical_and(k > 0, primary))
            def _():
                @pl.when(jnp.logical_and(at.p == 1, place >= 2))
                def _():
                    at.send(block, block, on_s.at[s, ch], x_r.at[s, ch], at.d, at.own_line(0))

                at.send(block, block, fwd_s.at[s, ch], x_r.at[s, ch], at.sib, z)

        cols = pl.ds(pl.multiple_of(s * share, share), share)
        biases = jnp.transpose(small_all[at.group])
        project(
            x_all[s], w_t[...], w_pad[...], biases[: 3 * width, 1:2], small_all[at.group, 2:3, : heads * 128], kmask[cols, :],
            hot[:, cols], cols, q_aug, k_aug, v_aug, k_t, v_t,
        )
        return 0

    lax.fori_loop(0, 4, gather_step, 0)

    for m, (src, dst) in enumerate(mats):
        r, c = piece(m, at.q, at.b)
        for k in (1, 2, 3):
            at.send(src.at[r, c], dst.at[z, r, c], p1_s.at[m, k - 1], w_r.at[m, z, 2 * at.q + at.b], at.d, (z + k) % 4)

    def spread(m):
        dst = mats[m][1]
        r, c = piece(m, at.q, at.b)
        for k in (1, 2, 3):
            s = (z + k) % 4
            sem = w_r.at[m, s, 2 * at.q + at.b]
            at.got(dst.at[s, r, c], sem)
            for j in (1, 2, 3):
                at.send(dst.at[s, r, c], dst.at[s, r, c], p2_s.at[m, k - 1, j], sem, at.chip(j), z)
            at.send(dst.at[s, r, c], dst.at[s, r, c], p2_s.at[m, k - 1, 0], sem, at.sib, z)

    def attend_step(i, _):
        cols = pl.ds(pl.multiple_of(i * share, share), share)
        for h in range(heads):
            mixed_heads[i, h * HEAD_DIM : (h + 1) * HEAD_DIM, :] = attend(h, cols, q_aug, k_aug, v_t, stats)
        mine = jnp.logical_and(primary, i == z)
        block = mixed_own.at[pl.ds(pl.multiple_of(at.group * width, 64), width)]

        @pl.when(mine)
        def _():
            pltpu.make_async_copy(mixed_heads.at[i], block, mix_s.at[i]).start()

        @pl.when(jnp.logical_not(mine))
        def _():
            at.send(mixed_heads.at[i], block, mix_s.at[i], mix_r.at[at.group], at.row, i)

        @pl.when(i == 1)
        def _():
            spread(0)

        @pl.when(i == 3)
        def _():
            spread(1)
            spread(2)

        return 0

    lax.fori_loop(0, 4, attend_step, 0)

    for m, (_, dst) in enumerate(mats):
        for j in (1, 2, 3):
            chip = (at.q + j) % 4
            r, c = piece(m, chip, at.b)
            for k in (1, 2, 3):
                s = (z + k) % 4
                sem = w_r.at[m, s, 2 * chip + at.b]
                at.got(dst.at[s, r, c], sem)
                at.send(dst.at[s, r, c], dst.at[s, r, c], p3_s.at[m, j - 1, k - 1], sem, at.sib, z)

    for g in range(4):
        mine = jnp.logical_and(primary, z == g)
        block = mixed_own.at[pl.ds(g * width, width)]

        @pl.when(jnp.logical_not(mine))
        def _():
            at.got(block, mix_r.at[g])

    for m, (src, dst) in enumerate(mats):
        pltpu.make_async_copy(src, dst.at[z], local.at[5 + m]).wait()
        for j in range(4):
            chip = (at.q + j) % 4
            r, c = piece(m, chip, 1 - at.b)
            for k in (1, 2, 3):
                s = (z + k) % 4
                at.got(dst.at[s, r, c], w_r.at[m, s, 2 * chip + 1 - at.b])

    for i in range(4):
        mine = jnp.logical_and(primary, z == i)

        @pl.when(mine)
        def _():
            block = mixed_own.at[pl.ds(pl.multiple_of(at.group * width, 64), width)]
            pltpu.make_async_copy(mixed_heads.at[i], block, mix_s.at[i]).wait()

        @pl.when(jnp.logical_not(mine))
        def _():
            at.sent(mixed_heads.at[i], mix_s.at[i])

    for k in range(3):
        at.sent(small_own, small_s.at[k])
    for ch in range(CHUNKS):
        at.sent(frames.at[rows(ch)], on_s.at[z, ch])

        @pl.when(at.p == 2)
        def _():
            at.sent(relay.at[rows(ch)], x_s.at[ch])

        @pl.when(at.p == 1)
        def _():
            for place in (2, 3):
                at.sent(x_all.at[at.own_line(place), rows(ch)], on_s.at[at.own_line(place), ch])

        @pl.when(primary)
        def _():
            for s in range(4):
                at.sent(x_all.at[s, rows(ch)], fwd_s.at[s, ch])

    @pl.when(primary)
    def _():
        at.sent(kmask_own, mask_s.at[0])
        at.sent(hot_own, mask_s.at[1])
        at.sent(w_own.at[wq_rows], wq_s.at[0])

    @pl.when(secondary)
    def _():
        for k in (1, 2, 3):
            at.sent(w_t.at[wq_rows], wq_s.at[k])

    for m, (src, dst) in enumerate(mats):
        r, c = piece(m, at.q, at.b)
        for k in range(3):
            at.sent(src.at[r, c], p1_s.at[m, k])
            for j in range(4):
                at.sent(src.at[r, c], p2_s.at[m, k, j])
            for j in range(3):
                at.sent(src.at[r, c], p3_s.at[m, j, k])


def run_forward(frames, w_t, small, kmask, hot, w_up, w_down, w_out):
    share, d = frames.shape
    length = hot.shape[1]
    width = w_t.shape[0] // 3
    heads = width // HEAD_DIM
    f = w_up.shape[1]
    any_ = pl.BlockSpec(memory_space=pl.ANY)
    dma, V = pltpu.SemaphoreType.DMA, pltpu.VMEM
    return pl.pallas_call(
        forward_kernel,
        out_shape=(
            S((4, share, d)), S(w_t.shape), S((4, width, share)), S((4 * width, share)),
            S((heads, 128, length)), S((heads, length, 128)), S((heads, length, 128)), S((heads, HEAD_DIM, length)),
            S((heads, 8, length), F32), S((4, 8, d), F32), S((4, d, f)), S((4, f, d)), S((4, width, d)),
        ),
        in_specs=[VMEM] * 5 + [any_] * 3, out_specs=[VMEM] * 10 + [any_] * 3,
        scratch_shapes=[
            V((share, d), BF16), V((heads, HEAD_DIM, length), BF16), V((2 * heads * 128, d), BF16),
            V((length, 128), BF16), V((16, length), BF16),
            dma((3,)), dma((4,)), dma((2,)), dma((2,)), dma((4,)), dma((4,)), dma((CHUNKS,)), dma((4, CHUNKS)), dma((CHUNKS,)),
            dma((4, CHUNKS)), dma((4, CHUNKS)), dma((4,)), dma((4,)), dma((8,)),
            dma((3, 3)), dma((3, 3, 4)), dma((3, 3, 3)), dma((3, 4, 8)),
        ],
        compiler_params=pltpu.CompilerParams(vmem_limit_bytes=LIMIT, collective_id=0, has_side_effects=True),
        name="attention_forward",
    )(frames, w_t, small, kmask, hot, w_up, w_down, w_out)


def norm_stats(v):
    centered = v - jnp.mean(v, -1, keepdims=True)
    r = lax.rsqrt(jnp.mean(centered * centered, -1, keepdims=True) + 1e-05)
    return centered * r, r


def norm_back(c, gain, hat, r):
    e = c * gain
    return r * (e - jnp.mean(e, -1, keepdims=True) - hat * jnp.mean(e * hat, -1, keepdims=True))


def middle_kernel(
    skip_ref, mixed_ref, frames_ref, cot_ref, vec_ref, bup_ref, wout_ref, wup_ref, wdown_ref,
    layer_ref, gone_ref, gmixed_ref, normed_ref, act_ref, ginner_ref, gbranch_ref, gatt_ref, small_ref,
    slope_ref,
):
    skipped = skip_ref[0] == 1
    b_out, gain_one, shift_one, b_down, gain_two, shift_two = (vec_ref[i : i + 1, :] for i in range(6))
    frames = frames_ref[...].astype(F32)
    attended = mm(mixed_ref[...], wout_ref[...], 0, 0) + b_out
    hat_one, r_one = norm_stats(frames + attended)
    normed = hat_one * gain_one + shift_one
    normed_ref[...] = normed.astype(BF16)
    parts = wup_ref.shape[0]
    branch = jnp.zeros_like(normed)
    for s in range(parts):
        inner = mm(normed_ref[...], wup_ref[s]) + bup_ref[s : s + 1, :]
        cdf = 0.5 * (1.0 + lax.erf(inner * (0.5**0.5)))
        slope_ref[s] = cdf + inner * (jnp.exp(-0.5 * inner * inner) * 0.3989422804014327)
        act = (inner * cdf).astype(BF16)
        act_ref[s] = act
        branch = branch + mm(act, wdown_ref[s])
    hat_two, r_two = norm_stats(normed + (branch + b_down))
    result = hat_two * gain_two + shift_two
    cot = cot_ref[...].astype(F32)
    layer_ref[...] = jnp.where(skipped, frames, result).astype(BF16)
    grad_out = jnp.where(skipped, 0.0, cot)
    grad_two = norm_back(grad_out, gain_two, hat_two, r_two)
    gbranch = grad_two.astype(BF16)
    gbranch_ref[...] = gbranch
    small_ref[0:1, :] = jnp.sum(gbranch.astype(F32), 0, keepdims=True)
    small_ref[1:2, :] = jnp.sum(grad_out * hat_two, 0, keepdims=True)
    small_ref[2:3, :] = jnp.sum(grad_out, 0, keepdims=True)
    grad_normed = grad_two
    for s in range(parts):
        gact = mm(gbranch_ref[...], wdown_ref[s], 1, 1)
        ginner = (gact * slope_ref[s]).astype(BF16)
        ginner_ref[s] = ginner
        small_ref[6 + s : 7 + s, :] = jnp.sum(ginner.astype(F32), 0, keepdims=True)
        grad_normed = grad_normed + mm(ginner, wup_ref[s], 1, 1)
    grad_one = norm_back(grad_normed, gain_one, hat_one, r_one)
    gone_ref[...] = grad_one
    gatt = grad_one.astype(BF16)
    gatt_ref[...] = gatt
    small_ref[3:4, :] = jnp.sum(gatt.astype(F32), 0, keepdims=True)
    small_ref[4:5, :] = jnp.sum(grad_normed * hat_one, 0, keepdims=True)
    small_ref[5:6, :] = jnp.sum(grad_normed, 0, keepdims=True)
    gmixed_ref[...] = mm(wout_ref[...], gatt, 1, 1).astype(BF16)


def attend_back(h, i, cols, q_aug, k_aug, v_aug, k_t, do_aug, dq_acc, dk_acc, dv_acc):
    weights = jnp.exp(mm(k_aug[h], q_aug[h, :, cols]))
    rounded = weights.astype(BF16)
    dv_acc[h] += mm(do_aug[h, 0:HEAD_DIM, cols], rounded, 1, 1)
    grad = (weights * mm(v_aug[h], do_aug[h, :, cols])).astype(BF16)
    dk_acc[h] += mm(q_aug[h, 0:HEAD_DIM, cols], grad, 1, 1)
    return mm(k_t[h], grad)


def backward_kernel(
    x_ref, w_ref, gmixed_ref, mixed_ref, stats, q_in, k_aug, v_aug, k_t,
    wgrad_ref, part_ref, bias_ref, unused_ref, q_aug, do_aug, dk_acc, dv_acc, grads
):
    heads = q_aug.shape[0]
    width = heads * HEAD_DIM
    length = x_ref.shape[0]
    block = 384
    n = length // block

    def prepare(i, _):
        cols = pl.ds(pl.multiple_of(i * block, block), block)
        for h in range(heads):
            at = slice(h * HEAD_DIM, (h + 1) * HEAD_DIM)
            do = gmixed_ref[i, at, :]
            do_aug[h, 0:HEAD_DIM, cols] = do
            inner = jnp.sum(do.astype(F32) * mixed_ref[i, at, :].astype(F32), 0, keepdims=True)
            parts = split3(-inner)
            do_aug[h, HEAD_DIM : HEAD_DIM + 16, cols] = pad_rows(parts, 16, block)
            do_aug[h, HEAD_DIM + 16 :, cols] = jnp.zeros((48, block), BF16)
            q_aug[h, 0:HEAD_DIM, cols] = q_in[h, 0:HEAD_DIM, cols]
            hot = q_in[h, HEAD_DIM : HEAD_DIM + 16, cols].astype(F32)[0:4]
            parts = split3(-stats[h, 0:1, cols])
            q_aug[h, HEAD_DIM : HEAD_DIM + 16, cols] = pad_rows((hot,) + parts, 16, block)
            q_aug[h, HEAD_DIM + 16 :, cols] = jnp.zeros((48, block), BF16)
        return 0

    lax.fori_loop(0, n, prepare, 0)
    dk_acc[...] = jnp.zeros_like(dk_acc)
    dv_acc[...] = jnp.zeros_like(dv_acc)

    def step(i, _):
        cols = pl.ds(pl.multiple_of(i * block, block), block)
        for h in range(heads):
            dq = attend_back(h, i, cols, q_aug, k_aug, v_aug, k_t, do_aug, None, dk_acc, dv_acc)
            grads[h * HEAD_DIM : (h + 1) * HEAD_DIM, cols] = dq.astype(BF16) * jnp.bfloat16(HEAD_DIM**-0.5)
        return 0

    lax.fori_loop(0, n, step, 0)
    for h in range(heads):
        at = width + h * HEAD_DIM
        grads[at : at + HEAD_DIM, :] = dk_acc[h].astype(BF16)
        at = 2 * width + h * HEAD_DIM
        grads[at : at + HEAD_DIM, :] = dv_acc[h].astype(BF16)
    wgrad_ref[...] = mm(grads[...], x_ref[...]).astype(BF16)
    bias_ref[...] = mm(jnp.ones((8, length), BF16), grads[...], 1, 1)

    def out_step(i, _):
        cols = pl.ds(pl.multiple_of(i * block, block), block)
        part_ref[cols, :] = mm(grads[:, cols], w_ref[...], 0, 0).astype(BF16)
        return 0

    lax.fori_loop(0, n, out_step, 0)


def weights_kernel(normed_ref, act_ref, ginner_ref, gbranch_ref, gatt_ref, mixed_ref, gup_ref, gdown_ref, gout_ref):
    for s in range(act_ref.shape[0]):
        gdown_ref[s] = mm(act_ref[s], gbranch_ref[...], 0, 0).astype(BF16)
        gup_ref[s] = mm(normed_ref[...], ginner_ref[s], 0, 0).astype(BF16)
    gout_ref[...] = mm(mixed_ref[...], gatt_ref[...]).astype(BF16)


def S(shape, dtype=BF16):
    return jax.ShapeDtypeStruct(shape, dtype)


def shards(
    frames, cotangent, segments, padding, skip_flag, w_query, b_query, w_key, w_value, b_value,
    w_out, b_out, gain_one, shift_one, w_up, b_up, w_down, b_down, gain_two, shift_two,
):
    mp = lax.axis_size("mp")
    share, d = frames.shape[1:]
    length = segments.shape[1]
    width = w_query.shape[1]
    heads = width // HEAD_DIM
    params = pltpu.CompilerParams(vmem_limit_bytes=LIMIT)
    scale = HEAD_DIM**-0.5
    own = frames[0]
    w_t = jnp.concatenate([w_query.T, w_key.T, w_value.T], 0)
    bias_col = jnp.concatenate([b_query, jnp.zeros_like(b_query), b_value])[:, None]
    v_row = jnp.concatenate(
        [b_value.reshape(heads, HEAD_DIM), jnp.ones((heads, 3)), jnp.zeros((heads, 61))], 1
    ).reshape(1, heads * 128)
    seg, pad = segments[0], padding[0]
    ids = jnp.arange(4)
    ok = (seg[:, None] == ids[None]) & (pad[:, None] == 1)
    k_mask = jnp.concatenate(
        [jnp.zeros((length, 64)), jnp.where(ok, 0.0, -1e30), jnp.ones((length, 3)), jnp.zeros((length, 57))], 1
    ).astype(BF16)
    hot = jnp.concatenate([(seg[None] == ids[:, None]).astype(BF16), jnp.zeros((12, length), BF16)], 0)

    everything = lax.all_gather(own, "mp", axis=0, tiled=True)
    mixed, q_aug, k_aug, v_aug, k_t, v_t, stats = pl.pallas_call(
        local_forward_kernel,
        out_shape=(
            S((mp, width, share)), S((heads, 128, length)), S((heads, length, 128)), S((heads, length, 128)),
            S((heads, HEAD_DIM, length)), S((heads, HEAD_DIM, length)), S((heads, 8, length), F32),
        ),
        in_specs=[VMEM] * 6, out_specs=[VMEM] * 7,
        scratch_shapes=[pltpu.VMEM((2 * heads * 128, d), BF16)],
        compiler_params=params, name="local_forward",
    )(everything, w_t, bias_col, v_row, k_mask, hot)
    zero = jnp.zeros((d,), F32)
    bias_row = jnp.concatenate([b_query, jnp.zeros_like(b_query), b_value, jnp.zeros((d - 3 * width,), F32)])
    v_row2 = jnp.concatenate([v_row[0], jnp.zeros((d - heads * 128,), F32)])
    small = jnp.stack([b_up, bias_row, v_row2] + [zero] * 5)
    _, _, _, mixed_own, _, _, _, _, _, small_all, wup, wdown, wout = run_forward(
        own, w_t, small, k_mask, hot, w_up, w_down, w_out
    )
    wout = wout.reshape(mp * width, d)
    bup = small_all[:, 0]
    vec = jnp.stack([b_out, gain_one, shift_one, b_down, gain_two, shift_two] + [b_out] * 2)
    f = w_up.shape[1]
    layer, gone, gmixed, normed, act, ginner, gbranch, gatt, small = pl.pallas_call(
        middle_kernel,
        out_shape=(
            S((share, d)), S((share, d), F32), S((mp * width, share)), S((share, d)), S((mp, share, f)),
            S((mp, share, f)), S((share, d)), S((share, d)), S((16, d), F32),
        ),
        in_specs=[SMEM] + [VMEM] * 8, out_specs=[VMEM] * 9,
        scratch_shapes=[pltpu.VMEM((mp, share, f), F32)],
        compiler_params=params, name="feed_forward",
    )(skip_flag, mixed_own, own, cotangent[0], vec, bup, wout, wup, wdown)
    gup, gdown, gout = pl.pallas_call(
        weights_kernel,
        out_shape=(S((mp, d, f)), S((mp, f, d)), S((mp * width, d))),
        in_specs=[VMEM] * 6, out_specs=[VMEM] * 3, compiler_params=params, name="weight_grads",
    )(normed, act, ginner, gbranch, gatt, mixed_own)
    gmixed_heads = lax.all_to_all(gmixed.reshape(mp, width, share), "mp", 0, 0)
    wgrad, part, bias = pl.pallas_call(
        backward_kernel,
        out_shape=(S((3 * width, d)), S((length, d)), S((8, 3 * width), F32), S((16, 128), F32)),
        in_specs=[VMEM] * 9, out_specs=[VMEM] * 4,
        scratch_shapes=[
            pltpu.VMEM((heads, 128, length), BF16), pltpu.VMEM((heads, 128, length), BF16),
            pltpu.VMEM((heads, HEAD_DIM, length), F32), pltpu.VMEM((heads, HEAD_DIM, length), F32),
            pltpu.VMEM((3 * width, length), BF16),
        ],
        compiler_params=params, name="attention_backward",
    )(everything, w_t, gmixed_heads, mixed, stats, q_aug, k_aug, v_aug, k_t)[:3]
    dx = lax.psum_scatter(part, "mp", scatter_dimension=0, tiled=True).astype(F32)
    skipped = (skip_flag == 1)[0]
    frames_grad = jnp.where(skipped, cotangent[0].astype(F32), gone + dx).astype(BF16)
    wgrad = lax.psum(wgrad, "dp").astype(F32)
    bias = lax.psum(bias[0], "dp")
    gup = lax.psum(lax.psum_scatter(gup, "mp"), "dp").astype(F32)
    gdown = lax.psum(lax.psum_scatter(gdown, "mp"), "dp").astype(F32)
    gout = lax.psum(lax.psum_scatter(gout.reshape(mp, width, d), "mp"), "dp").astype(F32)
    small = lax.psum(small, ("dp", "mp"))
    z = lax.axis_index("mp")
    return (
        layer[None], frames_grad[None],
        wgrad[:width].T, bias[:width], wgrad[width : 2 * width].T, wgrad[2 * width :].T, bias[2 * width :],
        gout, small[3], small[4], small[5],
        gup, small[6 + z], gdown, small[0], small[1], small[2],
    )


def solution(mesh):
    split = (P("dp", "mp", None), P(None, "mp"), P("mp"), P("mp", None), P())
    row, col, one, top, rep = split
    return jax.shard_map(
        shards,
        mesh=mesh,
        in_specs=(row, row, P("dp", None), P("dp", None), P("dp"), col, one, col, col, one, top, rep, rep, rep, col, one, top, rep, rep, rep),
        out_specs=(row, row, col, one, col, col, one, top, rep, rep, rep, col, one, top, rep, rep, rep),
        check_vma=False,
    )
```

```python
import functools

import jax
import jax.numpy as jnp
from jax import lax
from jax.experimental import pallas as pl
from jax.experimental.pallas import tpu as pltpu
from jax.sharding import PartitionSpec as P

HEAD_DIM = 64
F32, BF16 = jnp.float32, jnp.bfloat16
VMEM = pl.BlockSpec(memory_space=pltpu.VMEM)
SMEM = pl.BlockSpec(memory_space=pltpu.SMEM)
LIMIT = 60 << 20


def mm(a, b, ca=1, cb=0):
    return lax.dot_general(a, b, (((ca,), (cb,)), ((), ())), preferred_element_type=F32)


def split3(v):
    hi = v.astype(BF16)
    rest = v - hi.astype(F32)
    mid = rest.astype(BF16)
    low = (rest - mid.astype(F32)).astype(BF16)
    return hi, mid, low


def pad_rows(parts, rows, width):
    parts = [p.astype(F32) for p in parts]
    have = sum(p.shape[0] for p in parts)
    return jnp.concatenate(parts + [jnp.zeros((rows - have, width), F32)], 0).astype(BF16)


def project(x, w_t, w_pad, bias_col, v_row, k_mask, one_hot, rows, q_aug, k_aug, v_aug, k_t, v_t):
    width = w_t.shape[0] // 3
    heads = width // HEAD_DIM
    every = mm(w_t, x, 1, 1) + bias_col
    every = jnp.concatenate([every[:width] * HEAD_DIM**-0.5, every[width:]], 0).astype(BF16)
    for h in range(heads):
        q_aug[h, 0:HEAD_DIM, rows] = every[h * HEAD_DIM : (h + 1) * HEAD_DIM]
        q_aug[h, HEAD_DIM : HEAD_DIM + 16, rows] = one_hot
        q_aug[h, HEAD_DIM + 16 :, rows] = jnp.zeros((48, x.shape[0]), BF16)
        k_t[h, :, rows] = every[width + h * HEAD_DIM : width + (h + 1) * HEAD_DIM]
        v_t[h, :, rows] = every[2 * width + h * HEAD_DIM : 2 * width + (h + 1) * HEAD_DIM]
    both = mm(x, w_pad, 1, 1)
    for h in range(heads):
        k_aug[h, rows, :] = both[:, h * 128 : (h + 1) * 128].astype(BF16) + k_mask
        at = (heads + h) * 128
        v_aug[h, rows, :] = (both[:, at : at + 128] + v_row[:, h * 128 : (h + 1) * 128]).astype(BF16)


def attend(h, cols, q_aug, k_aug, v_t):
    scores = mm(k_aug[h], q_aug[h, :, cols])
    peak = jnp.max(scores, 0, keepdims=True)
    raised = jnp.exp(scores - peak)
    summed = jnp.sum(raised, 0, keepdims=True)
    mixed = mm(v_t[h], raised.astype(BF16)) / summed
    one_hot = q_aug[h, HEAD_DIM : HEAD_DIM + 16, cols].astype(F32)[0:4]
    q_aug[h, HEAD_DIM : HEAD_DIM + 16, cols] = pad_rows((one_hot,) + split3(-(peak + jnp.log(summed))), 16, mixed.shape[1])
    return mixed.astype(BF16)


MESH = pl.DeviceIdType.MESH
CHUNKS = 3


class Place:
    def __init__(self):
        self.d, self.z = lax.axis_index("dp"), lax.axis_index("mp")
        d, z = self.d, self.z
        self.b = d % 2
        self.p = z + self.b * (3 - 2 * z)
        self.sib = d + 1 - 2 * self.b
        self.q = (d // 2) % 4
        self.base = d - d % 8
        self.primary = self.p < 2
        self.rb = z // 2
        self.row = d - self.b + self.rb
        self.pp = z + self.rb * (3 - 2 * z)
        self.far = (z + 2) % 4
        self.group = jnp.where(self.primary, z, self.far)

    def own_line(self, place):
        return place + self.b * (3 - 2 * place)

    def line(self, place):
        return place + self.rb * (3 - 2 * place)

    def chip(self, k):
        return self.base + 2 * ((self.q + k) % 4) + self.b

    def other(self, k):
        return self.base + 2 * ((self.q + k) % 4) + 1 - self.b

    def barrier(self):
        sem = pltpu.get_barrier_semaphore()
        others = [((self.d), (self.z + k) % 4) for k in (1, 2, 3)]
        others += [(self.sib, (self.z + k) % 4) for k in range(4)]
        others += [(self.chip(k), self.z) for k in (1, 2, 3)]
        others += [(self.other(k), self.z) for k in (1, 2, 3)]
        for dp, mp in others:
            pl.semaphore_signal(sem, inc=1, device_id=(dp, mp), device_id_type=MESH)
        pl.semaphore_wait(sem, len(others))

    def send(self, src, dst, send_sem, recv_sem, dp, mp):
        pltpu.make_async_remote_copy(
            src_ref=src, dst_ref=dst, send_sem=send_sem, recv_sem=recv_sem, device_id=(dp, mp), device_id_type=MESH
        ).start()

    def sent(self, src, send_sem):
        pltpu.make_async_remote_copy(
            src_ref=src, dst_ref=src, send_sem=send_sem, recv_sem=send_sem, device_id=(self.sib, self.z), device_id_type=MESH
        ).wait_send()

    def got(self, dst, recv_sem):
        pltpu.make_async_remote_copy(
            src_ref=dst, dst_ref=dst, send_sem=recv_sem, recv_sem=recv_sem, device_id=(self.sib, self.z), device_id_type=MESH
        ).wait_recv()


def forward_kernel(
    frames, w_own, small_own, kmask_own, hot_own, w_up, w_down, w_out,
    x_all, w_t, mixed_heads, mixed_own, q_aug, k_aug, v_aug, k_t, small_all, up_all, down_all, out_all,
    relay, v_t, w_pad, kmask, hot,
    small_s, small_r, mask_s, mask_r, wq_s, wq_r, x_s, x_r, relay_r, on_s, fwd_s, mix_s, mix_r, local,
    p1_s, p2_s, p3_s, w_r,
):
    at = Place()
    heads = q_aug.shape[0]
    width = heads * HEAD_DIM
    share = frames.shape[0]
    step_rows = share // CHUNKS
    quarter = w_own.shape[0] // 4
    at.barrier()
    primary = at.primary
    secondary = jnp.logical_not(primary)
    z = at.z

    def rows(ch):
        return pl.ds(ch * step_rows, step_rows)

    def piece(m, chip, core):
        if m == 2:
            n = w_out.shape[0] // 4
            half = w_out.shape[1] // 2
            return (pl.ds(pl.multiple_of(chip * n, 16), n), pl.ds(pl.multiple_of(core * half, 128), half))
        n = w_up.shape[0] // 8
        return (pl.ds(pl.multiple_of((2 * chip + core) * n, 16), n), slice(None))

    mats = ((w_up, up_all), (w_down, down_all), (w_out, out_all))

    wq_rows = pl.ds(pl.multiple_of(at.q * quarter, 16), quarter)
    first = jnp.where(at.p == 0, 1, at.p - 1)

    @pl.when(primary)
    def _():
        at.send(w_own.at[wq_rows], w_t.at[wq_rows], wq_s.at[0], wq_r.at[at.q], at.d, at.far)

    for ch in range(CHUNKS):
        @pl.when(at.p < 3)
        def _():
            at.send(frames.at[rows(ch)], x_all.at[z, rows(ch)], on_s.at[z, ch], x_r.at[z, ch], at.d, at.own_line(first))

        @pl.when(at.p == 3)
        def _():
            at.send(frames.at[rows(ch)], relay.at[rows(ch)], on_s.at[z, ch], relay_r.at[ch], at.d, at.own_line(2))

    @pl.when(primary)
    def _():
        at.send(kmask_own, kmask, mask_s.at[0], mask_r.at[0], at.sib, z)
        at.send(hot_own, hot, mask_s.at[1], mask_r.at[1], at.sib, z)
        pltpu.make_async_copy(kmask_own, kmask, local.at[0]).start()
        pltpu.make_async_copy(hot_own, hot, local.at[1]).start()
        pltpu.make_async_copy(w_own, w_t, local.at[2]).start()
        pltpu.make_async_copy(frames, x_all.at[z], local.at[3]).start()
        for ch in range(CHUNKS):
            at.send(frames.at[rows(ch)], x_all.at[z, rows(ch)], fwd_s.at[z, ch], x_r.at[z, ch], at.sib, z)

    for k in (1, 2, 3):
        to = (z + k) % 4
        at.send(small_own, small_all.at[z], small_s.at[k - 1], small_r.at[z], at.d, to)
    pltpu.make_async_copy(small_own, small_all.at[z], local.at[4]).start()
    for m, (src, dst) in enumerate(mats):
        pltpu.make_async_copy(src, dst.at[z], local.at[5 + m]).start()

    @pl.when(at.p == 2)
    def _():
        for ch in range(CHUNKS):
            at.got(relay.at[rows(ch)], relay_r.at[ch])
            at.send(relay.at[rows(ch)], x_all.at[at.own_line(3), rows(ch)], x_s.at[ch], x_r.at[at.own_line(3), ch], at.d, at.own_line(1))

    @pl.when(secondary)
    def _():
        at.got(w_t.at[wq_rows], wq_r.at[at.q])
        for k in (1, 2, 3):
            at.send(w_t.at[wq_rows], w_t.at[wq_rows], wq_s.at[k], wq_r.at[at.q], at.chip(k), z)
        at.got(kmask, mask_r.at[0])
        at.got(hot, mask_r.at[1])

    @pl.when(primary)
    def _():
        pltpu.make_async_copy(kmask_own, kmask, local.at[0]).wait()
        pltpu.make_async_copy(hot_own, hot, local.at[1]).wait()
        pltpu.make_async_copy(w_own, w_t, local.at[2]).wait()
        pltpu.make_async_copy(frames, x_all.at[z], local.at[3]).wait()

    pltpu.make_async_copy(small_own, small_all.at[z], local.at[4]).wait()
    for k in (1, 2, 3):
        at.got(small_all.at[(z + k) % 4], small_r.at[(z + k) % 4])

    @pl.when(secondary)
    def _():
        for k in (1, 2, 3):
            other = (at.q + k) % 4
            at.got(w_t.at[pl.ds(pl.multiple_of(other * quarter, 16), quarter)], wq_r.at[other])

    w_pad[...] = jnp.zeros_like(w_pad)
    for i in range(2):
        for h in range(heads):
            w_pad[(i * heads + h) * 128 : (i * heads + h) * 128 + HEAD_DIM] = w_t[
                (i + 1) * width + h * HEAD_DIM : (i + 1) * width + (h + 1) * HEAD_DIM
            ]

    def shard_of(k):
        place = jnp.where(at.pp == 0, k, jnp.where(k == 0, 1, jnp.where(k == 1, 2, jnp.where(k == 2, 0, 3))))
        return place, at.line(place)

    def gather_step(k, _):
        place, s = shard_of(k)
        for ch in range(CHUNKS):
            block = x_all.at[s, rows(ch)]

            @pl.when(jnp.logical_or(k > 0, secondary))
            def _():
                at.got(block, x_r.at[s, ch])

            @pl.when(jnp.logical_and(k > 0, primary))
            def _():
                @pl.when(jnp.logical_and(at.p == 1, place >= 2))
                def _():
                    at.send(block, block, on_s.at[s, ch], x_r.at[s, ch], at.d, at.own_line(0))

                at.send(block, block, fwd_s.at[s, ch], x_r.at[s, ch], at.sib, z)

        cols = pl.ds(pl.multiple_of(s * share, share), share)
        biases = jnp.transpose(small_all[at.group])
        project(
            x_all[s], w_t[...], w_pad[...], biases[: 3 * width, 1:2], small_all[at.group, 2:3, : heads * 128], kmask[cols, :],
            hot[:, cols], cols, q_aug, k_aug, v_aug, k_t, v_t,
        )
        return 0

    lax.fori_loop(0, 4, gather_step, 0)

    for m, (src, dst) in enumerate(mats):
        r, c = piece(m, at.q, at.b)
        for k in (1, 2, 3):
            at.send(src.at[r, c], dst.at[z, r, c], p1_s.at[m, k - 1], w_r.at[m, z, 2 * at.q + at.b], at.d, (z + k) % 4)

    def spread(m):
        dst = mats[m][1]
        r, c = piece(m, at.q, at.b)
        for k in (1, 2, 3):
            s = (z + k) % 4
            sem = w_r.at[m, s, 2 * at.q + at.b]
            at.got(dst.at[s, r, c], sem)
            for j in (1, 2, 3):
                at.send(dst.at[s, r, c], dst.at[s, r, c], p2_s.at[m, k - 1, j], sem, at.chip(j), z)
            at.send(dst.at[s, r, c], dst.at[s, r, c], p2_s.at[m, k - 1, 0], sem, at.sib, z)

    def attend_step(i, _):
        cols = pl.ds(pl.multiple_of(i * share, share), share)
        for h in range(heads):
            mixed_heads[i, h * HEAD_DIM : (h + 1) * HEAD_DIM, :] = attend(h, cols, q_aug, k_aug, v_t)
        mine = jnp.logical_and(primary, i == z)
        block = mixed_own.at[pl.ds(pl.multiple_of(at.group * width, 64), width)]

        @pl.when(mine)
        def _():
            pltpu.make_async_copy(mixed_heads.at[i], block, mix_s.at[i]).start()

        @pl.when(jnp.logical_not(mine))
        def _():
            at.send(mixed_heads.at[i], block, mix_s.at[i], mix_r.at[at.group], at.row, i)

        @pl.when(i == 1)
        def _():
            spread(0)

        @pl.when(i == 3)
        def _():
            spread(1)
            spread(2)

        return 0

    lax.fori_loop(0, 4, attend_step, 0)

    for m, (_, dst) in enumerate(mats):
        for j in (1, 2, 3):
            chip = (at.q + j) % 4
            r, c = piece(m, chip, at.b)
            for k in (1, 2, 3):
                s = (z + k) % 4
                sem = w_r.at[m, s, 2 * chip + at.b]
                at.got(dst.at[s, r, c], sem)
                at.send(dst.at[s, r, c], dst.at[s, r, c], p3_s.at[m, j - 1, k - 1], sem, at.sib, z)

    for g in range(4):
        mine = jnp.logical_and(primary, z == g)
        block = mixed_own.at[pl.ds(g * width, width)]

        @pl.when(jnp.logical_not(mine))
        def _():
            at.got(block, mix_r.at[g])

    for m, (src, dst) in enumerate(mats):
        pltpu.make_async_copy(src, dst.at[z], local.at[5 + m]).wait()
        for j in range(4):
            chip = (at.q + j) % 4
            r, c = piece(m, chip, 1 - at.b)
            for k in (1, 2, 3):
                s = (z + k) % 4
                at.got(dst.at[s, r, c], w_r.at[m, s, 2 * chip + 1 - at.b])

    for i in range(4):
        mine = jnp.logical_and(primary, z == i)

        @pl.when(mine)
        def _():
            block = mixed_own.at[pl.ds(pl.multiple_of(at.group * width, 64), width)]
            pltpu.make_async_copy(mixed_heads.at[i], block, mix_s.at[i]).wait()

        @pl.when(jnp.logical_not(mine))
        def _():
            at.sent(mixed_heads.at[i], mix_s.at[i])

    for k in range(3):
        at.sent(small_own, small_s.at[k])
    for ch in range(CHUNKS):
        at.sent(frames.at[rows(ch)], on_s.at[z, ch])

        @pl.when(at.p == 2)
        def _():
            at.sent(relay.at[rows(ch)], x_s.at[ch])

        @pl.when(at.p == 1)
        def _():
            for place in (2, 3):
                at.sent(x_all.at[at.own_line(place), rows(ch)], on_s.at[at.own_line(place), ch])

        @pl.when(primary)
        def _():
            for s in range(4):
                at.sent(x_all.at[s, rows(ch)], fwd_s.at[s, ch])

    @pl.when(primary)
    def _():
        at.sent(kmask_own, mask_s.at[0])
        at.sent(hot_own, mask_s.at[1])
        at.sent(w_own.at[wq_rows], wq_s.at[0])

    @pl.when(secondary)
    def _():
        for k in (1, 2, 3):
            at.sent(w_t.at[wq_rows], wq_s.at[k])

    for m, (src, dst) in enumerate(mats):
        r, c = piece(m, at.q, at.b)
        for k in range(3):
            at.sent(src.at[r, c], p1_s.at[m, k])
            for j in range(4):
                at.sent(src.at[r, c], p2_s.at[m, k, j])
            for j in range(3):
                at.sent(src.at[r, c], p3_s.at[m, j, k])


def run_forward(frames, w_t, small, kmask, hot, w_up, w_down, w_out):
    share, d = frames.shape
    length = hot.shape[1]
    width = w_t.shape[0] // 3
    heads = width // HEAD_DIM
    f = w_up.shape[1]
    any_ = pl.BlockSpec(memory_space=pl.ANY)
    dma, V = pltpu.SemaphoreType.DMA, pltpu.VMEM
    return pl.pallas_call(
        forward_kernel,
        out_shape=(
            S((4, share, d)), S(w_t.shape), S((4, width, share)), S((4 * width, share)),
            S((heads, 128, length)), S((heads, length, 128)), S((heads, length, 128)), S((heads, HEAD_DIM, length)),
            S((4, 8, d), F32), S((4, d, f)), S((4, f, d)), S((4, width, d)),
        ),
        in_specs=[VMEM] * 5 + [any_] * 3, out_specs=[VMEM] * 9 + [any_] * 3,
        scratch_shapes=[
            V((share, d), BF16), V((heads, HEAD_DIM, length), BF16), V((2 * heads * 128, d), BF16),
            V((length, 128), BF16), V((16, length), BF16),
            dma((3,)), dma((4,)), dma((2,)), dma((2,)), dma((4,)), dma((4,)), dma((CHUNKS,)), dma((4, CHUNKS)), dma((CHUNKS,)),
            dma((4, CHUNKS)), dma((4, CHUNKS)), dma((4,)), dma((4,)), dma((8,)),
            dma((3, 3)), dma((3, 3, 4)), dma((3, 3, 3)), dma((3, 4, 8)),
        ],
        compiler_params=pltpu.CompilerParams(vmem_limit_bytes=LIMIT, collective_id=0, has_side_effects=True),
        name="attention_forward",
    )(frames, w_t, small, kmask, hot, w_up, w_down, w_out)


def norm_stats(v):
    centered = v - jnp.mean(v, -1, keepdims=True)
    r = lax.rsqrt(jnp.mean(centered * centered, -1, keepdims=True) + 1e-05)
    return centered * r, r


def norm_back(c, gain, hat, r):
    e = c * gain
    return r * (e - jnp.mean(e, -1, keepdims=True) - hat * jnp.mean(e * hat, -1, keepdims=True))


def middle_kernel(
    skip_ref, mixed_ref, frames_ref, cot_ref, vec_ref, bup_ref, wout_ref, wup_ref, wdown_ref,
    layer_ref, gone_ref, gmixed_ref, normed_ref, act_ref, ginner_ref, gbranch_ref, gatt_ref, small_ref,
    slope_ref,
):
    skipped = skip_ref[0] == 1
    b_out, gain_one, shift_one, b_down, gain_two, shift_two = (vec_ref[i : i + 1, :] for i in range(6))
    frames = frames_ref[...].astype(F32)
    attended = mm(mixed_ref[...], wout_ref[...], 0, 0) + b_out
    hat_one, r_one = norm_stats(frames + attended)
    normed = hat_one * gain_one + shift_one
    normed_ref[...] = normed.astype(BF16)
    parts = wup_ref.shape[0]
    branch = jnp.zeros_like(normed)
    for s in range(parts):
        inner = mm(normed_ref[...], wup_ref[s]) + bup_ref[s : s + 1, :]
        cdf = 0.5 * (1.0 + lax.erf(inner * (0.5**0.5)))
        slope_ref[s] = cdf + inner * (jnp.exp(-0.5 * inner * inner) * 0.3989422804014327)
        act = (inner * cdf).astype(BF16)
        act_ref[s] = act
        branch = branch + mm(act, wdown_ref[s])
    hat_two, r_two = norm_stats(normed + (branch + b_down))
    result = hat_two * gain_two + shift_two
    cot = cot_ref[...].astype(F32)
    layer_ref[...] = jnp.where(skipped, frames, result).astype(BF16)
    grad_out = jnp.where(skipped, 0.0, cot)
    grad_two = norm_back(grad_out, gain_two, hat_two, r_two)
    gbranch = grad_two.astype(BF16)
    gbranch_ref[...] = gbranch
    small_ref[10:16, :] = jnp.zeros_like(small_ref[10:16, :])
    small_ref[0:1, :] = jnp.sum(gbranch.astype(F32), 0, keepdims=True)
    small_ref[1:2, :] = jnp.sum(grad_out * hat_two, 0, keepdims=True)
    small_ref[2:3, :] = jnp.sum(grad_out, 0, keepdims=True)
    grad_normed = grad_two
    for s in range(parts):
        gact = mm(gbranch_ref[...], wdown_ref[s], 1, 1)
        ginner = (gact * slope_ref[s]).astype(BF16)
        ginner_ref[s] = ginner
        small_ref[6 + s : 7 + s, :] = jnp.sum(ginner.astype(F32), 0, keepdims=True)
        grad_normed = grad_normed + mm(ginner, wup_ref[s], 1, 1)
    grad_one = norm_back(grad_normed, gain_one, hat_one, r_one)
    gone_ref[...] = grad_one
    gatt = grad_one.astype(BF16)
    gatt_ref[...] = gatt
    small_ref[3:4, :] = jnp.sum(gatt.astype(F32), 0, keepdims=True)
    small_ref[4:5, :] = jnp.sum(grad_normed * hat_one, 0, keepdims=True)
    small_ref[5:6, :] = jnp.sum(grad_normed, 0, keepdims=True)
    gmixed_ref[...] = mm(wout_ref[...], gatt, 1, 1).astype(BF16)


def attend_back(h, i, cols, q_aug, k_aug, v_aug, k_t, do_aug, dq_acc, dk_acc, dv_acc):
    weights = jnp.exp(mm(k_aug[h], q_aug[h, :, cols]))
    rounded = weights.astype(BF16)
    dv_acc[h] += mm(do_aug[h, 0:HEAD_DIM, cols], rounded, 1, 1)
    grad = (weights * mm(v_aug[h], do_aug[h, :, cols])).astype(BF16)
    dk_acc[h] += mm(q_aug[h, 0:HEAD_DIM, cols], grad, 1, 1)
    return mm(k_t[h], grad)


def total(first, *others):
    out = first.astype(F32)
    for other in others:
        out = out + other.astype(F32)
    return out


def backward_kernel(
    skip_ref, gmixed, mixed_own, normed, act, ginner, gbranch, gatt, small, gone, cot,
    x_all, w_t, mixed_heads, q_aug, k_aug, v_aug, k_t,
    frames_grad, dw_out, up_out, down_out, out_out, small_out,
    do_in, do_aug, dk_acc, dv_acc, grads,
    big, away, core_in, plane_in, mid, z_in, bigo, core_ino, plane_ino, mido, z_ino,
    part, sib_in, line_in, dw_own, dw_in, dw_mid, dw_z, small_mine, small_plane, small_mid, small_z,
    gm_s, gm_r, ci_s, ci_r, pl_s, pl_r, z_s, z_r, ag_s, ag_r, agf_s,
    part_s, part_r, line_s, line_r, dwp_s, dwp_r, dwz_s, dwz_r, dwo_s, dwo_r, dwf_s, sp_s, sp_r, sz_s, sz_r,
):
    at = Place()
    heads = q_aug.shape[0]
    width = heads * HEAD_DIM
    share = gatt.shape[0]
    length = x_all.shape[0] * share
    step_rows = share // CHUNKS
    z, c, q = at.z, at.b, at.q
    primary = at.primary
    secondary = jnp.logical_not(primary)
    at.barrier()

    for g in range(4):
        block = gmixed.at[pl.ds(g * width, width)]
        near = at.b == g // 2
        to_d = jnp.where(near, at.d, at.sib)
        to_z = jnp.where(near, g, (g + 2) % 4)
        mine = jnp.logical_and(near, z == g)

        @pl.when(mine)
        def _():
            pltpu.make_async_copy(block, do_in.at[z], gm_s.at[g]).start()

        @pl.when(jnp.logical_not(mine))
        def _():
            at.send(block, do_in.at[z], gm_s.at[g], gm_r.at[z], to_d, to_z)

    n_big = 8
    half = big.shape[1]
    quarter = half // 4
    halfo = bigo.shape[3]
    quartero = bigo.shape[2] // 4
    finals = (down_out, up_out, out_out)

    def big_rows(chip):
        return pl.ds(pl.multiple_of(chip * quarter, 16), quarter)

    def out_rows(chip):
        return pl.ds(pl.multiple_of(chip * quartero, 16), quartero)

    def weight_job(j):
        if j < n_big:
            kind, s = j // 4, j % 4
            made = mm(act[s], gbranch[...], 0, 0) if kind == 0 else mm(normed[...], ginner[s], 0, 0)
            made = made.astype(BF16)
            if j >= 4:
                at.sent(away.at[j % 4], ci_s.at[j - 4])

            @pl.when(c == 0)
            def _():
                big[j] = made[:half]
                away[j % 4] = made[half:]

            @pl.when(c == 1)
            def _():
                big[j] = made[half:]
                away[j % 4] = made[:half]

            at.send(away.at[j % 4], core_in.at[j], ci_s.at[j], ci_r.at[j], at.sib, z)
        else:
            for s in range(4):
                made = mm(mixed_own[s * width : (s + 1) * width, :], gatt[...])
                for i in range(2):
                    bigo[i, s] = made[:, i * halfo : (i + 1) * halfo].astype(BF16)
            at.send(bigo.at[1 - c], core_ino, ci_s.at[j], ci_r.at[j], at.sib, z)

    def core_job(j):
        if j < n_big:
            at.got(core_in.at[j], ci_r.at[j])
            big[j] = total(big[j], core_in[j]).astype(BF16)
            for k in (1, 2, 3):
                at.send(big.at[j, big_rows((q + k) % 4)], plane_in.at[3 - k, j], pl_s.at[j, k - 1], pl_r.at[j, 3 - k], at.chip(k), z)
        else:
            at.got(core_ino, ci_r.at[j])
            bigo[c] = total(bigo[c], core_ino[...]).astype(BF16)
            for k in (1, 2, 3):
                at.send(bigo.at[c, :, out_rows((q + k) % 4)], plane_ino.at[3 - k], pl_s.at[j, k - 1], pl_r.at[j, 3 - k], at.chip(k), z)

    def plane_job(j):
        if j < n_big:
            kind, s = j // 4, j % 4
            for k in range(3):
                at.got(plane_in.at[k, j], pl_r.at[j, k])
            mid[j] = total(big[j, big_rows(q)], plane_in[0, j], plane_in[1, j], plane_in[2, j]).astype(BF16)

            @pl.when(z != s)
            def _():
                slot = 3 - (s - z + 4) % 4
                at.send(mid.at[j], z_in.at[slot, kind], z_s.at[j], z_r.at[kind, slot], at.d, s)
        else:
            for k in range(3):
                at.got(plane_ino.at[k], pl_r.at[j, k])
            mido[...] = total(bigo[c, :, out_rows(q)], plane_ino[0], plane_ino[1], plane_ino[2]).astype(BF16)
            for s in range(4):
                @pl.when(z != s)
                def _():
                    slot = 3 - (s - z + 4) % 4
                    at.send(mido.at[s], z_ino.at[slot], z_s.at[j + s], z_r.at[2, slot], at.d, s)

    def final_piece(kind, chip, core):
        if kind < 2:
            return finals[kind].at[pl.ds(pl.multiple_of(core * half + chip * quarter, 16), quarter)]
        return out_out.at[out_rows(chip), pl.ds(pl.multiple_of(core * halfo, 128), halfo)]

    def final_job(kind):
        for k in range(3):
            at.got(z_in.at[k, kind] if kind < 2 else z_ino.at[k], z_r.at[kind, k])
        piece = final_piece(kind, q, c)
        if kind < 2:
            piece[...] = total(mid[4 * kind + z], z_in[0, kind], z_in[1, kind], z_in[2, kind]).astype(BF16)
        else:
            piece[...] = total(mido[z], z_ino[0], z_ino[1], z_ino[2]).astype(BF16)
        sem = ag_r.at[kind, 2 * q + c]
        for k in (1, 2, 3):
            at.send(piece, piece, ag_s.at[kind, k], sem, at.chip(k), z)
        at.send(piece, piece, ag_s.at[kind, 0], sem, at.sib, z)

    def share_job(kind):
        for k in (1, 2, 3):
            chip = (q + k) % 4
            piece = final_piece(kind, chip, c)
            sem = ag_r.at[kind, 2 * chip + c]
            at.got(piece, sem)
            at.send(piece, piece, agf_s.at[kind, k - 1], sem, at.sib, z)

    def end_job(kind):
        for k in range(4):
            chip = (q + k) % 4
            at.got(final_piece(kind, chip, 1 - c), ag_r.at[kind, 2 * chip + 1 - c])

    for j in range(n_big + 1):
        weight_job(j)
        if j >= 2:
            core_job(j - 2)
    core_job(n_big - 1)
    core_job(n_big)

    for s in range(4):
        mine = jnp.logical_and(primary, z == s)

        @pl.when(mine)
        def _():
            pltpu.make_async_copy(gmixed.at[pl.ds(s * width, width)], do_in.at[s], gm_s.at[s]).wait()

        @pl.when(jnp.logical_not(mine))
        def _():
            at.got(do_in.at[s], gm_r.at[s])

    def prepare(i, _):
        cols = pl.ds(pl.multiple_of(i * share, share), share)
        for h in range(heads):
            hs = slice(h * HEAD_DIM, (h + 1) * HEAD_DIM)
            do = do_in[i, hs, :]
            do_aug[h, 0:HEAD_DIM, cols] = do
            inner = jnp.sum(do.astype(F32) * mixed_heads[i, hs, :].astype(F32), 0, keepdims=True)
            do_aug[h, HEAD_DIM : HEAD_DIM + 16, cols] = pad_rows(split3(-inner), 16, share)
            do_aug[h, HEAD_DIM + 16 :, cols] = jnp.zeros((48, share), BF16)
        return 0

    lax.fori_loop(0, 4, prepare, 0)
    dk_acc[...] = jnp.zeros_like(dk_acc)
    dv_acc[...] = jnp.zeros_like(dv_acc)

    def attention_step(i, _):
        cols = pl.ds(pl.multiple_of(i * share, share), share)
        for h in range(heads):
            dq = attend_back(h, i, cols, q_aug, k_aug, v_aug, k_t, do_aug, None, dk_acc, dv_acc)
            grads[h * HEAD_DIM : (h + 1) * HEAD_DIM, cols] = (dq.astype(BF16).astype(F32) * HEAD_DIM**-0.5).astype(BF16)
        for n in range(4):
            @pl.when(i == n)
            def _():
                for j in (2 * n, 2 * n + 1):
                    plane_job(j)
        return 0

    lax.fori_loop(0, 4, attention_step, 0)
    for h in range(heads):
        grads[width + h * HEAD_DIM : width + (h + 1) * HEAD_DIM, :] = dk_acc[h].astype(BF16)
        grads[2 * width + h * HEAD_DIM : 2 * width + (h + 1) * HEAD_DIM, :] = dv_acc[h].astype(BF16)


    small_mine[...] = small[...]
    small_mine[pl.ds(10 + at.group, 1), 0 : 3 * width] = mm(jnp.ones((8, length), BF16), grads[...], 1, 1)[0:1]
    at.send(small_mine, small_plane.at[0], sp_s.at[0], sp_r.at[0], at.sib, z)
    for k in (1, 2, 3):
        at.send(small_mine, small_plane.at[4 - k], sp_s.at[k], sp_r.at[4 - k], at.chip(k), z)
        at.send(small_mine, small_plane.at[7 - k], sp_s.at[3 + k], sp_r.at[7 - k], at.other(k), z)

    def rows(ch):
        return pl.ds(ch * step_rows, step_rows)

    def order(k):
        return jnp.where(at.pp == 0, 3 - k, (4 - k) % 4)

    def part_job(s):
        part[s] = mm(grads[:, pl.ds(pl.multiple_of(s * share, share), share)], w_t[...], 0, 0).astype(BF16)

        @pl.when(secondary)
        def _():
            for ch in range(CHUNKS):
                at.send(part.at[s, rows(ch)], sib_in.at[s, rows(ch)], part_s.at[s, ch], part_r.at[s, ch], at.sib, z)

    def line_job(place):
        s = at.line(place)
        for ch in range(CHUNKS):
            here = (s, rows(ch))

            @pl.when(jnp.logical_and(primary, place != at.p))
            def _():
                at.got(sib_in.at[here], part_r.at[s, ch])

                @pl.when(jnp.logical_and(at.p == 1, place >= 2))
                def _():
                    at.got(line_in.at[here], line_r.at[s, ch])
                    part[here] = total(part[here], sib_in[here], line_in[here]).astype(BF16)
                    at.send(part.at[here], line_in.at[here], line_s.at[s, ch], line_r.at[s, ch], at.d, at.own_line(2))

                @pl.when(jnp.logical_or(at.p == 0, place == 0))
                def _():
                    part[here] = total(part[here], sib_in[here]).astype(BF16)
                    at.send(part.at[here], line_in.at[here], line_s.at[s, ch], line_r.at[s, ch], at.d, at.own_line(1 - at.p))

    def part_step(k, _):
        part_job(at.line(order(k)))

        @pl.when(k > 0)
        def _():
            line_job(order(k - 1))

        return 0

    lax.fori_loop(0, 4, part_step, 0)
    line_job(order(3))

    made = mm(grads[:, 0:share], x_all[0])
    for s in range(1, 4):
        made = made + mm(grads[:, s * share : (s + 1) * share], x_all[s])
    made = made.astype(BF16)
    fourth = made.shape[0] // 4
    for i in range(4):
        dw_own[i] = made[i * fourth : (i + 1) * fourth]
    for k in (1, 2, 3):
        at.send(dw_own.at[(q + k) % 4], dw_in.at[3 - k], dwp_s.at[k - 1], dwp_r.at[3 - k], at.chip(k), z)

    plane_job(n_big)
    for k in range(7):
        at.got(small_plane.at[k], sp_r.at[k])
    small_mid[...] = total(small_mine[...], *(small_plane[k] for k in range(7)))
    for k in (1, 2, 3):
        at.send(small_mid, small_z.at[3 - k], sz_s.at[k - 1], sz_r.at[3 - k], at.d, (z + k) % 4)

    final_job(0)

    @pl.when(at.p == 2)
    def _():
        s = at.own_line(3)
        for ch in range(CHUNKS):
            here = (s, rows(ch))
            at.got(line_in.at[here], line_r.at[s, ch])
            at.send(line_in.at[here], line_in.at[here], line_s.at[s, ch], line_r.at[s, ch], at.d, s)

    def dw_rows(i):
        return pl.ds(pl.multiple_of(i * fourth, 16), fourth)

    for k in range(3):
        at.got(dw_in.at[k], dwp_r.at[k])
    dw_mid[...] = total(dw_own[q], dw_in[0], dw_in[1], dw_in[2]).astype(BF16)

    @pl.when(secondary)
    def _():
        at.send(dw_mid, dw_z, dwz_s.at[0], dwz_r.at[0], at.d, at.far)

    final_job(1)
    final_job(2)
    share_job(0)

    @pl.when(primary)
    def _():
        at.got(dw_z, dwz_r.at[0])
        piece = dw_out.at[dw_rows(q)]
        piece[...] = total(dw_mid[...], dw_z[...]).astype(BF16)
        for k in (1, 2, 3):
            at.send(piece, piece, dwo_s.at[k], dwo_r.at[q], at.chip(k), z)
        at.send(piece, piece, dwo_s.at[0], dwo_r.at[q], at.sib, z)

    for k in range(3):
        at.got(small_z.at[k], sz_r.at[k])
    small_out[...] = total(small_mid[...], small_z[0], small_z[1], small_z[2])

    skipped = skip_ref[0] == 1
    for ch in range(CHUNKS):
        at.got(line_in.at[z, rows(ch)], line_r.at[z, ch])

    @pl.when(primary)
    def _():
        for ch in range(CHUNKS):
            at.got(sib_in.at[z, rows(ch)], part_r.at[z, ch])
        grad = gone[...] + total(part[z], sib_in[z], line_in[z])
        frames_grad[...] = jnp.where(skipped, cot[...].astype(F32), grad).astype(BF16)

    @pl.when(secondary)
    def _():
        grad = gone[...] + line_in[z].astype(F32)
        frames_grad[...] = jnp.where(skipped, cot[...].astype(F32), grad).astype(BF16)

    share_job(1)
    share_job(2)

    @pl.when(primary)
    def _():
        for k in (1, 2, 3):
            i = (q + k) % 4
            piece = dw_out.at[dw_rows(i)]
            at.got(piece, dwo_r.at[i])
            at.send(piece, piece, dwf_s.at[k - 1], dwo_r.at[i], at.sib, z)

    @pl.when(secondary)
    def _():
        for i in range(4):
            at.got(dw_out.at[dw_rows(i)], dwo_r.at[i])

    for kind in range(3):
        end_job(kind)

    for g in range(4):
        mine = jnp.logical_and(primary, z == g)

        @pl.when(jnp.logical_not(mine))
        def _():
            at.sent(gmixed.at[pl.ds(g * width, width)], gm_s.at[g])

    for j in range(n_big):
        if j >= 4:
            at.sent(core_in.at[j], ci_s.at[j])
        for k in range(3):
            at.sent(plane_in.at[k, j], pl_s.at[j, k])

        @pl.when(z != j % 4)
        def _():
            at.sent(mid.at[j], z_s.at[j])

    at.sent(core_ino, ci_s.at[n_big])
    for k in range(3):
        at.sent(plane_ino.at[k], pl_s.at[n_big, k])
    for s in range(4):
        @pl.when(z != s)
        def _():
            at.sent(mido.at[s], z_s.at[n_big + s])

    for kind in range(3):
        for k in range(4):
            at.sent(final_piece(kind, q, c), ag_s.at[kind, k])
        for k in range(3):
            at.sent(final_piece(kind, q, c), agf_s.at[kind, k])
    for k in range(7):
        at.sent(small_mine, sp_s.at[k])
    for k in range(3):
        at.sent(small_mid, sz_s.at[k])
        at.sent(dw_mid, dwp_s.at[k])

    @pl.when(secondary)
    def _():
        at.sent(dw_mid, dwz_s.at[0])
        for s in range(4):
            for ch in range(CHUNKS):
                at.sent(part.at[s, rows(ch)], part_s.at[s, ch])

    @pl.when(primary)
    def _():
        for k in range(4):
            at.sent(dw_mid, dwo_s.at[k])
        for k in range(3):
            at.sent(dw_mid, dwf_s.at[k])
        for k in (1, 2, 3):
            for ch in range(CHUNKS):
                s = at.line((at.p + k) % 4)
                at.sent(part.at[s, rows(ch)], line_s.at[s, ch])

    @pl.when(at.p == 2)
    def _():
        for ch in range(CHUNKS):
            at.sent(line_in.at[at.own_line(3), rows(ch)], line_s.at[at.own_line(3), ch])


def run_backward(skip, gmixed, mixed_own, normed, act, ginner, gbranch, gatt, small, gone, cot,
                 x_all, w_t, mixed_heads, q_aug, k_aug, v_aug, k_t):
    share, d = gatt.shape
    f = act.shape[2]
    heads, _, length = q_aug.shape
    width = heads * HEAD_DIM
    dma, V = pltpu.SemaphoreType.DMA, pltpu.VMEM
    hd, hf, ho = d // 2, f // 2, d // 2
    return pl.pallas_call(
        backward_kernel,
        out_shape=(
            S((share, d)), S((3 * width, d)), S((d, f)), S((f, d)), S((width, d)), S((16, d), F32),
        ),
        in_specs=[SMEM] + [VMEM] * 17, out_specs=[VMEM] * 6,
        scratch_shapes=[
            V((4, width, share), BF16), V((heads, 128, length), BF16),
            V((heads, HEAD_DIM, length), F32), V((heads, HEAD_DIM, length), F32), V((3 * width, length), BF16),
            V((8, hd, d), BF16), V((4, hd, d), BF16), V((8, hd, d), BF16), V((3, 8, hd // 4, d), BF16), V((8, hd // 4, d), BF16),
            V((3, 2, hd // 4, d), BF16),
            V((2, 4, width, ho), BF16), V((4, width, ho), BF16), V((3, 4, width // 4, ho), BF16), V((4, width // 4, ho), BF16),
            V((3, width // 4, ho), BF16),
            V((4, share, d), BF16), V((4, share, d), BF16), V((4, share, d), BF16),
            V((4, 3 * width // 4, d), BF16), V((3, 3 * width // 4, d), BF16), V((3 * width // 4, d), BF16), V((3 * width // 4, d), BF16),
            V((16, d), F32), V((7, 16, d), F32), V((16, d), F32), V((3, 16, d), F32),
            dma((4,)), dma((4,)), dma((9,)), dma((9,)), dma((9, 3)), dma((9, 3)), dma((12,)), dma((3, 3)),
            dma((3, 4)), dma((3, 8)), dma((3, 3)),
            dma((4, CHUNKS)), dma((4, CHUNKS)), dma((4, CHUNKS)), dma((4, CHUNKS)), dma((3,)), dma((3,)), dma((1,)), dma((1,)),
            dma((4,)), dma((4,)), dma((3,)), dma((7,)), dma((7,)), dma((3,)), dma((3,)),
        ],
        compiler_params=pltpu.CompilerParams(vmem_limit_bytes=LIMIT, collective_id=1, has_side_effects=True),
        name="attention_backward",
    )(skip, gmixed, mixed_own, normed, act, ginner, gbranch, gatt, small, gone, cot,
      x_all, w_t, mixed_heads, q_aug, k_aug, v_aug, k_t)


def S(shape, dtype=BF16):
    return jax.ShapeDtypeStruct(shape, dtype)


def shards(
    frames, cotangent, segments, padding, skip_flag, w_query, b_query, w_key, w_value, b_value,
    w_out, b_out, gain_one, shift_one, w_up, b_up, w_down, b_down, gain_two, shift_two,
):
    mp = lax.axis_size("mp")
    share, d = frames.shape[1:]
    length = segments.shape[1]
    width = w_query.shape[1]
    heads = width // HEAD_DIM
    params = pltpu.CompilerParams(vmem_limit_bytes=LIMIT)
    scale = HEAD_DIM**-0.5
    own = frames[0]
    w_t = jnp.concatenate([w_query.T, w_key.T, w_value.T], 0)
    v_row = jnp.concatenate(
        [b_value.reshape(heads, HEAD_DIM), jnp.ones((heads, 3)), jnp.zeros((heads, 61))], 1
    ).reshape(1, heads * 128)
    seg, pad = segments[0], padding[0]
    ids = jnp.arange(4)
    ok = (seg[:, None] == ids[None]) & (pad[:, None] == 1)
    k_mask = jnp.concatenate(
        [jnp.zeros((length, 64)), jnp.where(ok, 0.0, -1e30), jnp.ones((length, 3)), jnp.zeros((length, 57))], 1
    ).astype(BF16)
    hot = jnp.concatenate([(seg[None] == ids[:, None]).astype(BF16), jnp.zeros((12, length), BF16)], 0)

    zero = jnp.zeros((d,), F32)
    bias_row = jnp.concatenate([b_query, jnp.zeros_like(b_query), b_value, jnp.zeros((d - 3 * width,), F32)])
    v_row = jnp.concatenate([v_row[0], jnp.zeros((d - heads * 128,), F32)])
    small = jnp.stack([b_up, bias_row, v_row] + [zero] * 5)
    x_all, w_t, mixed, mixed_own, q_aug, k_aug, v_aug, k_t, small_all, wup, wdown, wout = run_forward(
        own, w_t, small, k_mask, hot, w_up, w_down, w_out
    )
    wout = wout.reshape(mp * width, d)
    bup = small_all[:, 0]
    vec = jnp.stack([b_out, gain_one, shift_one, b_down, gain_two, shift_two] + [b_out] * 2)
    f = w_up.shape[1]
    layer, gone, gmixed, normed, act, ginner, gbranch, gatt, small = pl.pallas_call(
        middle_kernel,
        out_shape=(
            S((share, d)), S((share, d), F32), S((mp * width, share)), S((share, d)), S((mp, share, f)),
            S((mp, share, f)), S((share, d)), S((share, d)), S((16, d), F32),
        ),
        in_specs=[SMEM] + [VMEM] * 8, out_specs=[VMEM] * 9,
        scratch_shapes=[pltpu.VMEM((mp, share, f), F32)],
        compiler_params=params, name="feed_forward",
    )(skip_flag, mixed_own, own, cotangent[0], vec, bup, wout, wup, wdown)
    frames_grad, wgrad, gup, gdown, gout, small = run_backward(
        skip_flag, gmixed, mixed_own, normed, act, ginner, gbranch, gatt, small, gone, cotangent[0],
        x_all, w_t, mixed, q_aug, k_aug, v_aug, k_t,
    )
    dp = lax.axis_size("dp")
    if dp > 8:
        groups = [list(range(i, dp, 8)) for i in range(8)]
        wgrad, gup, gdown, gout, small = (
            lax.psum(v.astype(F32), "dp", axis_index_groups=groups) for v in (wgrad, gup, gdown, gout, small)
        )
    wgrad, gup, gdown, gout = (v.astype(F32) for v in (wgrad, gup, gdown, gout))
    z = lax.axis_index("mp")
    bias = small[10 + z]
    return (
        layer[None], frames_grad[None],
        wgrad[:width].T, bias[:width], wgrad[width : 2 * width].T, wgrad[2 * width :].T, bias[2 * width : 3 * width],
        gout, small[3], small[4], small[5],
        gup, small[6 + z], gdown, small[0], small[1], small[2],
    )


def solution(mesh):
    split = (P("dp", "mp", None), P(None, "mp"), P("mp"), P("mp", None), P())
    row, col, one, top, rep = split
    return jax.shard_map(
        shards,
        mesh=mesh,
        in_specs=(row, row, P("dp", None), P("dp", None), P("dp"), col, one, col, col, one, top, rep, rep, rep, col, one, top, rep, rep, rep),
        out_specs=(row, row, col, one, col, col, one, top, rep, rep, rep, col, one, top, rep, rep, rep),
        check_vma=False,
    )
```

```python
import functools

import jax
import jax.numpy as jnp
from jax import lax
from jax.experimental import pallas as pl
from jax.experimental.pallas import tpu as pltpu
from jax.sharding import PartitionSpec as P

HEAD_DIM = 64
F32, BF16 = jnp.float32, jnp.bfloat16
VMEM = pl.BlockSpec(memory_space=pltpu.VMEM)
SMEM = pl.BlockSpec(memory_space=pltpu.SMEM)
LIMIT = 60 << 20


def mm(a, b, ca=1, cb=0):
    return lax.dot_general(a, b, (((ca,), (cb,)), ((), ())), preferred_element_type=F32)


def row_of(ref):
    return ref[...].reshape(1, ref.shape[0])


def split3(v):
    hi = v.astype(BF16)
    rest = v - hi.astype(F32)
    mid = rest.astype(BF16)
    low = (rest - mid.astype(F32)).astype(BF16)
    return hi, mid, low


def pad_rows(parts, rows, width):
    parts = [p.astype(F32) for p in parts]
    have = sum(p.shape[0] for p in parts)
    return jnp.concatenate(parts + [jnp.zeros((rows - have, width), F32)], 0).astype(BF16)


def project(x, w_t, w_pad, bias_col, v_row, k_mask, one_hot, rows, q_aug, k_aug, v_aug, k_t, v_t):
    width = w_t.shape[0] // 3
    heads = width // HEAD_DIM
    every = mm(w_t, x, 1, 1) + bias_col
    every = jnp.concatenate([every[:width] * HEAD_DIM**-0.5, every[width:]], 0).astype(BF16)
    for h in range(heads):
        q_aug[h, 0:HEAD_DIM, rows] = every[h * HEAD_DIM : (h + 1) * HEAD_DIM]
        q_aug[h, HEAD_DIM : HEAD_DIM + 16, rows] = one_hot
        q_aug[h, HEAD_DIM + 16 :, rows] = jnp.zeros((48, x.shape[0]), BF16)
        k_t[h, :, rows] = every[width + h * HEAD_DIM : width + (h + 1) * HEAD_DIM]
        v_t[h, :, rows] = every[2 * width + h * HEAD_DIM : 2 * width + (h + 1) * HEAD_DIM]
    both = mm(x, w_pad, 1, 1)
    for h in range(heads):
        k_aug[h, rows, :] = both[:, h * 128 : (h + 1) * 128].astype(BF16) + k_mask
        at = (heads + h) * 128
        v_aug[h, rows, :] = (both[:, at : at + 128] + v_row[:, h * 128 : (h + 1) * 128]).astype(BF16)


def attend(h, cols, q_aug, k_aug, v_t):
    scores = mm(k_aug[h], q_aug[h, :, cols])
    peak = jnp.max(scores, 0, keepdims=True)
    raised = jnp.exp(scores - peak)
    summed = jnp.sum(raised, 0, keepdims=True)
    mixed = mm(v_t[h], raised.astype(BF16)) / summed
    one_hot = q_aug[h, HEAD_DIM : HEAD_DIM + 16, cols].astype(F32)[0:4]
    q_aug[h, HEAD_DIM : HEAD_DIM + 16, cols] = pad_rows((one_hot,) + split3(-(peak + jnp.log(summed))), 16, mixed.shape[1])
    return mixed.astype(BF16)


MESH = pl.DeviceIdType.MESH
CHUNKS = 3


class Place:
    def __init__(self):
        self.d, self.z = lax.axis_index("dp"), lax.axis_index("mp")
        d, z = self.d, self.z
        self.b = d % 2
        self.p = z + self.b * (3 - 2 * z)
        self.sib = d + 1 - 2 * self.b
        self.q = (d // 2) % 4
        self.base = d - d % 8
        q = self.q
        turn, over = q + 1 - 2 * (q % 2), (q + 2) % 4
        self.near_chip = turn + self.b * (over - turn)
        self.across_chip = over + self.b * (turn - over)
        self.opposite_chip = 3 - q
        self.near = self.base + 2 * self.near_chip + self.b
        self.across = self.base + 2 * self.across_chip + self.b
        self.primary = self.p < 2
        self.rb = z // 2
        self.row = d - self.b + self.rb
        self.pp = z + self.rb * (3 - 2 * z)
        self.far = (z + 2) % 4
        self.group = jnp.where(self.primary, z, self.far)

    def own_line(self, place):
        return place + self.b * (3 - 2 * place)

    def line(self, place):
        return place + self.rb * (3 - 2 * place)

    def chip(self, k):
        return self.base + 2 * ((self.q + k) % 4) + self.b

    def other(self, k):
        return self.base + 2 * ((self.q + k) % 4) + 1 - self.b

    def barrier(self):
        sem = pltpu.get_barrier_semaphore()
        others = [((self.d), (self.z + k) % 4) for k in (1, 2, 3)]
        others += [(self.sib, (self.z + k) % 4) for k in range(4)]
        others += [(self.chip(k), self.z) for k in (1, 2, 3)]
        others += [(self.other(k), self.z) for k in (1, 2, 3)]
        for dp, mp in others:
            pl.semaphore_signal(sem, inc=1, device_id=(dp, mp), device_id_type=MESH)
        pl.semaphore_wait(sem, len(others))

    def send(self, src, dst, send_sem, recv_sem, dp, mp):
        pltpu.make_async_remote_copy(
            src_ref=src, dst_ref=dst, send_sem=send_sem, recv_sem=recv_sem, device_id=(dp, mp), device_id_type=MESH
        ).start()

    def sent(self, src, send_sem):
        pltpu.make_async_remote_copy(
            src_ref=src, dst_ref=src, send_sem=send_sem, recv_sem=send_sem, device_id=(self.sib, self.z), device_id_type=MESH
        ).wait_send()

    def got(self, dst, recv_sem):
        pltpu.make_async_remote_copy(
            src_ref=dst, dst_ref=dst, send_sem=recv_sem, recv_sem=recv_sem, device_id=(self.sib, self.z), device_id_type=MESH
        ).wait_recv()


def forward_kernel(
    frames, w_query, w_key, w_value, b_query, b_value, b_up, segments, padding, w_up, w_down, w_out,
    x_all, w_t, mixed_heads, mixed_own, q_aug, k_aug, v_aug, k_t, small_all, up_all, down_all, out_all,
    relay, v_t, w_pad, kmask, hot, w_own, small_own, kmask_own, hot_own,
    small_s, small_r, mask_s, mask_r, wq_s, wq_r, x_s, x_r, relay_r, on_s, fwd_s, mix_s, mix_r, local,
    line_s, near_s, far_s, core_s, w_r,
):
    at = Place()
    heads = q_aug.shape[0]
    width = heads * HEAD_DIM
    share = frames.shape[0]
    step_rows = share // CHUNKS
    quarter = w_own.shape[0] // 4
    for i, w in enumerate((w_query, w_key, w_value)):
        w_own[i * width : (i + 1) * width] = w[...]
    small_own[...] = jnp.zeros_like(small_own)
    small_own[0:1, :] = row_of(b_up)
    small_own[1:2, 0:width] = row_of(b_query)
    values = row_of(b_value)
    small_own[1:2, 2 * width : 3 * width] = values
    for h in range(heads):
        small_own[2:3, h * 128 : h * 128 + HEAD_DIM] = values[:, h * HEAD_DIM : (h + 1) * HEAD_DIM]
        small_own[2:3, h * 128 + HEAD_DIM : h * 128 + HEAD_DIM + 3] = jnp.ones((1, 3), F32)
    at.barrier()
    primary = at.primary
    secondary = jnp.logical_not(primary)
    z = at.z

    def rows(ch):
        return pl.ds(ch * step_rows, step_rows)

    def piece(m, chip, core):
        if m == 2:
            n = w_out.shape[0] // 4
            half = w_out.shape[1] // 2
            return (pl.ds(pl.multiple_of(chip * n, 16), n), pl.ds(pl.multiple_of(core * half, 128), half))
        n = w_up.shape[0] // 8
        return (pl.ds(pl.multiple_of((2 * chip + core) * n, 16), n), slice(None))

    mats = ((w_up, up_all), (w_down, down_all), (w_out, out_all))

    for k in (1, 2, 3):
        at.send(small_own, small_all.at[z], small_s.at[k - 1], small_r.at[z], at.d, (z + k) % 4)
    wq_rows = pl.ds(pl.multiple_of(at.q * quarter, 16), quarter)
    first = jnp.where(at.p == 0, 1, at.p - 1)

    @pl.when(primary)
    def _():
        at.send(w_own.at[wq_rows], w_t.at[wq_rows], wq_s.at[0], wq_r.at[at.q], at.d, at.far)

    for ch in range(CHUNKS):
        @pl.when(at.p < 3)
        def _():
            at.send(frames.at[rows(ch)], x_all.at[z, rows(ch)], on_s.at[z, ch], x_r.at[z, ch], at.d, at.own_line(first))

        @pl.when(at.p == 3)
        def _():
            at.send(frames.at[rows(ch)], relay.at[rows(ch)], on_s.at[z, ch], relay_r.at[ch], at.d, at.own_line(2))

    @pl.when(primary)
    def _():
        for i in range(4):
            cols = slice(i * share, (i + 1) * share)
            seg, pad = segments[:, cols], padding[:, cols]
            row = lax.broadcasted_iota(jnp.int32, (128, share), 0)
            told = jnp.logical_and(row - HEAD_DIM == seg, pad == 1)
            mask = jnp.where(row < HEAD_DIM, 0.0, jnp.where(row < HEAD_DIM + 4, jnp.where(told, 0.0, -1e30), jnp.where(row < HEAD_DIM + 7, 1.0, 0.0)))
            kmask_own[cols, :] = mask.T.astype(BF16)
            hot_own[:, cols] = jnp.where(row[:16] == seg, 1.0, 0.0).astype(BF16)
        at.send(kmask_own, kmask, mask_s.at[0], mask_r.at[0], at.sib, z)
        at.send(hot_own, hot, mask_s.at[1], mask_r.at[1], at.sib, z)
        for ch in range(CHUNKS):
            at.send(frames.at[rows(ch)], x_all.at[z, rows(ch)], fwd_s.at[z, ch], x_r.at[z, ch], at.sib, z)
        pltpu.make_async_copy(w_own, w_t, local.at[2]).start()
        pltpu.make_async_copy(frames, x_all.at[z], local.at[3]).start()
        pltpu.make_async_copy(kmask_own, kmask, local.at[0]).start()
        pltpu.make_async_copy(hot_own, hot, local.at[1]).start()

    pltpu.make_async_copy(small_own, small_all.at[z], local.at[4]).start()

    def weights_first(m):
        src, dst = mats[m]
        r, c = piece(m, at.q, at.b)
        sem = w_r.at[m, z, 2 * at.q + at.b]

        @pl.when(z < 3)
        def _():
            at.send(src.at[r, c], dst.at[z, r, c], line_s.at[m, z, 0], sem, at.d, z + 1)

        @pl.when(z > 0)
        def _():
            at.send(src.at[r, c], dst.at[z, r, c], line_s.at[m, z, 1], sem, at.d, z - 1)

    def shard_at(n):
        low = z // 2
        near = z + low * (3 - 2 * z)
        s = jnp.where(near == 0, n + 1, 2 if n == 0 else (0 if n == 1 else 3))
        return s + low * (3 - 2 * s)

    def weights_line(m, n):
        dst = mats[m][1]
        s = shard_at(n)
        r, c = piece(m, at.q, at.b)
        block = dst.at[s, r, c]
        sem = w_r.at[m, s, 2 * at.q + at.b]
        at.got(block, sem)

        @pl.when(jnp.logical_and(s < z, z < 3))
        def _():
            at.send(block, block, line_s.at[m, s, 0], sem, at.d, z + 1)

        @pl.when(jnp.logical_and(s > z, z > 0))
        def _():
            at.send(block, block, line_s.at[m, s, 1], sem, at.d, z - 1)

        at.send(block, block, near_s.at[m, s], sem, at.near, z)
        at.send(block, block, far_s.at[m, s, 0], sem, at.across, z)
        at.send(block, block, core_s.at[m, s, 0], sem, at.sib, z)

    def weights_near(m, n):
        dst = mats[m][1]
        s = shard_at(n)
        r, c = piece(m, at.near_chip, at.b)
        block = dst.at[s, r, c]
        sem = w_r.at[m, s, 2 * at.near_chip + at.b]
        at.got(block, sem)
        at.send(block, block, far_s.at[m, s, 1], sem, at.across, z)
        at.send(block, block, core_s.at[m, s, 1], sem, at.sib, z)

    def weights_across(m, n):
        dst = mats[m][1]
        s = shard_at(n)
        for i, chip in ((2, at.across_chip), (3, at.opposite_chip)):
            r, c = piece(m, chip, at.b)
            block = dst.at[s, r, c]
            sem = w_r.at[m, s, 2 * chip + at.b]
            at.got(block, sem)
            at.send(block, block, core_s.at[m, s, i], sem, at.sib, z)

    for m in range(3):
        weights_first(m)

    def relay_job(ch):
        @pl.when(at.p == 2)
        def _():
            at.got(relay.at[rows(ch)], relay_r.at[ch])
            at.send(relay.at[rows(ch)], x_all.at[at.own_line(3), rows(ch)], x_s.at[ch], x_r.at[at.own_line(3), ch], at.d, at.own_line(1))

    relay_job(0)

    @pl.when(secondary)
    def _():
        at.got(w_t.at[wq_rows], wq_r.at[at.q])
        for k in (1, 2, 3):
            at.send(w_t.at[wq_rows], w_t.at[wq_rows], wq_s.at[k], wq_r.at[at.q], at.chip(k), z)

    for ch in range(1, CHUNKS):
        relay_job(ch)

    @pl.when(primary)
    def _():
        pltpu.make_async_copy(kmask_own, kmask, local.at[0]).wait()
        pltpu.make_async_copy(hot_own, hot, local.at[1]).wait()
        pltpu.make_async_copy(w_own, w_t, local.at[2]).wait()
        pltpu.make_async_copy(frames, x_all.at[z], local.at[3]).wait()

    pltpu.make_async_copy(small_own, small_all.at[z], local.at[4]).wait()
    for k in (1, 2, 3):
        at.got(small_all.at[(z + k) % 4], small_r.at[(z + k) % 4])

    @pl.when(secondary)
    def _():
        at.got(kmask, mask_r.at[0])
        at.got(hot, mask_r.at[1])
        for k in (1, 2, 3):
            other = (at.q + k) % 4
            at.got(w_t.at[pl.ds(pl.multiple_of(other * quarter, 16), quarter)], wq_r.at[other])

    w_pad[...] = jnp.zeros_like(w_pad)
    for i in range(2):
        for h in range(heads):
            w_pad[(i * heads + h) * 128 : (i * heads + h) * 128 + HEAD_DIM] = w_t[
                (i + 1) * width + h * HEAD_DIM : (i + 1) * width + (h + 1) * HEAD_DIM
            ]

    A, B, C = weights_line, weights_near, weights_across
    early = {1: ((A, 0, 0), (A, 1, 0), (A, 2, 0),), 2: ((A, 0, 1), (A, 1, 1), (A, 2, 1), (B, 0, 0), (B, 1, 0), (B, 2, 0),), 3: ((A, 0, 2), (C, 0, 0), (C, 1, 0), (C, 2, 0),)}
    jobs = {0: ((A, 1, 2), (B, 0, 1),), 1: ((A, 2, 2), (B, 1, 1),), 2: ((B, 2, 1), (C, 0, 1),), 3: ((C, 1, 1), (B, 0, 2),), 4: ((C, 2, 1), (B, 1, 2),), 5: ((B, 2, 2),), 6: ((C, 0, 2),), 7: ((C, 1, 2),), 8: ((C, 2, 2),)}

    def run_jobs(table, now):
        for when, todo in table.items():
            @pl.when(now == when)
            def _():
                for job, m, n in todo:
                    job(m, n)

    def gather_step(k, _):
        place = jnp.where(at.pp == 0, k, jnp.where(k == 0, 1, jnp.where(k == 1, 2, jnp.where(k == 2, 0, 3))))
        s = at.line(place)
        for ch in range(CHUNKS):
            block = x_all.at[s, rows(ch)]

            @pl.when(jnp.logical_or(k > 0, secondary))
            def _():
                at.got(block, x_r.at[s, ch])

            @pl.when(jnp.logical_and(k > 0, primary))
            def _():
                @pl.when(jnp.logical_and(at.p == 1, place >= 2))
                def _():
                    at.send(block, block, on_s.at[s, ch], x_r.at[s, ch], at.d, at.own_line(0))

                at.send(block, block, fwd_s.at[s, ch], x_r.at[s, ch], at.sib, z)

        run_jobs(early, k)
        cols = pl.ds(pl.multiple_of(s * share, share), share)
        biases = jnp.transpose(small_all[at.group])
        project(
            x_all[s], w_t[...], w_pad[...], biases[: 3 * width, 1:2], small_all[at.group, 2:3, : heads * 128], kmask[cols, :],
            hot[:, cols], cols, q_aug, k_aug, v_aug, k_t, v_t,
        )
        return 0

    lax.fori_loop(0, 4, gather_step, 0)

    def attend_step(t, _):
        turn, h = t // heads, t % heads
        i = (z + jnp.where(turn == 0, 2, jnp.where(turn == 1, 1, jnp.where(turn == 2, 3, 0)))) % 4
        cols = pl.ds(pl.multiple_of(i * share, share), share)
        mixed_heads[i, pl.ds(pl.multiple_of(h * HEAD_DIM, HEAD_DIM), HEAD_DIM), :] = attend(h, cols, q_aug, k_aug, v_t)
        mine = jnp.logical_and(primary, i == z)
        block = mixed_own.at[pl.ds(pl.multiple_of(at.group * width, 64), width)]

        @pl.when(jnp.logical_and(h == heads - 1, mine))
        def _():
            pltpu.make_async_copy(mixed_heads.at[i], block, mix_s.at[i]).start()

        @pl.when(jnp.logical_and(h == heads - 1, jnp.logical_not(mine)))
        def _():
            at.send(mixed_heads.at[i], block, mix_s.at[i], mix_r.at[at.group], at.row, i)

        run_jobs(jobs, t)
        return 0

    lax.fori_loop(0, 4 * heads, attend_step, 0)
    for job, m, n in jobs.get(99, ()):
        job(m, n)

    for g in range(4):
        mine = jnp.logical_and(primary, z == g)
        block = mixed_own.at[pl.ds(g * width, width)]

        @pl.when(jnp.logical_not(mine))
        def _():
            at.got(block, mix_r.at[g])

    for m, (_, dst) in enumerate(mats):
        for j in range(4):
            chip = (at.q + j) % 4
            r, c = piece(m, chip, 1 - at.b)
            for k in (1, 2, 3):
                s = (z + k) % 4
                at.got(dst.at[s, r, c], w_r.at[m, s, 2 * chip + 1 - at.b])

    for i in range(4):
        mine = jnp.logical_and(primary, z == i)

        @pl.when(mine)
        def _():
            block = mixed_own.at[pl.ds(pl.multiple_of(at.group * width, 64), width)]
            pltpu.make_async_copy(mixed_heads.at[i], block, mix_s.at[i]).wait()

        @pl.when(jnp.logical_not(mine))
        def _():
            at.sent(mixed_heads.at[i], mix_s.at[i])

    for k in range(3):
        at.sent(small_own, small_s.at[k])
    for ch in range(CHUNKS):
        at.sent(frames.at[rows(ch)], on_s.at[z, ch])

        @pl.when(at.p == 2)
        def _():
            at.sent(relay.at[rows(ch)], x_s.at[ch])

        @pl.when(at.p == 1)
        def _():
            for place in (2, 3):
                at.sent(x_all.at[at.own_line(place), rows(ch)], on_s.at[at.own_line(place), ch])

        @pl.when(primary)
        def _():
            for s in range(4):
                at.sent(x_all.at[s, rows(ch)], fwd_s.at[s, ch])

    @pl.when(primary)
    def _():
        at.sent(kmask_own, mask_s.at[0])
        at.sent(hot_own, mask_s.at[1])
        at.sent(w_own.at[wq_rows], wq_s.at[0])

    @pl.when(secondary)
    def _():
        for k in (1, 2, 3):
            at.sent(w_t.at[wq_rows], wq_s.at[k])

    for m, (src, dst) in enumerate(mats):
        r, c = piece(m, at.q, at.b)
        block = src.at[r, c]
        for s in range(4):
            @pl.when(jnp.logical_and(s <= z, z < 3))
            def _():
                at.sent(block, line_s.at[m, s, 0])

            @pl.when(jnp.logical_and(s >= z, z > 0))
            def _():
                at.sent(block, line_s.at[m, s, 1])

            @pl.when(s != z)
            def _():
                at.sent(block, near_s.at[m, s])
                for i in range(2):
                    at.sent(block, far_s.at[m, s, i])
                for i in range(4):
                    at.sent(block, core_s.at[m, s, i])


def run_forward(frames, w_query, w_key, w_value, b_query, b_value, b_up, segments, padding, w_up, w_down, w_out):
    share, d = frames.shape
    length = segments.shape[1]
    width = w_query.shape[0]
    heads = width // HEAD_DIM
    f = w_up.shape[1]
    any_ = pl.BlockSpec(memory_space=pl.ANY)
    dma, V = pltpu.SemaphoreType.DMA, pltpu.VMEM
    return pl.pallas_call(
        forward_kernel,
        out_shape=(
            S((4, share, d)), S((3 * width, d)), S((4, width, share)), S((4 * width, share)),
            S((heads, 128, length)), S((heads, length, 128)), S((heads, length, 128)), S((heads, HEAD_DIM, length)),
            S((4, 8, d), F32), S((4, d, f)), S((4, f, d)), S((4, width, d)),
        ),
        in_specs=[VMEM] * 9 + [any_] * 3, out_specs=[VMEM] * 9 + [any_] * 3,
        scratch_shapes=[
            V((share, d), BF16), V((heads, HEAD_DIM, length), BF16), V((2 * heads * 128, d), BF16),
            V((length, 128), BF16), V((16, length), BF16),
            V((3 * width, d), BF16), V((8, d), F32), V((length, 128), BF16), V((16, length), BF16),
            dma((3,)), dma((4,)), dma((2,)), dma((2,)), dma((4,)), dma((4,)), dma((CHUNKS,)), dma((4, CHUNKS)), dma((CHUNKS,)),
            dma((4, CHUNKS)), dma((4, CHUNKS)), dma((4,)), dma((4,)), dma((8,)),
            dma((3, 4, 2)), dma((3, 4)), dma((3, 4, 2)), dma((3, 4, 4)), dma((3, 4, 8)),
        ],
        compiler_params=pltpu.CompilerParams(vmem_limit_bytes=LIMIT, collective_id=0, has_side_effects=True),
        name="attention_forward",
    )(frames, w_query, w_key, w_value, b_query, b_value, b_up, segments, padding, w_up, w_down, w_out)


def norm_stats(v):
    centered = v - jnp.mean(v, -1, keepdims=True)
    r = lax.rsqrt(jnp.mean(centered * centered, -1, keepdims=True) + 1e-05)
    return centered * r, r


def norm_back(c, gain, hat, r):
    e = c * gain
    return r * (e - jnp.mean(e, -1, keepdims=True) - hat * jnp.mean(e * hat, -1, keepdims=True))


def middle_kernel(
    skip_ref, mixed_ref, frames_ref, cot_ref, b_out, gain_one, shift_one, b_down, gain_two, shift_two, bup_ref, w_out, w_up, w_down, out_all, up_all, down_all,
    layer_ref, gone_ref, gmixed_ref, normed_ref, act_ref, ginner_ref, gbranch_ref, gatt_ref, small_ref,
    slope_ref, wout_ref, wup_ref, wdown_ref, sems,
):
    z = lax.axis_index("mp")
    mats = ((w_out, out_all, wout_ref), (w_up, up_all, wup_ref), (w_down, down_all, wdown_ref))
    for m, (own, everyone, dst) in enumerate(mats):
        for s in range(4):
            @pl.when(z == s)
            def _():
                pltpu.make_async_copy(own, dst.at[s], sems.at[m, s]).start()

            @pl.when(z != s)
            def _():
                pltpu.make_async_copy(everyone.at[s], dst.at[s], sems.at[m, s]).start()

    def arrive(m, s):
        pltpu.make_async_copy(mats[m][0], mats[m][2].at[s], sems.at[m, s]).wait()

    skipped = skip_ref[0] == 1
    b_out, gain_one, shift_one, b_down, gain_two, shift_two = (row_of(v) for v in (b_out, gain_one, shift_one, b_down, gain_two, shift_two))
    frames = frames_ref[...].astype(F32)
    for s in range(4):
        arrive(0, s)
    all_out = wout_ref[...].reshape(mixed_ref.shape[0], frames.shape[1])
    attended = mm(mixed_ref[...], all_out, 0, 0) + b_out
    hat_one, r_one = norm_stats(frames + attended)
    normed = hat_one * gain_one + shift_one
    normed_ref[...] = normed.astype(BF16)
    parts = wup_ref.shape[0]
    branch = jnp.zeros_like(normed)
    for s in range(parts):
        arrive(1, s)
        inner = mm(normed_ref[...], wup_ref[s]) + bup_ref[s, 0:1, :]
        cdf = 0.5 * (1.0 + lax.erf(inner * (0.5**0.5)))
        slope_ref[s] = cdf + inner * (jnp.exp(-0.5 * inner * inner) * 0.3989422804014327)
        act = (inner * cdf).astype(BF16)
        act_ref[s] = act
        arrive(2, s)
        branch = branch + mm(act, wdown_ref[s])
    hat_two, r_two = norm_stats(normed + (branch + b_down))
    result = hat_two * gain_two + shift_two
    cot = cot_ref[...].astype(F32)
    layer_ref[...] = jnp.where(skipped, frames, result).astype(BF16)
    grad_out = jnp.where(skipped, 0.0, cot)
    grad_two = norm_back(grad_out, gain_two, hat_two, r_two)
    gbranch = grad_two.astype(BF16)
    gbranch_ref[...] = gbranch
    small_ref[10:16, :] = jnp.zeros_like(small_ref[10:16, :])
    small_ref[0:1, :] = jnp.sum(gbranch.astype(F32), 0, keepdims=True)
    small_ref[1:2, :] = jnp.sum(grad_out * hat_two, 0, keepdims=True)
    small_ref[2:3, :] = jnp.sum(grad_out, 0, keepdims=True)
    grad_normed = grad_two
    for s in range(parts):
        gact = mm(gbranch_ref[...], wdown_ref[s], 1, 1)
        ginner = (gact * slope_ref[s]).astype(BF16)
        ginner_ref[s] = ginner
        small_ref[6 + s : 7 + s, :] = jnp.sum(ginner.astype(F32), 0, keepdims=True)
        grad_normed = grad_normed + mm(ginner, wup_ref[s], 1, 1)
    grad_one = norm_back(grad_normed, gain_one, hat_one, r_one)
    gone_ref[...] = grad_one
    gatt = grad_one.astype(BF16)
    gatt_ref[...] = gatt
    small_ref[3:4, :] = jnp.sum(gatt.astype(F32), 0, keepdims=True)
    small_ref[4:5, :] = jnp.sum(grad_normed * hat_one, 0, keepdims=True)
    small_ref[5:6, :] = jnp.sum(grad_normed, 0, keepdims=True)
    gmixed_ref[...] = mm(all_out, gatt, 1, 1).astype(BF16)


def attend_back(h, i, cols, q_aug, k_aug, v_aug, k_t, do_aug, dq_acc, dk_acc, dv_acc):
    weights = jnp.exp(mm(k_aug[h], q_aug[h, :, cols]))
    rounded = weights.astype(BF16)
    dv_acc[h] += mm(do_aug[h, 0:HEAD_DIM, cols], rounded, 1, 1)
    grad = (weights * mm(v_aug[h], do_aug[h, :, cols])).astype(BF16)
    dk_acc[h] += mm(q_aug[h, 0:HEAD_DIM, cols], grad, 1, 1)
    return mm(k_t[h], grad)


def total(first, *others):
    out = first.astype(F32)
    for other in others:
        out = out + other.astype(F32)
    return out


def backward_kernel(
    skip_ref, gmixed, mixed_own, normed, act, ginner, gbranch, gatt, small, gone, cot,
    x_all, w_t, mixed_heads, q_aug, k_aug, v_aug, k_t,
    frames_grad, dw_out, up_out, down_out, out_out, small_out,
    do_in, do_aug, dk_acc, dv_acc, grads,
    big, away, core_in, near_in, across_in, mid, z_in, bigo, core_ino, near_ino, across_ino, mido, z_ino,
    part, sib_in, line_in, dw_own, dw_in, dw_mid, dw_z, small_mine, small_plane, small_mid, small_z,
    gm_s, gm_r, ci_s, ci_r, nr_s, nr_r, ac_s, ac_r, z_s, z_r, ag_s, ag_r,
    part_s, part_r, line_s, line_r, dwp_s, dwp_r, dwz_s, dwz_r, dwo_s, dwo_r, dwf_s, sp_s, sp_r, sz_s, sz_r,
):
    at = Place()
    heads = q_aug.shape[0]
    width = heads * HEAD_DIM
    share = gatt.shape[0]
    length = x_all.shape[0] * share
    step_rows = share // CHUNKS
    z, c, q = at.z, at.b, at.q
    primary = at.primary
    secondary = jnp.logical_not(primary)
    at.barrier()

    for g in range(4):
        block = gmixed.at[pl.ds(g * width, width)]
        near = at.b == g // 2
        to_d = jnp.where(near, at.d, at.sib)
        to_z = jnp.where(near, g, (g + 2) % 4)
        mine = jnp.logical_and(near, z == g)

        @pl.when(mine)
        def _():
            pltpu.make_async_copy(block, do_in.at[z], gm_s.at[g]).start()

        @pl.when(jnp.logical_not(mine))
        def _():
            at.send(block, do_in.at[z], gm_s.at[g], gm_r.at[z], to_d, to_z)

    n_big = 8
    half = big.shape[1]
    quarter = half // 4
    halfo = bigo.shape[3]
    quartero = bigo.shape[2] // 4
    finals = (down_out, up_out, out_out)

    def big_rows(chip):
        return pl.ds(pl.multiple_of(chip * quarter, 16), quarter)

    def out_rows(chip):
        return pl.ds(pl.multiple_of(chip * quartero, 16), quartero)

    def weight_job(j):
        if j < n_big:
            kind, s = j // 4, j % 4
            made = mm(act[s], gbranch[...], 0, 0) if kind == 0 else mm(normed[...], ginner[s], 0, 0)
            made = made.astype(BF16)
            if j >= 4:
                at.sent(away.at[j % 4], ci_s.at[j - 4])

            @pl.when(c == 0)
            def _():
                big[j] = made[:half]
                away[j % 4] = made[half:]

            @pl.when(c == 1)
            def _():
                big[j] = made[half:]
                away[j % 4] = made[:half]

            at.send(away.at[j % 4], core_in.at[j], ci_s.at[j], ci_r.at[j], at.sib, z)
        else:
            for s in range(4):
                made = mm(mixed_own[s * width : (s + 1) * width, :], gatt[...])
                for i in range(2):
                    bigo[i, s] = made[:, i * halfo : (i + 1) * halfo].astype(BF16)
            at.send(bigo.at[1 - c], core_ino, ci_s.at[j], ci_r.at[j], at.sib, z)

    def core_job(j):
        at.got(core_in.at[j] if j < n_big else core_ino, ci_r.at[j])
        if j < n_big:
            big[j] = total(big[j], core_in[j]).astype(BF16)
        else:
            bigo[c] = total(bigo[c], core_ino[...]).astype(BF16)
        for i, chip in enumerate((at.near_chip, at.opposite_chip)):
            if j < n_big:
                at.send(big.at[j, big_rows(chip)], near_in.at[i, j], nr_s.at[j, i], nr_r.at[j, i], at.near, z)
            else:
                at.send(bigo.at[c, :, out_rows(chip)], near_ino.at[i], nr_s.at[j, i], nr_r.at[j, i], at.near, z)

    def near_job(j):
        if j < n_big:
            for i in range(2):
                at.got(near_in.at[i, j], nr_r.at[j, i])
            near_in[1, j] = total(big[j, big_rows(at.across_chip)], near_in[1, j]).astype(BF16)
            at.send(near_in.at[1, j], across_in.at[j], ac_s.at[j], ac_r.at[j], at.across, z)
        else:
            for i in range(2):
                at.got(near_ino.at[i], nr_r.at[j, i])
            near_ino[1] = total(bigo[c, :, out_rows(at.across_chip)], near_ino[1]).astype(BF16)
            at.send(near_ino.at[1], across_ino, ac_s.at[j], ac_r.at[j], at.across, z)

    def plane_job(j):
        if j < n_big:
            kind, s = j // 4, j % 4
            at.got(across_in.at[j], ac_r.at[j])
            mid[j] = total(big[j, big_rows(q)], near_in[0, j], across_in[j]).astype(BF16)

            @pl.when(z != s)
            def _():
                slot = 3 - (s - z + 4) % 4
                at.send(mid.at[j], z_in.at[slot, kind], z_s.at[j], z_r.at[kind, slot], at.d, s)
        else:
            at.got(across_ino, ac_r.at[j])
            mido[...] = total(bigo[c, :, out_rows(q)], near_ino[0], across_ino[...]).astype(BF16)
            for s in range(4):
                @pl.when(z != s)
                def _():
                    slot = 3 - (s - z + 4) % 4
                    at.send(mido.at[s], z_ino.at[slot], z_s.at[j + s], z_r.at[2, slot], at.d, s)

    def final_piece(kind, chip, core):
        if kind < 2:
            return finals[kind].at[pl.ds(pl.multiple_of(core * half + chip * quarter, 16), quarter)]
        return out_out.at[out_rows(chip), pl.ds(pl.multiple_of(core * halfo, 128), halfo)]

    def final_job(kind):
        for k in range(3):
            at.got(z_in.at[k, kind] if kind < 2 else z_ino.at[k], z_r.at[kind, k])
        piece = final_piece(kind, q, c)
        if kind < 2:
            piece[...] = total(mid[4 * kind + z], z_in[0, kind], z_in[1, kind], z_in[2, kind]).astype(BF16)
        else:
            piece[...] = total(mido[z], z_ino[0], z_ino[1], z_ino[2]).astype(BF16)
        sem = ag_r.at[kind, 2 * q + c]
        at.send(piece, piece, ag_s.at[kind, 0], sem, at.near, z)
        at.send(piece, piece, ag_s.at[kind, 1], sem, at.across, z)
        at.send(piece, piece, ag_s.at[kind, 2], sem, at.sib, z)

    def pass_job(kind):
        piece = final_piece(kind, at.near_chip, c)
        sem = ag_r.at[kind, 2 * at.near_chip + c]
        at.got(piece, sem)
        at.send(piece, piece, ag_s.at[kind, 3], sem, at.across, z)
        at.send(piece, piece, ag_s.at[kind, 4], sem, at.sib, z)

    def share_job(kind):
        for i, chip in enumerate((at.across_chip, at.opposite_chip)):
            piece = final_piece(kind, chip, c)
            sem = ag_r.at[kind, 2 * chip + c]
            at.got(piece, sem)
            at.send(piece, piece, ag_s.at[kind, 5 + i], sem, at.sib, z)

    def end_job(kind):
        for k in range(4):
            chip = (q + k) % 4
            at.got(final_piece(kind, chip, 1 - c), ag_r.at[kind, 2 * chip + 1 - c])

    for j in range(n_big + 1):
        weight_job(j)
        if j >= 2:
            core_job(j - 2)
    core_job(n_big - 1)
    core_job(n_big)

    def block_of(turn):
        low = z // 2
        near = z + low * (3 - 2 * z)
        s = jnp.where(near == 0, turn, jnp.where(turn == 0, 1, jnp.where(turn == 1, 2, jnp.where(turn == 2, 0, 3))))
        return s + low * (3 - 2 * s)

    def prepare(i):
        mine = jnp.logical_and(primary, z == i)

        @pl.when(mine)
        def _():
            pltpu.make_async_copy(gmixed.at[pl.ds(pl.multiple_of(i * width, 64), width)], do_in.at[i], gm_s.at[i]).wait()

        @pl.when(jnp.logical_not(mine))
        def _():
            at.got(do_in.at[i], gm_r.at[i])

        cols = pl.ds(pl.multiple_of(i * share, share), share)
        for h in range(heads):
            hs = slice(h * HEAD_DIM, (h + 1) * HEAD_DIM)
            do = do_in[i, hs, :]
            do_aug[h, 0:HEAD_DIM, cols] = do
            inner = jnp.sum(do.astype(F32) * mixed_heads[i, hs, :].astype(F32), 0, keepdims=True)
            do_aug[h, HEAD_DIM : HEAD_DIM + 16, cols] = pad_rows(split3(-inner), 16, share)
            do_aug[h, HEAD_DIM + 16 :, cols] = jnp.zeros((48, share), BF16)

    dk_acc[...] = jnp.zeros_like(dk_acc)
    dv_acc[...] = jnp.zeros_like(dv_acc)

    N, M, Q = near_job, plane_job, final_job
    jobs = {-1: ((N, 0), (N, 1),), 0: ((N, 2), (M, 0),), 1: ((M, 1),), 2: ((N, 3), (M, 2),), 4: ((N, 4), (M, 3),), 6: ((N, 5), (M, 4),), 8: ((N, 6), (M, 5), (Q, 0),), 10: ((N, 7), (M, 6),)}

    def attention_step(t, _):
        i, h = block_of(t // heads), t % heads

        @pl.when(h == 0)
        def _():
            prepare(i)

        cols = pl.ds(pl.multiple_of(i * share, share), share)
        dq = attend_back(h, i, cols, q_aug, k_aug, v_aug, k_t, do_aug, None, dk_acc, dv_acc)
        hs = pl.ds(pl.multiple_of(h * HEAD_DIM, HEAD_DIM), HEAD_DIM)
        grads[hs, cols] = (dq.astype(BF16).astype(F32) * HEAD_DIM**-0.5).astype(BF16)
        for when, todo in jobs.items():
            if 0 <= when < 99:
                @pl.when(t == when)
                def _():
                    for job, j in todo:
                        job(j)

        return 0

    for job, j in jobs.get(-1, ()):
        job(j)
    lax.fori_loop(0, 4 * heads, attention_step, 0)
    for job, j in jobs.get(99, ()):
        job(j)
    for h in range(heads):
        grads[width + h * HEAD_DIM : width + (h + 1) * HEAD_DIM, :] = dk_acc[h].astype(BF16)
        grads[2 * width + h * HEAD_DIM : 2 * width + (h + 1) * HEAD_DIM, :] = dv_acc[h].astype(BF16)


    small_mine[...] = small[...]
    small_mine[pl.ds(10 + at.group, 1), 0 : 3 * width] = mm(jnp.ones((8, length), BF16), grads[...], 1, 1)[0:1]
    at.send(small_mine, small_plane.at[0], sp_s.at[0], sp_r.at[0], at.sib, z)
    for k in (1, 2, 3):
        at.send(small_mine, small_plane.at[4 - k], sp_s.at[k], sp_r.at[4 - k], at.chip(k), z)
        at.send(small_mine, small_plane.at[7 - k], sp_s.at[3 + k], sp_r.at[7 - k], at.other(k), z)

    def rows(ch):
        return pl.ds(ch * step_rows, step_rows)

    def order(k):
        return jnp.where(at.pp == 0, 3 - k, (4 - k) % 4)

    def part_job(s):
        part[s] = mm(grads[:, pl.ds(pl.multiple_of(s * share, share), share)], w_t[...], 0, 0).astype(BF16)

        @pl.when(secondary)
        def _():
            for ch in range(CHUNKS):
                at.send(part.at[s, rows(ch)], sib_in.at[s, rows(ch)], part_s.at[s, ch], part_r.at[s, ch], at.sib, z)

    def line_job(place):
        s = at.line(place)
        for ch in range(CHUNKS):
            here = (s, rows(ch))

            @pl.when(jnp.logical_and(primary, place != at.p))
            def _():
                at.got(sib_in.at[here], part_r.at[s, ch])

                @pl.when(jnp.logical_and(at.p == 1, place >= 2))
                def _():
                    at.got(line_in.at[here], line_r.at[s, ch])
                    part[here] = total(part[here], sib_in[here], line_in[here]).astype(BF16)
                    at.send(part.at[here], line_in.at[here], line_s.at[s, ch], line_r.at[s, ch], at.d, at.own_line(2))

                @pl.when(jnp.logical_or(at.p == 0, place == 0))
                def _():
                    part[here] = total(part[here], sib_in[here]).astype(BF16)
                    at.send(part.at[here], line_in.at[here], line_s.at[s, ch], line_r.at[s, ch], at.d, at.own_line(1 - at.p))

    for k in range(4):
        part_job(at.line(order(k)))
        if k > 0:
            @pl.when(jnp.logical_or(at.p == 0, k == 1))
            def _():
                line_job(order(k - 1))

    @pl.when(at.p == 0)
    def _():
        line_job(order(3))

    made = mm(grads[:, 0:share], x_all[0])
    for s in range(1, 4):
        made = made + mm(grads[:, s * share : (s + 1) * share], x_all[s])
    made = made.astype(BF16)
    fourth = made.shape[0] // 4
    for i in range(4):
        dw_own[i] = made[i * fourth : (i + 1) * fourth]
    at.send(dw_own.at[at.near_chip], dw_in.at[0], dwp_s.at[0], dwp_r.at[0], at.near, z)
    at.send(dw_own.at[at.opposite_chip], dw_in.at[1], dwp_s.at[1], dwp_r.at[1], at.near, z)

    def dw_rows(i):
        return pl.ds(pl.multiple_of(i * fourth, 16), fourth)

    def small_sum(_):
        for k in range(7):
            at.got(small_plane.at[k], sp_r.at[k])
        small_mid[...] = total(small_mine[...], *(small_plane[k] for k in range(7)))
        for k in (1, 2, 3):
            at.send(small_mid, small_z.at[3 - k], sz_s.at[k - 1], sz_r.at[3 - k], at.d, (z + k) % 4)

    def small_end(_):
        for k in range(3):
            at.got(small_z.at[k], sz_r.at[k])
        small_out[...] = total(small_mid[...], small_z[0], small_z[1], small_z[2])

    def onward(k):
        @pl.when(at.p == 1)
        def _():
            line_job(order(k))

        if k == 1:
            @pl.when(at.p == 2)
            def _():
                s = at.own_line(3)
                for ch in range(CHUNKS):
                    here = (s, rows(ch))
                    at.got(line_in.at[here], line_r.at[s, ch])
                    at.send(line_in.at[here], line_in.at[here], line_s.at[s, ch], line_r.at[s, ch], at.d, s)

    def dw_across(_):
        for k in range(2):
            at.got(dw_in.at[k], dwp_r.at[k])
        dw_in[1] = total(dw_own[at.across_chip], dw_in[1]).astype(BF16)
        at.send(dw_in.at[1], dw_in.at[2], dwp_s.at[2], dwp_r.at[2], at.across, z)

    def dw_plane(_):
        at.got(dw_in.at[2], dwp_r.at[2])
        dw_mid[...] = total(dw_own[q], dw_in[0], dw_in[2]).astype(BF16)

        @pl.when(secondary)
        def _():
            at.send(dw_mid, dw_z, dwz_s.at[0], dwz_r.at[0], at.d, at.far)

    def dw_final(_):
        @pl.when(primary)
        def _():
            at.got(dw_z, dwz_r.at[0])
            piece = dw_out.at[dw_rows(q)]
            piece[...] = total(dw_mid[...], dw_z[...]).astype(BF16)
            at.send(piece, piece, dwo_s.at[0], dwo_r.at[q], at.near, z)
            at.send(piece, piece, dwo_s.at[1], dwo_r.at[q], at.across, z)
            at.send(piece, piece, dwo_s.at[2], dwo_r.at[q], at.sib, z)

    def dw_pass(_):
        @pl.when(primary)
        def _():
            i = at.near_chip
            piece = dw_out.at[dw_rows(i)]
            at.got(piece, dwo_r.at[i])
            at.send(piece, piece, dwo_s.at[3], dwo_r.at[i], at.across, z)
            at.send(piece, piece, dwf_s.at[0], dwo_r.at[i], at.sib, z)

    N, M, Q, U, V = near_job, plane_job, final_job, pass_job, share_job
    for job, j in ((M, 7), (N, 8), (small_sum, 0), (dw_across, 0), (dw_plane, 0), (onward, 1), (M, 8), (onward, 2), (dw_final, 0), (Q, 1), (U, 0), (dw_pass, 0), (onward, 3), (V, 0), (Q, 2), (U, 1), (small_end, 0), (U, 2), (V, 1), (V, 2)):
        job(j)

    skipped = skip_ref[0] == 1
    for ch in range(CHUNKS):
        at.got(line_in.at[z, rows(ch)], line_r.at[z, ch])

    @pl.when(primary)
    def _():
        for ch in range(CHUNKS):
            at.got(sib_in.at[z, rows(ch)], part_r.at[z, ch])
        grad = gone[...] + total(part[z], sib_in[z], line_in[z])
        frames_grad[...] = jnp.where(skipped, cot[...].astype(F32), grad).astype(BF16)

    @pl.when(secondary)
    def _():
        grad = gone[...] + line_in[z].astype(F32)
        frames_grad[...] = jnp.where(skipped, cot[...].astype(F32), grad).astype(BF16)


    @pl.when(primary)
    def _():
        for k, i in ((1, at.across_chip), (2, at.opposite_chip)):
            piece = dw_out.at[dw_rows(i)]
            at.got(piece, dwo_r.at[i])
            at.send(piece, piece, dwf_s.at[k], dwo_r.at[i], at.sib, z)

    @pl.when(secondary)
    def _():
        for i in range(4):
            at.got(dw_out.at[dw_rows(i)], dwo_r.at[i])

    for kind in range(3):
        end_job(kind)

    for g in range(4):
        mine = jnp.logical_and(primary, z == g)

        @pl.when(jnp.logical_not(mine))
        def _():
            at.sent(gmixed.at[pl.ds(g * width, width)], gm_s.at[g])

    for j in range(n_big):
        if j >= 4:
            at.sent(core_in.at[j], ci_s.at[j])
        for k in range(2):
            at.sent(near_in.at[k, j], nr_s.at[j, k])
        at.sent(across_in.at[j], ac_s.at[j])

        @pl.when(z != j % 4)
        def _():
            at.sent(mid.at[j], z_s.at[j])

    at.sent(core_ino, ci_s.at[n_big])
    for k in range(2):
        at.sent(near_ino.at[k], nr_s.at[n_big, k])
    at.sent(across_ino, ac_s.at[n_big])
    for s in range(4):
        @pl.when(z != s)
        def _():
            at.sent(mido.at[s], z_s.at[n_big + s])

    for kind in range(3):
        for k in range(7):
            at.sent(final_piece(kind, q, c), ag_s.at[kind, k])
    for k in range(7):
        at.sent(small_mine, sp_s.at[k])
    for k in range(3):
        at.sent(small_mid, sz_s.at[k])
        at.sent(dw_mid, dwp_s.at[k])

    @pl.when(secondary)
    def _():
        at.sent(dw_mid, dwz_s.at[0])
        for s in range(4):
            for ch in range(CHUNKS):
                at.sent(part.at[s, rows(ch)], part_s.at[s, ch])

    @pl.when(primary)
    def _():
        for k in range(4):
            at.sent(dw_mid, dwo_s.at[k])
        for k in range(3):
            at.sent(dw_mid, dwf_s.at[k])
        for k in (1, 2, 3):
            for ch in range(CHUNKS):
                s = at.line((at.p + k) % 4)
                at.sent(part.at[s, rows(ch)], line_s.at[s, ch])

    @pl.when(at.p == 2)
    def _():
        for ch in range(CHUNKS):
            at.sent(line_in.at[at.own_line(3), rows(ch)], line_s.at[at.own_line(3), ch])


def run_backward(skip, gmixed, mixed_own, normed, act, ginner, gbranch, gatt, small, gone, cot,
                 x_all, w_t, mixed_heads, q_aug, k_aug, v_aug, k_t):
    share, d = gatt.shape
    f = act.shape[2]
    heads, _, length = q_aug.shape
    width = heads * HEAD_DIM
    dma, V = pltpu.SemaphoreType.DMA, pltpu.VMEM
    hd, hf, ho = d // 2, f // 2, d // 2
    return pl.pallas_call(
        backward_kernel,
        out_shape=(
            S((share, d)), S((3 * width, d)), S((d, f)), S((f, d)), S((width, d)), S((16, d), F32),
        ),
        in_specs=[SMEM] + [VMEM] * 17, out_specs=[VMEM] * 6,
        scratch_shapes=[
            V((4, width, share), BF16), V((heads, 128, length), BF16),
            V((heads, HEAD_DIM, length), F32), V((heads, HEAD_DIM, length), F32), V((3 * width, length), BF16),
            V((8, hd, d), BF16), V((4, hd, d), BF16), V((8, hd, d), BF16), V((2, 8, hd // 4, d), BF16), V((8, hd // 4, d), BF16), V((8, hd // 4, d), BF16),
            V((3, 2, hd // 4, d), BF16),
            V((2, 4, width, ho), BF16), V((4, width, ho), BF16), V((2, 4, width // 4, ho), BF16), V((4, width // 4, ho), BF16), V((4, width // 4, ho), BF16),
            V((3, width // 4, ho), BF16),
            V((4, share, d), BF16), V((4, share, d), BF16), V((4, share, d), BF16),
            V((4, 3 * width // 4, d), BF16), V((3, 3 * width // 4, d), BF16), V((3 * width // 4, d), BF16), V((3 * width // 4, d), BF16),
            V((16, d), F32), V((7, 16, d), F32), V((16, d), F32), V((3, 16, d), F32),
            dma((4,)), dma((4,)), dma((9,)), dma((9,)), dma((9, 2)), dma((9, 2)), dma((9,)), dma((9,)), dma((12,)), dma((3, 3)),
            dma((3, 7)), dma((3, 8)),
            dma((4, CHUNKS)), dma((4, CHUNKS)), dma((4, CHUNKS)), dma((4, CHUNKS)), dma((3,)), dma((3,)), dma((1,)), dma((1,)),
            dma((4,)), dma((4,)), dma((3,)), dma((7,)), dma((7,)), dma((3,)), dma((3,)),
        ],
        compiler_params=pltpu.CompilerParams(vmem_limit_bytes=LIMIT, collective_id=1, has_side_effects=True),
        name="attention_backward",
    )(skip, gmixed, mixed_own, normed, act, ginner, gbranch, gatt, small, gone, cot,
      x_all, w_t, mixed_heads, q_aug, k_aug, v_aug, k_t)


def last_kernel(dw, up, down, out, small, *outs):
    z = lax.axis_index("mp")
    d_query, d_key, d_value, d_up, d_down, d_out, b_query, b_value, b_up = outs[:9]
    width = d_out.shape[0]
    for i, target in enumerate((d_query, d_key, d_value)):
        target[...] = dw[i * width : (i + 1) * width].astype(F32)
    d_up[...] = up[...].astype(F32)
    d_down[...] = down[...].astype(F32)
    d_out[...] = out[...].astype(F32)
    bias = small[pl.ds(10 + z, 1), :]
    b_query[...] = bias[:, 0:width].reshape(width)
    b_value[...] = bias[:, 2 * width : 3 * width].reshape(width)
    b_up[...] = small[pl.ds(6 + z, 1), :].reshape(small.shape[1])
    for i, target in enumerate(outs[9:]):
        target[...] = small[i : i + 1, :].reshape(small.shape[1])


def S(shape, dtype=BF16):
    return jax.ShapeDtypeStruct(shape, dtype)


def shards(
    frames, cotangent, segments, padding, skip_flag, w_query, b_query, w_key, w_value, b_value,
    w_out, b_out, gain_one, shift_one, w_up, b_up, w_down, b_down, gain_two, shift_two,
):
    mp = lax.axis_size("mp")
    share, d = frames.shape[1:]
    length = segments.shape[1]
    width = w_query.shape[1]
    heads = width // HEAD_DIM
    params = pltpu.CompilerParams(vmem_limit_bytes=LIMIT)
    own = frames[0]
    x_all, w_t, mixed, mixed_own, q_aug, k_aug, v_aug, k_t, small_all, wup, wdown, wout = run_forward(
        own, w_query.T, w_key.T, w_value.T, b_query, b_value, b_up, segments, padding, w_up, w_down, w_out
    )
    f = w_up.shape[1]
    layer, gone, gmixed, normed, act, ginner, gbranch, gatt, small = pl.pallas_call(
        middle_kernel,
        out_shape=(
            S((share, d)), S((share, d), F32), S((mp * width, share)), S((share, d)), S((mp, share, f)),
            S((mp, share, f)), S((share, d)), S((share, d)), S((16, d), F32),
        ),
        in_specs=[SMEM] + [VMEM] * 10 + [pl.BlockSpec(memory_space=pl.ANY)] * 6, out_specs=[VMEM] * 9,
        scratch_shapes=[
            pltpu.VMEM((mp, share, f), F32), pltpu.VMEM((mp, width, d), BF16), pltpu.VMEM((mp, d, f), BF16),
            pltpu.VMEM((mp, f, d), BF16), pltpu.SemaphoreType.DMA((3, 4)),
        ],
        compiler_params=params, name="feed_forward",
    )(skip_flag, mixed_own, own, cotangent[0], b_out, gain_one, shift_one, b_down, gain_two, shift_two, small_all, w_out, w_up, w_down, wout, wup, wdown)
    frames_grad, wgrad, gup, gdown, gout, small = run_backward(
        skip_flag, gmixed, mixed_own, normed, act, ginner, gbranch, gatt, small, gone, cotangent[0],
        x_all, w_t, mixed, q_aug, k_aug, v_aug, k_t,
    )
    dp = lax.axis_size("dp")
    if dp > 8:
        groups = [list(range(i, dp, 8)) for i in range(8)]
        wgrad, gup, gdown, gout, small = (
            lax.psum(v.astype(F32), "dp", axis_index_groups=groups) for v in (wgrad, gup, gdown, gout, small)
        )
    d_query, d_key, d_value, d_up, d_down, d_out, b_q, b_v, b_u, *rest = pl.pallas_call(
        last_kernel,
        out_shape=tuple(
            S(s, F32) for s in [(width, d)] * 3 + [(d, f), (f, d), (width, d), (width,), (width,), (f,)] + [(d,)] * 6
        ),
        in_specs=[VMEM] * 5, out_specs=[VMEM] * 15, compiler_params=params, name="outputs",
    )(wgrad, gup, gdown, gout, small)
    b_down_grad, gain_two_grad, shift_two_grad, b_out_grad, gain_one_grad, shift_one_grad = rest
    return (
        layer[None], frames_grad[None], d_query.T, b_q, d_key.T, d_value.T, b_v,
        d_out, b_out_grad, gain_one_grad, shift_one_grad,
        d_up, b_u, d_down, b_down_grad, gain_two_grad, shift_two_grad,
    )


def solution(mesh):
    split = (P("dp", "mp", None), P(None, "mp"), P("mp"), P("mp", None), P())
    row, col, one, top, rep = split
    return jax.shard_map(
        shards,
        mesh=mesh,
        in_specs=(row, row, P("dp", None), P("dp", None), P("dp"), col, one, col, col, one, top, rep, rep, rep, col, one, top, rep, rep, rep),
        out_specs=(row, row, col, one, col, col, one, top, rep, rep, rep, col, one, top, rep, rep, rep),
        check_vma=False,
    )
```

```python
import functools

import jax
import jax.numpy as jnp
from jax import lax
from jax.experimental import pallas as pl
from jax.experimental.pallas import tpu as pltpu
from jax.sharding import PartitionSpec as P

HEAD_DIM = 64
F32, BF16 = jnp.float32, jnp.bfloat16
VMEM = pl.BlockSpec(memory_space=pltpu.VMEM)
SMEM = pl.BlockSpec(memory_space=pltpu.SMEM)
LIMIT = 60 << 20


def mm(a, b, ca=1, cb=0):
    return lax.dot_general(a, b, (((ca,), (cb,)), ((), ())), preferred_element_type=F32)


def row_of(ref):
    return ref[...].reshape(1, ref.shape[0])


def split3(v):
    hi = v.astype(BF16)
    rest = v - hi.astype(F32)
    mid = rest.astype(BF16)
    low = (rest - mid.astype(F32)).astype(BF16)
    return hi, mid, low


def pad_rows(parts, rows, width):
    parts = [p.astype(F32) for p in parts]
    have = sum(p.shape[0] for p in parts)
    return jnp.concatenate(parts + [jnp.zeros((rows - have, width), F32)], 0).astype(BF16)


def project(x, w_t, w_pad, bias_col, v_row, k_mask, one_hot, rows, q_aug, k_aug, v_aug, k_t, v_t):
    width = w_t.shape[0] // 3
    heads = width // HEAD_DIM
    every = mm(w_t, x, 1, 1) + bias_col
    every = jnp.concatenate([every[:width] * HEAD_DIM**-0.5, every[width:]], 0).astype(BF16)
    for h in range(heads):
        q_aug[h, 0:HEAD_DIM, rows] = every[h * HEAD_DIM : (h + 1) * HEAD_DIM]
        q_aug[h, HEAD_DIM : HEAD_DIM + 16, rows] = one_hot
        q_aug[h, HEAD_DIM + 16 :, rows] = jnp.zeros((48, x.shape[0]), BF16)
        k_t[h, :, rows] = every[width + h * HEAD_DIM : width + (h + 1) * HEAD_DIM]
        v_t[h, :, rows] = every[2 * width + h * HEAD_DIM : 2 * width + (h + 1) * HEAD_DIM]
    both = mm(x, w_pad, 1, 1)
    for h in range(heads):
        k_aug[h, rows, :] = both[:, h * 128 : (h + 1) * 128].astype(BF16) + k_mask
        at = (heads + h) * 128
        v_aug[h, rows, :] = (both[:, at : at + 128] + v_row[:, h * 128 : (h + 1) * 128]).astype(BF16)


def attend(h, cols, q_aug, k_aug, v_t):
    scores = mm(k_aug[h], q_aug[h, :, cols])
    peak = jnp.max(scores, 0, keepdims=True)
    raised = jnp.exp(scores - peak)
    summed = jnp.sum(raised, 0, keepdims=True)
    mixed = mm(v_t[h], raised.astype(BF16)) / summed
    one_hot = q_aug[h, HEAD_DIM : HEAD_DIM + 16, cols].astype(F32)[0:4]
    q_aug[h, HEAD_DIM : HEAD_DIM + 16, cols] = pad_rows((one_hot,) + split3(-(peak + jnp.log(summed))), 16, mixed.shape[1])
    return mixed.astype(BF16)


def norm_stats(v):
    centered = v - jnp.mean(v, -1, keepdims=True)
    r = lax.rsqrt(jnp.mean(centered * centered, -1, keepdims=True) + 1e-05)
    return centered * r, r


def norm_back(c, gain, hat, r):
    e = c * gain
    return r * (e - jnp.mean(e, -1, keepdims=True) - hat * jnp.mean(e * hat, -1, keepdims=True))


def feed_forward(
    skip_ref, mixed_ref, frames_ref, cot_ref, b_out, gain_one, shift_one, b_down, gain_two, shift_two, small_all,
    wout_ref, wup_ref, wdown_ref, arrive, leave, outside,
    layer_ref, gone_ref, gmixed_ref, normed_ref, act_ref, ginner_ref, gbranch_ref, gatt_ref, small_ref, slope_ref,
):
    skipped = skip_ref[0] == 1
    mixed_h, layer_h, gone_h, gmixed_h, normed_h, act_h, ginner_h, gbranch_h, gatt_h = outside
    b_out, gain_one, shift_one, b_down, gain_two, shift_two = (row_of(v) for v in (b_out, gain_one, shift_one, b_down, gain_two, shift_two))
    frames = frames_ref[...].astype(F32)
    arrive(2)
    all_out = wout_ref[...].reshape(mixed_ref.shape[0], frames.shape[1])
    attended = mm(mixed_ref[...], all_out, 0, 0) + b_out
    hat_one, r_one = norm_stats(frames + attended)
    normed = hat_one * gain_one + shift_one
    normed_ref[...] = normed.astype(BF16)
    leave(7, mixed_ref, mixed_h)
    leave(8, normed_ref, normed_h)
    parts = wup_ref.shape[0]
    arrive(0)
    for s in range(parts):
        inner = mm(normed_ref[...], wup_ref[s]) + small_all[s, 0:1, :]
        cdf = 0.5 * (1.0 + lax.erf(inner * (0.5**0.5)))
        slope_ref[s] = cdf + inner * (jnp.exp(-0.5 * inner * inner) * 0.3989422804014327)
        act_ref[s] = (inner * cdf).astype(BF16)
        leave(9, act_ref, act_h, s)
    arrive(1)
    branch = mm(act_ref[0], wdown_ref[0])
    for s in range(1, parts):
        branch = branch + mm(act_ref[s], wdown_ref[s])
    hat_two, r_two = norm_stats(normed + (branch + b_down))
    result = hat_two * gain_two + shift_two
    cot = cot_ref[...].astype(F32)
    layer_ref[...] = jnp.where(skipped, frames, result).astype(BF16)
    grad_out = jnp.where(skipped, 0.0, cot)
    grad_two = norm_back(grad_out, gain_two, hat_two, r_two)
    gbranch = grad_two.astype(BF16)
    gbranch_ref[...] = gbranch
    leave(13, layer_ref, layer_h)
    leave(14, gbranch_ref, gbranch_h)
    small_ref[10:16, :] = jnp.zeros_like(small_ref[10:16, :])
    small_ref[0:1, :] = jnp.sum(gbranch.astype(F32), 0, keepdims=True)
    small_ref[1:2, :] = jnp.sum(grad_out * hat_two, 0, keepdims=True)
    small_ref[2:3, :] = jnp.sum(grad_out, 0, keepdims=True)
    grad_normed = grad_two
    for s in range(parts):
        gact = mm(gbranch_ref[...], wdown_ref[s], 1, 1)
        ginner = (gact * slope_ref[s]).astype(BF16)
        ginner_ref[s] = ginner
        leave(15, ginner_ref, ginner_h, s)
        small_ref[6 + s : 7 + s, :] = jnp.sum(ginner.astype(F32), 0, keepdims=True)
        grad_normed = grad_normed + mm(ginner, wup_ref[s], 1, 1)
    grad_one = norm_back(grad_normed, gain_one, hat_one, r_one)
    gone_ref[...] = grad_one
    gatt = grad_one.astype(BF16)
    gatt_ref[...] = gatt
    leave(19, gone_ref, gone_h)
    leave(20, gatt_ref, gatt_h)
    small_ref[3:4, :] = jnp.sum(gatt.astype(F32), 0, keepdims=True)
    small_ref[4:5, :] = jnp.sum(grad_normed * hat_one, 0, keepdims=True)
    small_ref[5:6, :] = jnp.sum(grad_normed, 0, keepdims=True)
    gmixed_ref[...] = mm(all_out, gatt, 1, 1).astype(BF16)
    leave(21, gmixed_ref, gmixed_h)


MESH = pl.DeviceIdType.MESH
CHUNKS = 3


class Place:
    def __init__(self):
        self.d, self.z = lax.axis_index("dp"), lax.axis_index("mp")
        d, z = self.d, self.z
        self.b = d % 2
        self.p = z + self.b * (3 - 2 * z)
        self.sib = d + 1 - 2 * self.b
        self.q = (d // 2) % 4
        self.base = d - d % 8
        q = self.q
        turn, over = q + 1 - 2 * (q % 2), (q + 2) % 4
        self.near_chip = turn + self.b * (over - turn)
        self.across_chip = over + self.b * (turn - over)
        self.opposite_chip = 3 - q
        self.near = self.base + 2 * self.near_chip + self.b
        self.across = self.base + 2 * self.across_chip + self.b
        self.primary = self.p < 2
        self.rb = z // 2
        self.row = d - self.b + self.rb
        self.pp = z + self.rb * (3 - 2 * z)
        self.far = (z + 2) % 4
        self.group = jnp.where(self.primary, z, self.far)

    def own_line(self, place):
        return place + self.b * (3 - 2 * place)

    def line(self, place):
        return place + self.rb * (3 - 2 * place)

    def chip(self, k):
        return self.base + 2 * ((self.q + k) % 4) + self.b

    def other(self, k):
        return self.base + 2 * ((self.q + k) % 4) + 1 - self.b

    def barrier(self):
        sem = pltpu.get_barrier_semaphore()
        others = [((self.d), (self.z + k) % 4) for k in (1, 2, 3)]
        others += [(self.sib, (self.z + k) % 4) for k in range(4)]
        others += [(self.chip(k), self.z) for k in (1, 2, 3)]
        others += [(self.other(k), self.z) for k in (1, 2, 3)]
        for dp, mp in others:
            pl.semaphore_signal(sem, inc=1, device_id=(dp, mp), device_id_type=MESH)
        pl.semaphore_wait(sem, len(others))

    def send(self, src, dst, send_sem, recv_sem, dp, mp):
        pltpu.make_async_remote_copy(
            src_ref=src, dst_ref=dst, send_sem=send_sem, recv_sem=recv_sem, device_id=(dp, mp), device_id_type=MESH
        ).start()

    def sent(self, src, send_sem):
        pltpu.make_async_remote_copy(
            src_ref=src, dst_ref=src, send_sem=send_sem, recv_sem=send_sem, device_id=(self.sib, self.z), device_id_type=MESH
        ).wait_send()

    def got(self, dst, recv_sem):
        pltpu.make_async_remote_copy(
            src_ref=dst, dst_ref=dst, send_sem=recv_sem, recv_sem=recv_sem, device_id=(self.sib, self.z), device_id_type=MESH
        ).wait_recv()


def forward_kernel(
    skip, frames, cot, w_query, w_key, w_value, b_query, b_value, b_up, b_out, gain_one, shift_one, b_down, gain_two, shift_two,
    segments, padding, w_up, w_down, w_out,
    x_all_h, w_t_h, mixed_heads_h, mixed_own_h, q_aug_h, k_aug_h, v_aug_h, k_t_h,
    layer_h, gone_h, gmixed_h, normed_h, act_h, ginner_h, gbranch_h, gatt_h, small_sums,
    x_all, w_t, mixed_heads, mixed_own, q_aug, k_aug, v_aug, k_t,
    layer, gone, gmixed, normed, act, ginner, gbranch, gatt, out_sems,
    small_all, up_all, down_all, out_all, slope,
    relay, v_t, w_pad, kmask, hot, w_own, small_own, kmask_own, hot_own,
    small_s, small_r, mask_s, mask_r, wq_s, wq_r, x_s, x_r, relay_r, on_s, fwd_s, mix_s, mix_r, local,
    line_s, near_s, far_s, core_s, w_r,
):
    at = Place()
    heads = q_aug.shape[0]
    width = heads * HEAD_DIM
    share = frames.shape[0]
    step_rows = share // CHUNKS
    quarter = w_own.shape[0] // 4
    for i, w in enumerate((w_query, w_key, w_value)):
        w_own[i * width : (i + 1) * width] = w[...]
    small_own[...] = jnp.zeros_like(small_own)
    small_own[0:1, :] = row_of(b_up)
    small_own[1:2, 0:width] = row_of(b_query)
    values = row_of(b_value)
    small_own[1:2, 2 * width : 3 * width] = values
    for h in range(heads):
        small_own[2:3, h * 128 : h * 128 + HEAD_DIM] = values[:, h * HEAD_DIM : (h + 1) * HEAD_DIM]
        small_own[2:3, h * 128 + HEAD_DIM : h * 128 + HEAD_DIM + 3] = jnp.ones((1, 3), F32)
    at.barrier()
    primary = at.primary
    secondary = jnp.logical_not(primary)
    z = at.z

    def rows(ch):
        return pl.ds(ch * step_rows, step_rows)

    def piece(m, chip, core):
        if m == 2:
            n = w_out.shape[0] // 4
            half = w_out.shape[1] // 2
            return (pl.ds(pl.multiple_of(chip * n, 16), n), pl.ds(pl.multiple_of(core * half, 128), half))
        n = w_up.shape[0] // 8
        return (pl.ds(pl.multiple_of((2 * chip + core) * n, 16), n), slice(None))

    mats = ((w_up, up_all), (w_down, down_all), (w_out, out_all))

    for k in (1, 2, 3):
        at.send(small_own, small_all.at[z], small_s.at[k - 1], small_r.at[z], at.d, (z + k) % 4)
    wq_rows = pl.ds(pl.multiple_of(at.q * quarter, 16), quarter)
    first = jnp.where(at.p == 0, 1, at.p - 1)

    @pl.when(primary)
    def _():
        at.send(w_own.at[wq_rows], w_t.at[wq_rows], wq_s.at[0], wq_r.at[at.q], at.d, at.far)

    for ch in range(CHUNKS):
        @pl.when(at.p < 3)
        def _():
            at.send(frames.at[rows(ch)], x_all.at[z, rows(ch)], on_s.at[z, ch], x_r.at[z, ch], at.d, at.own_line(first))

        @pl.when(at.p == 3)
        def _():
            at.send(frames.at[rows(ch)], relay.at[rows(ch)], on_s.at[z, ch], relay_r.at[ch], at.d, at.own_line(2))

    @pl.when(primary)
    def _():
        for i in range(4):
            cols = slice(i * share, (i + 1) * share)
            seg, pad = segments[:, cols], padding[:, cols]
            row = lax.broadcasted_iota(jnp.int32, (128, share), 0)
            told = jnp.logical_and(row - HEAD_DIM == seg, pad == 1)
            mask = jnp.where(row < HEAD_DIM, 0.0, jnp.where(row < HEAD_DIM + 4, jnp.where(told, 0.0, -1e30), jnp.where(row < HEAD_DIM + 7, 1.0, 0.0)))
            kmask_own[cols, :] = mask.T.astype(BF16)
            hot_own[:, cols] = jnp.where(row[:16] == seg, 1.0, 0.0).astype(BF16)
        at.send(kmask_own, kmask, mask_s.at[0], mask_r.at[0], at.sib, z)
        at.send(hot_own, hot, mask_s.at[1], mask_r.at[1], at.sib, z)
        for ch in range(CHUNKS):
            at.send(frames.at[rows(ch)], x_all.at[z, rows(ch)], fwd_s.at[z, ch], x_r.at[z, ch], at.sib, z)
        pltpu.make_async_copy(w_own, w_t, local.at[2]).start()
        pltpu.make_async_copy(frames, x_all.at[z], local.at[3]).start()
        pltpu.make_async_copy(kmask_own, kmask, local.at[0]).start()
        pltpu.make_async_copy(hot_own, hot, local.at[1]).start()

    pltpu.make_async_copy(small_own, small_all.at[z], local.at[4]).start()

    def weights_first(m):
        src, dst = mats[m]
        r, c = piece(m, at.q, at.b)
        sem = w_r.at[m, z, 2 * at.q + at.b]

        @pl.when(z < 3)
        def _():
            at.send(src.at[r, c], dst.at[z, r, c], line_s.at[m, z, 0], sem, at.d, z + 1)

        @pl.when(z > 0)
        def _():
            at.send(src.at[r, c], dst.at[z, r, c], line_s.at[m, z, 1], sem, at.d, z - 1)

    def shard_at(n):
        low = z // 2
        near = z + low * (3 - 2 * z)
        s = jnp.where(near == 0, n + 1, 2 if n == 0 else (0 if n == 1 else 3))
        return s + low * (3 - 2 * s)

    def weights_line(m, n):
        dst = mats[m][1]
        s = shard_at(n)
        r, c = piece(m, at.q, at.b)
        block = dst.at[s, r, c]
        sem = w_r.at[m, s, 2 * at.q + at.b]
        at.got(block, sem)

        @pl.when(jnp.logical_and(s < z, z < 3))
        def _():
            at.send(block, block, line_s.at[m, s, 0], sem, at.d, z + 1)

        @pl.when(jnp.logical_and(s > z, z > 0))
        def _():
            at.send(block, block, line_s.at[m, s, 1], sem, at.d, z - 1)

        at.send(block, block, near_s.at[m, s], sem, at.near, z)
        at.send(block, block, far_s.at[m, s, 0], sem, at.across, z)
        at.send(block, block, core_s.at[m, s, 0], sem, at.sib, z)

    def weights_near(m, n):
        dst = mats[m][1]
        s = shard_at(n)
        r, c = piece(m, at.near_chip, at.b)
        block = dst.at[s, r, c]
        sem = w_r.at[m, s, 2 * at.near_chip + at.b]
        at.got(block, sem)
        at.send(block, block, far_s.at[m, s, 1], sem, at.across, z)
        at.send(block, block, core_s.at[m, s, 1], sem, at.sib, z)

    def weights_across(m, n):
        dst = mats[m][1]
        s = shard_at(n)
        for i, chip in ((2, at.across_chip), (3, at.opposite_chip)):
            r, c = piece(m, chip, at.b)
            block = dst.at[s, r, c]
            sem = w_r.at[m, s, 2 * chip + at.b]
            at.got(block, sem)
            at.send(block, block, core_s.at[m, s, i], sem, at.sib, z)

    for m in range(3):
        weights_first(m)
    for m, (src, dst) in enumerate(mats):
        pltpu.make_async_copy(src, dst.at[z], local.at[5 + m]).start()

    def relay_job(ch):
        @pl.when(at.p == 2)
        def _():
            at.got(relay.at[rows(ch)], relay_r.at[ch])
            at.send(relay.at[rows(ch)], x_all.at[at.own_line(3), rows(ch)], x_s.at[ch], x_r.at[at.own_line(3), ch], at.d, at.own_line(1))

    relay_job(0)

    @pl.when(secondary)
    def _():
        at.got(w_t.at[wq_rows], wq_r.at[at.q])
        for k in (1, 2, 3):
            at.send(w_t.at[wq_rows], w_t.at[wq_rows], wq_s.at[k], wq_r.at[at.q], at.chip(k), z)

    for ch in range(1, CHUNKS):
        relay_job(ch)

    @pl.when(primary)
    def _():
        pltpu.make_async_copy(kmask_own, kmask, local.at[0]).wait()
        pltpu.make_async_copy(hot_own, hot, local.at[1]).wait()
        pltpu.make_async_copy(w_own, w_t, local.at[2]).wait()
        pltpu.make_async_copy(frames, x_all.at[z], local.at[3]).wait()

    pltpu.make_async_copy(small_own, small_all.at[z], local.at[4]).wait()
    for k in (1, 2, 3):
        at.got(small_all.at[(z + k) % 4], small_r.at[(z + k) % 4])

    @pl.when(secondary)
    def _():
        at.got(kmask, mask_r.at[0])
        at.got(hot, mask_r.at[1])
        for k in (1, 2, 3):
            other = (at.q + k) % 4
            at.got(w_t.at[pl.ds(pl.multiple_of(other * quarter, 16), quarter)], wq_r.at[other])

    w_pad[...] = jnp.zeros_like(w_pad)
    for i in range(2):
        for h in range(heads):
            w_pad[(i * heads + h) * 128 : (i * heads + h) * 128 + HEAD_DIM] = w_t[
                (i + 1) * width + h * HEAD_DIM : (i + 1) * width + (h + 1) * HEAD_DIM
            ]

    A, B, C = weights_line, weights_near, weights_across
    early = {1: ((A, 0, 0), (A, 2, 0), (A, 1, 0),), 2: ((A, 0, 1), (A, 2, 1), (A, 1, 1), (B, 0, 0), (B, 2, 0), (B, 1, 0),), 3: ((A, 0, 2), (C, 0, 0), (C, 2, 0), (C, 1, 0),)}
    jobs = {0: ((A, 2, 2), (B, 0, 1),), 1: ((B, 2, 1), (A, 1, 2),), 3: ((C, 0, 1), (B, 1, 1),), 4: ((C, 2, 1), (B, 0, 2),), 5: ((B, 2, 2), (C, 1, 1),), 7: ((C, 0, 2), (C, 2, 2),), 9: ((B, 1, 2),)}

    def run_jobs(table, now):
        for when, todo in table.items():
            @pl.when(now == when)
            def _():
                for job, m, n in todo:
                    job(m, n)

    def gather_step(k, _):
        place = jnp.where(at.pp == 0, k, jnp.where(k == 0, 1, jnp.where(k == 1, 2, jnp.where(k == 2, 0, 3))))
        s = at.line(place)
        for ch in range(CHUNKS):
            block = x_all.at[s, rows(ch)]

            @pl.when(jnp.logical_or(k > 0, secondary))
            def _():
                at.got(block, x_r.at[s, ch])

            @pl.when(jnp.logical_and(k > 0, primary))
            def _():
                @pl.when(jnp.logical_and(at.p == 1, place >= 2))
                def _():
                    at.send(block, block, on_s.at[s, ch], x_r.at[s, ch], at.d, at.own_line(0))

                at.send(block, block, fwd_s.at[s, ch], x_r.at[s, ch], at.sib, z)

        run_jobs(early, k)
        cols = pl.ds(pl.multiple_of(s * share, share), share)
        biases = jnp.transpose(small_all[at.group])
        project(
            x_all[s], w_t[...], w_pad[...], biases[: 3 * width, 1:2], small_all[at.group, 2:3, : heads * 128], kmask[cols, :],
            hot[:, cols], cols, q_aug, k_aug, v_aug, k_t, v_t,
        )
        return 0

    lax.fori_loop(0, 4, gather_step, 0)

    def attend_step(t, _):
        turn, h = t // heads, t % heads
        i = (z + jnp.where(turn == 0, 2, jnp.where(turn == 1, 1, jnp.where(turn == 2, 3, 0)))) % 4
        cols = pl.ds(pl.multiple_of(i * share, share), share)
        mixed_heads[i, pl.ds(pl.multiple_of(h * HEAD_DIM, HEAD_DIM), HEAD_DIM), :] = attend(h, cols, q_aug, k_aug, v_t)
        mine = jnp.logical_and(primary, i == z)
        block = mixed_own.at[pl.ds(pl.multiple_of(at.group * width, 64), width)]

        @pl.when(jnp.logical_and(h == heads - 1, mine))
        def _():
            pltpu.make_async_copy(mixed_heads.at[i], block, mix_s.at[i]).start()

        @pl.when(jnp.logical_and(h == heads - 1, jnp.logical_not(mine)))
        def _():
            at.send(mixed_heads.at[i], block, mix_s.at[i], mix_r.at[at.group], at.row, i)

        run_jobs(jobs, t)
        return 0

    lax.fori_loop(0, 4 * heads, attend_step, 0)
    for job, m, n in jobs.get(99, ()):
        job(m, n)

    def leave(i, src, dst, part=None):
        if part is not None:
            src, dst, i = src.at[part], dst.at[part], i + part
        left.append((src, dst, out_sems.at[i]))
        pltpu.make_async_copy(src, dst, out_sems.at[i]).start()

    left = []
    for i, (src, dst) in enumerate((
        (x_all, x_all_h), (w_t, w_t_h), (mixed_heads, mixed_heads_h), (q_aug, q_aug_h), (k_aug, k_aug_h), (v_aug, v_aug_h), (k_t, k_t_h),
    )):
        leave(i, src, dst)

    def arrive(m):
        if m == 2:
            for g in range(4):
                mine = jnp.logical_and(primary, z == g)
                block = mixed_own.at[pl.ds(g * width, width)]

                @pl.when(mine)
                def _():
                    pltpu.make_async_copy(mixed_heads.at[g], block, mix_s.at[g]).wait()

                @pl.when(jnp.logical_not(mine))
                def _():
                    at.got(block, mix_r.at[g])

        for job, m2, n in {0: ((C, 1, 2),)}.get(m, ()):
            job(m2, n)
        src, dst = mats[m]
        pltpu.make_async_copy(src, dst.at[z], local.at[5 + m]).wait()
        for j in range(4):
            chip = (at.q + j) % 4
            r, c = piece(m, chip, 1 - at.b)
            for k in (1, 2, 3):
                s = (z + k) % 4
                at.got(dst.at[s, r, c], w_r.at[m, s, 2 * chip + 1 - at.b])

    feed_forward(
        skip, mixed_own, frames, cot, b_out, gain_one, shift_one, b_down, gain_two, shift_two, small_all,
        out_all, up_all, down_all, arrive, leave,
        (mixed_own_h, layer_h, gone_h, gmixed_h, normed_h, act_h, ginner_h, gbranch_h, gatt_h),
        layer, gone, gmixed, normed, act, ginner, gbranch, gatt, small_sums, slope,
    )
    for src, dst, sem in left:
        pltpu.make_async_copy(src, dst, sem).wait()

    for i in range(4):
        mine = jnp.logical_and(primary, z == i)

        @pl.when(jnp.logical_not(mine))
        def _():
            at.sent(mixed_heads.at[i], mix_s.at[i])

    for k in range(3):
        at.sent(small_own, small_s.at[k])
    for ch in range(CHUNKS):
        at.sent(frames.at[rows(ch)], on_s.at[z, ch])

        @pl.when(at.p == 2)
        def _():
            at.sent(relay.at[rows(ch)], x_s.at[ch])

        @pl.when(at.p == 1)
        def _():
            for place in (2, 3):
                at.sent(x_all.at[at.own_line(place), rows(ch)], on_s.at[at.own_line(place), ch])

        @pl.when(primary)
        def _():
            for s in range(4):
                at.sent(x_all.at[s, rows(ch)], fwd_s.at[s, ch])

    @pl.when(primary)
    def _():
        at.sent(kmask_own, mask_s.at[0])
        at.sent(hot_own, mask_s.at[1])
        at.sent(w_own.at[wq_rows], wq_s.at[0])

    @pl.when(secondary)
    def _():
        for k in (1, 2, 3):
            at.sent(w_t.at[wq_rows], wq_s.at[k])

    for m, (src, dst) in enumerate(mats):
        r, c = piece(m, at.q, at.b)
        block = src.at[r, c]
        for s in range(4):
            @pl.when(jnp.logical_and(s <= z, z < 3))
            def _():
                at.sent(block, line_s.at[m, s, 0])

            @pl.when(jnp.logical_and(s >= z, z > 0))
            def _():
                at.sent(block, line_s.at[m, s, 1])

            @pl.when(s != z)
            def _():
                at.sent(block, near_s.at[m, s])
                for i in range(2):
                    at.sent(block, far_s.at[m, s, i])
                for i in range(4):
                    at.sent(block, core_s.at[m, s, i])


def run_forward(
    skip, frames, cot, w_query, w_key, w_value, b_query, b_value, b_up, b_out, gain_one, shift_one, b_down, gain_two, shift_two,
    segments, padding, w_up, w_down, w_out,
):
    share, d = frames.shape
    length = segments.shape[1]
    width = w_query.shape[0]
    heads = width // HEAD_DIM
    f = w_up.shape[1]
    any_ = pl.BlockSpec(memory_space=pl.ANY)
    dma, V = pltpu.SemaphoreType.DMA, pltpu.VMEM
    return pl.pallas_call(
        forward_kernel,
        out_shape=(
            S((4, share, d)), S((3 * width, d)), S((4, width, share)), S((4 * width, share)),
            S((heads, 128, length)), S((heads, length, 128)), S((heads, length, 128)), S((heads, HEAD_DIM, length)),
            S((share, d)), S((share, d), F32), S((4 * width, share)), S((share, d)), S((4, share, f)),
            S((4, share, f)), S((share, d)), S((share, d)), S((16, d), F32),
        ),
        in_specs=[SMEM] + [VMEM] * 16 + [any_] * 3, out_specs=[any_] * 16 + [VMEM],
        scratch_shapes=[
            V((4, share, d), BF16), V((3 * width, d), BF16), V((4, width, share), BF16), V((4 * width, share), BF16),
            V((heads, 128, length), BF16), V((heads, length, 128), BF16), V((heads, length, 128), BF16), V((heads, HEAD_DIM, length), BF16),
            V((share, d), BF16), V((share, d), F32), V((4 * width, share), BF16), V((share, d), BF16), V((4, share, f), BF16),
            V((4, share, f), BF16), V((share, d), BF16), V((share, d), BF16), dma((22,)),
            V((4, 8, d), F32), V((4, d, f), BF16), V((4, f, d), BF16), V((4, width, d), BF16), V((4, share, f), F32),
            V((share, d), BF16), V((heads, HEAD_DIM, length), BF16), V((2 * heads * 128, d), BF16),
            V((length, 128), BF16), V((16, length), BF16),
            V((3 * width, d), BF16), V((8, d), F32), V((length, 128), BF16), V((16, length), BF16),
            dma((3,)), dma((4,)), dma((2,)), dma((2,)), dma((4,)), dma((4,)), dma((CHUNKS,)), dma((4, CHUNKS)), dma((CHUNKS,)),
            dma((4, CHUNKS)), dma((4, CHUNKS)), dma((4,)), dma((4,)), dma((8,)),
            dma((3, 4, 2)), dma((3, 4)), dma((3, 4, 2)), dma((3, 4, 4)), dma((3, 4, 8)),
        ],
        compiler_params=pltpu.CompilerParams(vmem_limit_bytes=LIMIT, collective_id=0, has_side_effects=True),
        name="forward",
    )(skip, frames, cot, w_query, w_key, w_value, b_query, b_value, b_up, b_out, gain_one, shift_one, b_down, gain_two, shift_two,
      segments, padding, w_up, w_down, w_out)


def attend_back(h, keys, queries, q_aug, k_aug, v_aug, k_t, do_aug, dk_acc, dv_acc):
    weights = jnp.exp(mm(k_aug[h, keys, :], q_aug[h, :, queries]))
    dv_acc[h, :, keys] += mm(do_aug[h, 0:HEAD_DIM, queries], weights.astype(BF16), 1, 1)
    grad = (weights * mm(v_aug[h, keys, :], do_aug[h, :, queries])).astype(BF16)
    dk_acc[h, :, keys] += mm(q_aug[h, 0:HEAD_DIM, queries], grad, 1, 1)
    return mm(k_t[h, :, keys], grad)


def total(first, *others):
    out = first.astype(F32)
    for other in others:
        out = out + other.astype(F32)
    return out


def backward_kernel(
    skip_ref, gmixed, mixed_own_h, normed_h, act_h, ginner_h, gbranch_h, gatt_h, small, gone_h, cot_h,
    x_all, w_t_h, mixed_heads_h, q_aug_h, k_aug_h, v_aug_h, k_t_h,
    frames_grad, dw_out, up_out, down_out, out_out, small_out,
    mixed_own, normed, act, ginner, gbranch, gatt, gone, cot, w_t, mixed_heads, q_aug, k_aug, v_aug, k_t, load_sems,
    do_in, do_aug, dk_acc, dv_acc, dq_acc, dq_keep, grads, x_sem,
    big, away, core_in, near_in, across_in, mid, z_in, bigo, core_ino, near_ino, across_ino, mido, z_ino,
    sib_in, line_in, dw_own, dw_in, dw_mid, dw_z, small_mine, small_plane, small_mid, small_z,
    gm_s, gm_r, ci_s, ci_r, nr_s, nr_r, ac_s, ac_r, z_s, z_r, ag_s, ag_r,
    part_s, part_r, line_s, line_r, dwp_s, dwp_r, dwz_s, dwz_r, dwo_s, dwo_r, dwf_s, sp_s, sp_r, sz_s, sz_r,
):
    at = Place()
    heads = q_aug.shape[0]
    width = heads * HEAD_DIM
    share = gatt.shape[0]
    length = q_aug.shape[2]
    step_rows = share // CHUNKS
    z, c, q = at.z, at.b, at.q
    primary = at.primary
    secondary = jnp.logical_not(primary)
    loads = []
    for src, dst in ((gbranch_h, gbranch), (act_h, act), (normed_h, normed), (ginner_h, ginner), (mixed_own_h, mixed_own), (gatt_h, gatt),
                     (mixed_heads_h, mixed_heads), (q_aug_h, q_aug), (k_aug_h, k_aug), (v_aug_h, v_aug), (k_t_h, k_t), (w_t_h, w_t),
                     (gone_h, gone), (cot_h, cot)):
        pltpu.make_async_copy(src, dst, load_sems.at[len(loads)]).start()
        loads.append((src, dst))

    def loaded(*numbers):
        for n in numbers:
            pltpu.make_async_copy(*loads[n], load_sems.at[n]).wait()

    at.barrier()

    for g in range(4):
        block = gmixed.at[pl.ds(g * width, width)]
        near = at.b == g // 2
        to_d = jnp.where(near, at.d, at.sib)
        to_z = jnp.where(near, g, (g + 2) % 4)
        mine = jnp.logical_and(near, z == g)

        @pl.when(mine)
        def _():
            pltpu.make_async_copy(block, do_in.at[z], gm_s.at[g]).start()

        @pl.when(jnp.logical_not(mine))
        def _():
            at.send(block, do_in.at[z], gm_s.at[g], gm_r.at[z], to_d, to_z)

    n_big = 8
    half = big.shape[1]
    quarter = half // 4
    halfo = bigo.shape[3]
    quartero = bigo.shape[2] // 4
    finals = (down_out, up_out, out_out)

    def big_rows(chip):
        return pl.ds(pl.multiple_of(chip * quarter, 16), quarter)

    def out_rows(chip):
        return pl.ds(pl.multiple_of(chip * quartero, 16), quartero)

    def weight_job(j):
        if j == 0:
            loaded(0, 1)
        if j == n_big // 2:
            loaded(2, 3)
        if j == n_big:
            loaded(4, 5)
        if j < n_big:
            kind, s = j // 4, j % 4
            made = mm(act[s], gbranch[...], 0, 0) if kind == 0 else mm(normed[...], ginner[s], 0, 0)
            made = made.astype(BF16)
            if j >= 4:
                at.sent(away.at[j % 4], ci_s.at[j - 4])

            @pl.when(c == 0)
            def _():
                big[j] = made[:half]
                away[j % 4] = made[half:]

            @pl.when(c == 1)
            def _():
                big[j] = made[half:]
                away[j % 4] = made[:half]

            at.send(away.at[j % 4], core_in.at[j], ci_s.at[j], ci_r.at[j], at.sib, z)
        else:
            for s in range(4):
                made = mm(mixed_own[s * width : (s + 1) * width, :], gatt[...])
                for i in range(2):
                    bigo[i, s] = made[:, i * halfo : (i + 1) * halfo].astype(BF16)
            at.send(bigo.at[1 - c], core_ino, ci_s.at[j], ci_r.at[j], at.sib, z)

    def core_job(j):
        at.got(core_in.at[j] if j < n_big else core_ino, ci_r.at[j])
        if j < n_big:
            big[j] = total(big[j], core_in[j]).astype(BF16)
        else:
            bigo[c] = total(bigo[c], core_ino[...]).astype(BF16)
        for i, chip in enumerate((at.near_chip, at.opposite_chip)):
            if j < n_big:
                at.send(big.at[j, big_rows(chip)], near_in.at[i, j], nr_s.at[j, i], nr_r.at[j, i], at.near, z)
            else:
                at.send(bigo.at[c, :, out_rows(chip)], near_ino.at[i], nr_s.at[j, i], nr_r.at[j, i], at.near, z)

    def near_job(j):
        if j < n_big:
            for i in range(2):
                at.got(near_in.at[i, j], nr_r.at[j, i])
            near_in[1, j] = total(big[j, big_rows(at.across_chip)], near_in[1, j]).astype(BF16)
            at.send(near_in.at[1, j], across_in.at[j], ac_s.at[j], ac_r.at[j], at.across, z)
        else:
            for i in range(2):
                at.got(near_ino.at[i], nr_r.at[j, i])
            near_ino[1] = total(bigo[c, :, out_rows(at.across_chip)], near_ino[1]).astype(BF16)
            at.send(near_ino.at[1], across_ino, ac_s.at[j], ac_r.at[j], at.across, z)

    def plane_job(j):
        if j < n_big:
            kind, s = j // 4, j % 4
            at.got(across_in.at[j], ac_r.at[j])
            mid[j] = total(big[j, big_rows(q)], near_in[0, j], across_in[j]).astype(BF16)

            @pl.when(z != s)
            def _():
                slot = 3 - (s - z + 4) % 4
                at.send(mid.at[j], z_in.at[slot, kind], z_s.at[j], z_r.at[kind, slot], at.d, s)
        else:
            at.got(across_ino, ac_r.at[j])
            mido[...] = total(bigo[c, :, out_rows(q)], near_ino[0], across_ino[...]).astype(BF16)
            for s in range(4):
                @pl.when(z != s)
                def _():
                    slot = 3 - (s - z + 4) % 4
                    at.send(mido.at[s], z_ino.at[slot], z_s.at[j + s], z_r.at[2, slot], at.d, s)

    def final_piece(kind, chip, core):
        if kind < 2:
            return finals[kind].at[pl.ds(pl.multiple_of(core * half + chip * quarter, 16), quarter)]
        return out_out.at[out_rows(chip), pl.ds(pl.multiple_of(core * halfo, 128), halfo)]

    def final_job(kind):
        for k in range(3):
            at.got(z_in.at[k, kind] if kind < 2 else z_ino.at[k], z_r.at[kind, k])
        piece = final_piece(kind, q, c)
        if kind < 2:
            piece[...] = total(mid[4 * kind + z], z_in[0, kind], z_in[1, kind], z_in[2, kind]).astype(BF16)
        else:
            piece[...] = total(mido[z], z_ino[0], z_ino[1], z_ino[2]).astype(BF16)
        sem = ag_r.at[kind, 2 * q + c]
        at.send(piece, piece, ag_s.at[kind, 0], sem, at.near, z)
        at.send(piece, piece, ag_s.at[kind, 1], sem, at.across, z)
        at.send(piece, piece, ag_s.at[kind, 2], sem, at.sib, z)

    def pass_job(kind):
        piece = final_piece(kind, at.near_chip, c)
        sem = ag_r.at[kind, 2 * at.near_chip + c]
        at.got(piece, sem)
        at.send(piece, piece, ag_s.at[kind, 3], sem, at.across, z)
        at.send(piece, piece, ag_s.at[kind, 4], sem, at.sib, z)

    def share_job(kind):
        for i, chip in enumerate((at.across_chip, at.opposite_chip)):
            piece = final_piece(kind, chip, c)
            sem = ag_r.at[kind, 2 * chip + c]
            at.got(piece, sem)
            at.send(piece, piece, ag_s.at[kind, 5 + i], sem, at.sib, z)

    def end_job(kind):
        for k in range(4):
            chip = (q + k) % 4
            at.got(final_piece(kind, chip, 1 - c), ag_r.at[kind, 2 * chip + 1 - c])

    for j in range(n_big + 1):
        weight_job(j)
        if j >= 2:
            core_job(j - 2)
    core_job(n_big - 1)
    core_job(n_big)
    x_here, part = core_in.at[0:4], core_in.at[4:8]
    pltpu.make_async_copy(x_all, x_here, x_sem.at[0]).start()

    late = at.rb
    side = length // 2

    def prepare(i):
        mine = jnp.logical_and(primary, z == i)

        @pl.when(mine)
        def _():
            pltpu.make_async_copy(gmixed.at[pl.ds(pl.multiple_of(i * width, 64), width)], do_in.at[i], gm_s.at[i]).wait()

        @pl.when(jnp.logical_not(mine))
        def _():
            at.got(do_in.at[i], gm_r.at[i])

        cols = pl.ds(pl.multiple_of(i * share, share), share)
        for h in range(heads):
            hs = slice(h * HEAD_DIM, (h + 1) * HEAD_DIM)
            do = do_in[i, hs, :]
            do_aug[h, 0:HEAD_DIM, cols] = do
            inner = jnp.sum(do.astype(F32) * mixed_heads[i, hs, :].astype(F32), 0, keepdims=True)
            do_aug[h, HEAD_DIM : HEAD_DIM + 16, cols] = pad_rows(split3(-inner), 16, share)
            do_aug[h, HEAD_DIM + 16 :, cols] = jnp.zeros((48, share), BF16)

    def half_row(n):
        return pl.ds(pl.multiple_of(n * side, side), side)

    dk_acc[...] = jnp.zeros_like(dk_acc)
    dv_acc[...] = jnp.zeros_like(dv_acc)

    N, M, Q, U, V = near_job, plane_job, final_job, pass_job, share_job
    jobs = {-1: ((N, 0), (N, 1),), 0: ((N, 2), (M, 0),), 1: ((M, 1),), 2: ((N, 3), (M, 2),), 4: ((N, 4), (M, 3),), 6: ((N, 5), (M, 4),), 8: ((N, 6), (M, 5),), 50: ((Q, 0),), 10: ((N, 7), (M, 6),)}

    def attention_step(t, _):
        last = t >= 3 * heads
        h = jnp.where(last, t - 3 * heads, t // 3)
        turn = jnp.where(last, 3, t % 3)
        keys = half_row(jnp.where(jnp.logical_or(turn == 0, last), late, 1 - late))
        queries = half_row(jnp.where(turn < 2, 1 - late, late))
        dq = attend_back(h, keys, queries, q_aug, k_aug, v_aug, k_t, do_aug, dk_acc, dv_acc)
        hs = pl.ds(pl.multiple_of(h * HEAD_DIM, HEAD_DIM), HEAD_DIM)

        @pl.when(turn == 0)
        def _():
            dq_acc[...] = dq

        @pl.when(turn == 1)
        def _():
            grads[hs, queries] = ((dq_acc[...] + dq).astype(BF16).astype(F32) * HEAD_DIM**-0.5).astype(BF16)

        @pl.when(turn == 2)
        def _():
            dq_keep[h] = dq

        @pl.when(turn == 3)
        def _():
            grads[hs, queries] = ((dq_keep[h] + dq).astype(BF16).astype(F32) * HEAD_DIM**-0.5).astype(BF16)

        for when, todo in jobs.items():
            if 0 <= when < 4 * heads:
                @pl.when(t == when)
                def _():
                    for job, j in todo:
                        job(j)

        return 0

    def rows(ch):
        return pl.ds(ch * step_rows, step_rows)

    def part_job(s):
        part[s] = mm(grads[:, pl.ds(pl.multiple_of(s * share, share), share)], w_t[...], 0, 0).astype(BF16)

        @pl.when(secondary)
        def _():
            for ch in range(CHUNKS):
                at.send(part.at[s, rows(ch)], sib_in.at[s, rows(ch)], part_s.at[s, ch], part_r.at[s, ch], at.sib, z)

    def line_job(place):
        s = at.line(place)
        for ch in range(CHUNKS):
            here = (s, rows(ch))

            @pl.when(jnp.logical_and(primary, place != at.p))
            def _():
                at.got(sib_in.at[here], part_r.at[s, ch])

                @pl.when(jnp.logical_and(at.p == 1, place >= 2))
                def _():
                    at.got(line_in.at[here], line_r.at[s, ch])
                    part[here] = total(part[here], sib_in[here], line_in[here]).astype(BF16)
                    at.send(part.at[here], line_in.at[here], line_s.at[s, ch], line_r.at[s, ch], at.d, at.own_line(2))

                @pl.when(jnp.logical_or(at.p == 0, place == 0))
                def _():
                    part[here] = total(part[here], sib_in[here]).astype(BF16)
                    at.send(part.at[here], line_in.at[here], line_s.at[s, ch], line_r.at[s, ch], at.d, at.own_line(1 - at.p))

    def finish(n):
        cols = half_row(n)
        for h in range(heads):
            grads[width + h * HEAD_DIM : width + (h + 1) * HEAD_DIM, cols] = dk_acc[h, :, cols].astype(BF16)
            grads[2 * width + h * HEAD_DIM : 2 * width + (h + 1) * HEAD_DIM, cols] = dv_acc[h, :, cols].astype(BF16)

    loaded(6, 7, 8, 9, 10, 11)
    for i in range(4):
        prepare(i)
    for job, j in jobs.get(-1, ()):
        job(j)
    lax.fori_loop(0, 3 * heads, attention_step, 0)
    finish(1 - late)
    for place in (3, 2):
        part_job(at.line(place))

    @pl.when(at.p == 0)
    def _():
        line_job(3)
        line_job(2)

    for job, j in jobs.get(50, ()):
        job(j)
    lax.fori_loop(3 * heads, 4 * heads, attention_step, 0)
    finish(late)
    for place in (0, 1):
        part_job(at.line(place))

    @pl.when(at.p == 0)
    def _():
        line_job(1)

    @pl.when(at.p == 1)
    def _():
        line_job(0)

    small_mine[...] = small[...]
    small_mine[pl.ds(10 + at.group, 1), 0 : 3 * width] = mm(jnp.ones((8, length), BF16), grads[...], 1, 1)[0:1]
    at.send(small_mine, small_plane.at[0], sp_s.at[0], sp_r.at[0], at.sib, z)
    for k in (1, 2, 3):
        at.send(small_mine, small_plane.at[4 - k], sp_s.at[k], sp_r.at[4 - k], at.chip(k), z)
        at.send(small_mine, small_plane.at[7 - k], sp_s.at[3 + k], sp_r.at[7 - k], at.other(k), z)

    pltpu.make_async_copy(x_all, x_here, x_sem.at[0]).wait()
    made = mm(grads[:, 0:share], x_here[0])
    for s in range(1, 4):
        made = made + mm(grads[:, s * share : (s + 1) * share], x_here[s])
    made = made.astype(BF16)
    fourth = made.shape[0] // 4
    for i in range(4):
        dw_own[i] = made[i * fourth : (i + 1) * fourth]
    at.send(dw_own.at[at.near_chip], dw_in.at[0], dwp_s.at[0], dwp_r.at[0], at.near, z)
    at.send(dw_own.at[at.opposite_chip], dw_in.at[1], dwp_s.at[1], dwp_r.at[1], at.near, z)

    def dw_rows(i):
        return pl.ds(pl.multiple_of(i * fourth, 16), fourth)

    def small_sum(_):
        for k in range(7):
            at.got(small_plane.at[k], sp_r.at[k])
        small_mid[...] = total(small_mine[...], *(small_plane[k] for k in range(7)))
        for k in (1, 2, 3):
            at.send(small_mid, small_z.at[3 - k], sz_s.at[k - 1], sz_r.at[3 - k], at.d, (z + k) % 4)

    def small_end(_):
        for k in range(3):
            at.got(small_z.at[k], sz_r.at[k])
        small_out[...] = total(small_mid[...], small_z[0], small_z[1], small_z[2])

    def onward(place):
        @pl.when(at.p == 1)
        def _():
            line_job(place)

        if place == 3:
            @pl.when(at.p == 2)
            def _():
                s = at.own_line(3)
                for ch in range(CHUNKS):
                    here = (s, rows(ch))
                    at.got(line_in.at[here], line_r.at[s, ch])
                    at.send(line_in.at[here], line_in.at[here], line_s.at[s, ch], line_r.at[s, ch], at.d, s)

    def dw_across(_):
        for k in range(2):
            at.got(dw_in.at[k], dwp_r.at[k])
        dw_in[1] = total(dw_own[at.across_chip], dw_in[1]).astype(BF16)
        at.send(dw_in.at[1], dw_in.at[2], dwp_s.at[2], dwp_r.at[2], at.across, z)

    def dw_plane(_):
        at.got(dw_in.at[2], dwp_r.at[2])
        dw_mid[...] = total(dw_own[q], dw_in[0], dw_in[2]).astype(BF16)

        @pl.when(secondary)
        def _():
            at.send(dw_mid, dw_z, dwz_s.at[0], dwz_r.at[0], at.d, at.far)

    def dw_final(_):
        @pl.when(primary)
        def _():
            at.got(dw_z, dwz_r.at[0])
            piece = dw_out.at[dw_rows(q)]
            piece[...] = total(dw_mid[...], dw_z[...]).astype(BF16)
            at.send(piece, piece, dwo_s.at[0], dwo_r.at[q], at.near, z)
            at.send(piece, piece, dwo_s.at[1], dwo_r.at[q], at.across, z)
            at.send(piece, piece, dwo_s.at[2], dwo_r.at[q], at.sib, z)

    def dw_pass(_):
        @pl.when(primary)
        def _():
            i = at.near_chip
            piece = dw_out.at[dw_rows(i)]
            at.got(piece, dwo_r.at[i])
            at.send(piece, piece, dwo_s.at[3], dwo_r.at[i], at.across, z)
            at.send(piece, piece, dwf_s.at[0], dwo_r.at[i], at.sib, z)

    for job, j in ((onward, 3), (M, 7), (small_sum, 0), (dw_across, 0), (N, 8), (dw_plane, 0), (M, 8), (onward, 2), (dw_final, 0), (U, 0), (Q, 1), (dw_pass, 0), (U, 1), (Q, 2), (V, 0), (small_end, 0), (U, 2), (V, 1), (V, 2)):
        job(j)

    skipped = skip_ref[0] == 1
    loaded(12, 13)
    for ch in range(CHUNKS):
        at.got(line_in.at[z, rows(ch)], line_r.at[z, ch])

    @pl.when(primary)
    def _():
        for ch in range(CHUNKS):
            at.got(sib_in.at[z, rows(ch)], part_r.at[z, ch])
        grad = gone[...] + total(part[z], sib_in[z], line_in[z])
        frames_grad[...] = jnp.where(skipped, cot[...].astype(F32), grad).astype(BF16)

    @pl.when(secondary)
    def _():
        grad = gone[...] + line_in[z].astype(F32)
        frames_grad[...] = jnp.where(skipped, cot[...].astype(F32), grad).astype(BF16)


    @pl.when(primary)
    def _():
        for k, i in ((1, at.across_chip), (2, at.opposite_chip)):
            piece = dw_out.at[dw_rows(i)]
            at.got(piece, dwo_r.at[i])
            at.send(piece, piece, dwf_s.at[k], dwo_r.at[i], at.sib, z)

    @pl.when(secondary)
    def _():
        for i in range(4):
            at.got(dw_out.at[dw_rows(i)], dwo_r.at[i])

    for kind in range(3):
        end_job(kind)

    for g in range(4):
        mine = jnp.logical_and(primary, z == g)

        @pl.when(jnp.logical_not(mine))
        def _():
            at.sent(gmixed.at[pl.ds(g * width, width)], gm_s.at[g])

    for j in range(n_big):
        if j >= 4:
            at.sent(core_in.at[j], ci_s.at[j])
        for k in range(2):
            at.sent(near_in.at[k, j], nr_s.at[j, k])
        at.sent(across_in.at[j], ac_s.at[j])

        @pl.when(z != j % 4)
        def _():
            at.sent(mid.at[j], z_s.at[j])

    at.sent(core_ino, ci_s.at[n_big])
    for k in range(2):
        at.sent(near_ino.at[k], nr_s.at[n_big, k])
    at.sent(across_ino, ac_s.at[n_big])
    for s in range(4):
        @pl.when(z != s)
        def _():
            at.sent(mido.at[s], z_s.at[n_big + s])

    for kind in range(3):
        for k in range(7):
            at.sent(final_piece(kind, q, c), ag_s.at[kind, k])
    for k in range(7):
        at.sent(small_mine, sp_s.at[k])
    for k in range(3):
        at.sent(small_mid, sz_s.at[k])
        at.sent(dw_mid, dwp_s.at[k])

    @pl.when(secondary)
    def _():
        at.sent(dw_mid, dwz_s.at[0])
        for s in range(4):
            for ch in range(CHUNKS):
                at.sent(part.at[s, rows(ch)], part_s.at[s, ch])

    @pl.when(primary)
    def _():
        for k in range(4):
            at.sent(dw_mid, dwo_s.at[k])
        for k in range(3):
            at.sent(dw_mid, dwf_s.at[k])
        for k in (1, 2, 3):
            for ch in range(CHUNKS):
                s = at.line((at.p + k) % 4)
                at.sent(part.at[s, rows(ch)], line_s.at[s, ch])

    @pl.when(at.p == 2)
    def _():
        for ch in range(CHUNKS):
            at.sent(line_in.at[at.own_line(3), rows(ch)], line_s.at[at.own_line(3), ch])


def run_backward(skip, gmixed, mixed_own, normed, act, ginner, gbranch, gatt, small, gone, cot,
                 x_all, w_t, mixed_heads, q_aug, k_aug, v_aug, k_t):
    share, d = gatt.shape
    any_ = pl.BlockSpec(memory_space=pl.ANY)
    f = act.shape[2]
    heads, _, length = q_aug.shape
    width = heads * HEAD_DIM
    dma, V = pltpu.SemaphoreType.DMA, pltpu.VMEM
    hd, hf, ho = d // 2, f // 2, d // 2
    return pl.pallas_call(
        backward_kernel,
        out_shape=(
            S((share, d)), S((3 * width, d)), S((d, f)), S((f, d)), S((width, d)), S((16, d), F32),
        ),
        in_specs=[SMEM] + [any_] * 7 + [VMEM] + [any_] * 9, out_specs=[VMEM] * 6,
        scratch_shapes=[
            V((4 * width, share), BF16), V((share, d), BF16), V((4, share, f), BF16), V((4, share, f), BF16), V((share, d), BF16),
            V((share, d), BF16), V((share, d), F32), V((share, d), BF16), V((3 * width, d), BF16), V((4, width, share), BF16),
            V((heads, 128, length), BF16), V((heads, length, 128), BF16), V((heads, length, 128), BF16),
            V((heads, HEAD_DIM, length), BF16), dma((14,)),
            V((4, width, share), BF16), V((heads, 128, length), BF16),
            V((heads, HEAD_DIM, length), F32), V((heads, HEAD_DIM, length), F32),
            V((HEAD_DIM, length // 2), F32), V((heads, HEAD_DIM, length // 2), F32), V((3 * width, length), BF16), dma((1,)),
            V((8, hd, d), BF16), V((4, hd, d), BF16), V((8, hd, d), BF16), V((2, 8, hd // 4, d), BF16), V((8, hd // 4, d), BF16), V((8, hd // 4, d), BF16),
            V((3, 2, hd // 4, d), BF16),
            V((2, 4, width, ho), BF16), V((4, width, ho), BF16), V((2, 4, width // 4, ho), BF16), V((4, width // 4, ho), BF16), V((4, width // 4, ho), BF16),
            V((3, width // 4, ho), BF16),
            V((4, share, d), BF16), V((4, share, d), BF16),
            V((4, 3 * width // 4, d), BF16), V((3, 3 * width // 4, d), BF16), V((3 * width // 4, d), BF16), V((3 * width // 4, d), BF16),
            V((16, d), F32), V((7, 16, d), F32), V((16, d), F32), V((3, 16, d), F32),
            dma((4,)), dma((4,)), dma((9,)), dma((9,)), dma((9, 2)), dma((9, 2)), dma((9,)), dma((9,)), dma((12,)), dma((3, 3)),
            dma((3, 7)), dma((3, 8)),
            dma((4, CHUNKS)), dma((4, CHUNKS)), dma((4, CHUNKS)), dma((4, CHUNKS)), dma((3,)), dma((3,)), dma((1,)), dma((1,)),
            dma((4,)), dma((4,)), dma((3,)), dma((7,)), dma((7,)), dma((3,)), dma((3,)),
        ],
        compiler_params=pltpu.CompilerParams(vmem_limit_bytes=LIMIT, collective_id=1, has_side_effects=True),
        name="attention_backward",
    )(skip, gmixed, mixed_own, normed, act, ginner, gbranch, gatt, small, gone, cot,
      x_all, w_t, mixed_heads, q_aug, k_aug, v_aug, k_t)


def last_kernel(dw, up, down, out, small, *outs):
    z = lax.axis_index("mp")
    d_query, d_key, d_value, d_up, d_down, d_out, b_query, b_value, b_up = outs[:9]
    width = d_out.shape[0]
    for i, target in enumerate((d_query, d_key, d_value)):
        target[...] = dw[i * width : (i + 1) * width].astype(F32)
    d_up[...] = up[...].astype(F32)
    d_down[...] = down[...].astype(F32)
    d_out[...] = out[...].astype(F32)
    bias = small[pl.ds(10 + z, 1), :]
    b_query[...] = bias[:, 0:width].reshape(width)
    b_value[...] = bias[:, 2 * width : 3 * width].reshape(width)
    b_up[...] = small[pl.ds(6 + z, 1), :].reshape(small.shape[1])
    for i, target in enumerate(outs[9:]):
        target[...] = small[i : i + 1, :].reshape(small.shape[1])


def S(shape, dtype=BF16):
    return jax.ShapeDtypeStruct(shape, dtype)


def shards(
    frames, cotangent, segments, padding, skip_flag, w_query, b_query, w_key, w_value, b_value,
    w_out, b_out, gain_one, shift_one, w_up, b_up, w_down, b_down, gain_two, shift_two,
):
    mp = lax.axis_size("mp")
    share, d = frames.shape[1:]
    length = segments.shape[1]
    width = w_query.shape[1]
    heads = width // HEAD_DIM
    params = pltpu.CompilerParams(vmem_limit_bytes=LIMIT)
    own = frames[0]
    f = w_up.shape[1]
    (
        x_all, w_t, mixed, mixed_own, q_aug, k_aug, v_aug, k_t,
        layer, gone, gmixed, normed, act, ginner, gbranch, gatt, small,
    ) = run_forward(
        skip_flag, own, cotangent[0], w_query.T, w_key.T, w_value.T, b_query, b_value, b_up,
        b_out, gain_one, shift_one, b_down, gain_two, shift_two, segments, padding, w_up, w_down, w_out,
    )
    frames_grad, wgrad, gup, gdown, gout, small = run_backward(
        skip_flag, gmixed, mixed_own, normed, act, ginner, gbranch, gatt, small, gone, cotangent[0],
        x_all, w_t, mixed, q_aug, k_aug, v_aug, k_t,
    )
    dp = lax.axis_size("dp")
    if dp > 8:
        groups = [list(range(i, dp, 8)) for i in range(8)]
        wgrad, gup, gdown, gout, small = (
            lax.psum(v.astype(F32), "dp", axis_index_groups=groups) for v in (wgrad, gup, gdown, gout, small)
        )
    d_query, d_key, d_value, d_up, d_down, d_out, b_q, b_v, b_u, *rest = pl.pallas_call(
        last_kernel,
        out_shape=tuple(
            S(s, F32) for s in [(width, d)] * 3 + [(d, f), (f, d), (width, d), (width,), (width,), (f,)] + [(d,)] * 6
        ),
        in_specs=[VMEM] * 5, out_specs=[VMEM] * 15, compiler_params=params, name="outputs",
    )(wgrad, gup, gdown, gout, small)
    b_down_grad, gain_two_grad, shift_two_grad, b_out_grad, gain_one_grad, shift_one_grad = rest
    return (
        layer[None], frames_grad[None], d_query.T, b_q, d_key.T, d_value.T, b_v,
        d_out, b_out_grad, gain_one_grad, shift_one_grad,
        d_up, b_u, d_down, b_down_grad, gain_two_grad, shift_two_grad,
    )


def solution(mesh):
    split = (P("dp", "mp", None), P(None, "mp"), P("mp"), P("mp", None), P())
    row, col, one, top, rep = split
    return jax.shard_map(
        shards,
        mesh=mesh,
        in_specs=(row, row, P("dp", None), P("dp", None), P("dp"), col, one, col, col, one, top, rep, rep, rep, col, one, top, rep, rep, rep),
        out_specs=(row, row, col, one, col, col, one, top, rep, rep, rep, col, one, top, rep, rep, rep),
        check_vma=False,
    )
```

```python
import functools

import jax
import jax.numpy as jnp
from jax import lax
from jax.experimental import pallas as pl
from jax.experimental.pallas import tpu as pltpu
from jax.sharding import PartitionSpec as P

HEAD_DIM = 64
F32, BF16 = jnp.float32, jnp.bfloat16
VMEM = pl.BlockSpec(memory_space=pltpu.VMEM)
SMEM = pl.BlockSpec(memory_space=pltpu.SMEM)
LIMIT = 60 << 20


def mm(a, b, ca=1, cb=0):
    return lax.dot_general(a, b, (((ca,), (cb,)), ((), ())), preferred_element_type=F32)


def row_of(ref):
    return ref[...].reshape(1, ref.shape[0])


def split3(v):
    hi = v.astype(BF16)
    rest = v - hi.astype(F32)
    mid = rest.astype(BF16)
    low = (rest - mid.astype(F32)).astype(BF16)
    return hi, mid, low


def pad_rows(parts, rows, width):
    parts = [p.astype(F32) for p in parts]
    have = sum(p.shape[0] for p in parts)
    return jnp.concatenate(parts + [jnp.zeros((rows - have, width), F32)], 0).astype(BF16)


def project(x, w_t, w_pad, bias_col, v_row, k_mask, one_hot, rows, q_aug, k_aug, v_aug, k_t, v_t):
    width = w_t.shape[0] // 3
    heads = width // HEAD_DIM
    every = mm(w_t, x, 1, 1) + bias_col
    every = jnp.concatenate([every[:width] * HEAD_DIM**-0.5, every[width:]], 0).astype(BF16)
    for h in range(heads):
        q_aug[h, 0:HEAD_DIM, rows] = every[h * HEAD_DIM : (h + 1) * HEAD_DIM]
        q_aug[h, HEAD_DIM : HEAD_DIM + 16, rows] = one_hot
        q_aug[h, HEAD_DIM + 16 :, rows] = jnp.zeros((48, x.shape[0]), BF16)
        k_t[h, :, rows] = every[width + h * HEAD_DIM : width + (h + 1) * HEAD_DIM]
        v_t[h, :, rows] = every[2 * width + h * HEAD_DIM : 2 * width + (h + 1) * HEAD_DIM]
    both = mm(x, w_pad, 1, 1)
    for h in range(heads):
        k_aug[h, rows, :] = both[:, h * 128 : (h + 1) * 128].astype(BF16) + k_mask
        at = (heads + h) * 128
        v_aug[h, rows, :] = (both[:, at : at + 128] + v_row[:, h * 128 : (h + 1) * 128]).astype(BF16)


def attend(h, cols, q_aug, k_aug, v_t):
    scores = mm(k_aug[h], q_aug[h, :, cols])
    peak = jnp.max(scores, 0, keepdims=True)
    raised = jnp.exp(scores - peak)
    summed = jnp.sum(raised, 0, keepdims=True)
    mixed = mm(v_t[h], raised.astype(BF16)) / summed
    one_hot = q_aug[h, HEAD_DIM : HEAD_DIM + 16, cols].astype(F32)[0:4]
    q_aug[h, HEAD_DIM : HEAD_DIM + 16, cols] = pad_rows((one_hot,) + split3(-(peak + jnp.log(summed))), 16, mixed.shape[1])
    return mixed.astype(BF16)


def norm_stats(v):
    centered = v - jnp.mean(v, -1, keepdims=True)
    r = lax.rsqrt(jnp.mean(centered * centered, -1, keepdims=True) + 1e-05)
    return centered * r, r


def norm_back(c, gain, hat, r):
    e = c * gain
    return r * (e - jnp.mean(e, -1, keepdims=True) - hat * jnp.mean(e * hat, -1, keepdims=True))


def feed_forward(
    skip_ref, mixed_ref, frames_ref, cot_ref, b_out, gain_one, shift_one, b_down, gain_two, shift_two, small_all,
    wout_ref, wup_ref, wdown_ref, arrive, leave, outside,
    layer_ref, gone_ref, gmixed_ref, normed_ref, act_ref, ginner_ref, gbranch_ref, gatt_ref, small_ref, slope_ref,
):
    skipped = skip_ref[0] == 1
    mixed_h, layer_h, gone_h, gmixed_h, normed_h, act_h, ginner_h, gbranch_h, gatt_h = outside
    b_out, gain_one, shift_one, b_down, gain_two, shift_two = (row_of(v) for v in (b_out, gain_one, shift_one, b_down, gain_two, shift_two))
    frames = frames_ref[...].astype(F32)
    arrive(2)
    all_out = wout_ref[...].reshape(mixed_ref.shape[0], frames.shape[1])
    attended = mm(mixed_ref[...], all_out, 0, 0) + b_out
    hat_one, r_one = norm_stats(frames + attended)
    normed = hat_one * gain_one + shift_one
    normed_ref[...] = normed.astype(BF16)
    leave(7, mixed_ref, mixed_h)
    leave(8, normed_ref, normed_h)
    parts = wup_ref.shape[0]
    arrive(0)
    for s in range(parts):
        inner = mm(normed_ref[...], wup_ref[s]) + small_all[s, 0:1, :]
        cdf = 0.5 * (1.0 + lax.erf(inner * (0.5**0.5)))
        slope_ref[s] = cdf + inner * (jnp.exp(-0.5 * inner * inner) * 0.3989422804014327)
        act_ref[s] = (inner * cdf).astype(BF16)
        leave(9, act_ref, act_h, s)
    arrive(1)
    branch = mm(act_ref[0], wdown_ref[0])
    for s in range(1, parts):
        branch = branch + mm(act_ref[s], wdown_ref[s])
    hat_two, r_two = norm_stats(normed + (branch + b_down))
    result = hat_two * gain_two + shift_two
    cot = cot_ref[...].astype(F32)
    layer_ref[...] = jnp.where(skipped, frames, result).astype(BF16)
    grad_out = jnp.where(skipped, 0.0, cot)
    grad_two = norm_back(grad_out, gain_two, hat_two, r_two)
    gbranch = grad_two.astype(BF16)
    gbranch_ref[...] = gbranch
    leave(13, layer_ref, layer_h)
    leave(14, gbranch_ref, gbranch_h)
    small_ref[10:16, :] = jnp.zeros_like(small_ref[10:16, :])
    small_ref[0:1, :] = jnp.sum(gbranch.astype(F32), 0, keepdims=True)
    small_ref[1:2, :] = jnp.sum(grad_out * hat_two, 0, keepdims=True)
    small_ref[2:3, :] = jnp.sum(grad_out, 0, keepdims=True)
    grad_normed = grad_two
    for s in range(parts):
        gact = mm(gbranch_ref[...], wdown_ref[s], 1, 1)
        ginner = (gact * slope_ref[s]).astype(BF16)
        ginner_ref[s] = ginner
        leave(15, ginner_ref, ginner_h, s)
        small_ref[6 + s : 7 + s, :] = jnp.sum(ginner.astype(F32), 0, keepdims=True)
        grad_normed = grad_normed + mm(ginner, wup_ref[s], 1, 1)
    grad_one = norm_back(grad_normed, gain_one, hat_one, r_one)
    gone_ref[...] = grad_one
    gatt = grad_one.astype(BF16)
    gatt_ref[...] = gatt
    leave(19, gone_ref, gone_h)
    leave(20, gatt_ref, gatt_h)
    small_ref[3:4, :] = jnp.sum(gatt.astype(F32), 0, keepdims=True)
    small_ref[4:5, :] = jnp.sum(grad_normed * hat_one, 0, keepdims=True)
    small_ref[5:6, :] = jnp.sum(grad_normed, 0, keepdims=True)
    gmixed_ref[...] = mm(all_out, gatt, 1, 1).astype(BF16)
    leave(21, gmixed_ref, gmixed_h)


MESH = pl.DeviceIdType.MESH
CHUNKS = 3


class Place:
    def __init__(self):
        self.d, self.z = lax.axis_index("dp"), lax.axis_index("mp")
        d, z = self.d, self.z
        self.b = d % 2
        self.p = z + self.b * (3 - 2 * z)
        self.sib = d + 1 - 2 * self.b
        self.q = (d // 2) % 4
        self.base = d - d % 8
        q = self.q
        turn, over = q + 1 - 2 * (q % 2), (q + 2) % 4
        self.near_chip = turn + self.b * (over - turn)
        self.across_chip = over + self.b * (turn - over)
        self.opposite_chip = 3 - q
        self.near = self.base + 2 * self.near_chip + self.b
        self.across = self.base + 2 * self.across_chip + self.b
        self.primary = self.p < 2
        self.rb = z // 2
        self.row = d - self.b + self.rb
        self.pp = z + self.rb * (3 - 2 * z)
        self.far = (z + 2) % 4
        self.group = jnp.where(self.primary, z, self.far)

    def own_line(self, place):
        return place + self.b * (3 - 2 * place)

    def line(self, place):
        return place + self.rb * (3 - 2 * place)

    def chip(self, k):
        return self.base + 2 * ((self.q + k) % 4) + self.b

    def other(self, k):
        return self.base + 2 * ((self.q + k) % 4) + 1 - self.b

    def barrier(self):
        sem = pltpu.get_barrier_semaphore()
        others = [((self.d), (self.z + k) % 4) for k in (1, 2, 3)]
        others += [(self.sib, (self.z + k) % 4) for k in range(4)]
        others += [(self.chip(k), self.z) for k in (1, 2, 3)]
        others += [(self.other(k), self.z) for k in (1, 2, 3)]
        for dp, mp in others:
            pl.semaphore_signal(sem, inc=1, device_id=(dp, mp), device_id_type=MESH)
        pl.semaphore_wait(sem, len(others))

    def send(self, src, dst, send_sem, recv_sem, dp, mp):
        pltpu.make_async_remote_copy(
            src_ref=src, dst_ref=dst, send_sem=send_sem, recv_sem=recv_sem, device_id=(dp, mp), device_id_type=MESH
        ).start()

    def sent(self, src, send_sem):
        pltpu.make_async_remote_copy(
            src_ref=src, dst_ref=src, send_sem=send_sem, recv_sem=send_sem, device_id=(self.sib, self.z), device_id_type=MESH
        ).wait_send()

    def got(self, dst, recv_sem):
        pltpu.make_async_remote_copy(
            src_ref=dst, dst_ref=dst, send_sem=recv_sem, recv_sem=recv_sem, device_id=(self.sib, self.z), device_id_type=MESH
        ).wait_recv()


def forward_kernel(
    skip, frames, cot, w_query, w_key, w_value, b_query, b_value, b_up, b_out, gain_one, shift_one, b_down, gain_two, shift_two,
    segments, padding, w_up, w_down, w_out,
    x_all_h, w_t_h, mixed_heads_h, mixed_own_h, q_aug_h, k_aug_h, v_aug_h, k_t_h,
    layer_h, gone_h, gmixed_h, normed_h, act_h, ginner_h, gbranch_h, gatt_h, small_sums,
    x_all, w_t, mixed_heads, mixed_own, q_aug, k_aug, v_aug, k_t,
    layer, gone, gmixed, normed, act, ginner, gbranch, gatt, out_sems,
    small_all, up_all, down_all, out_all, slope,
    relay, v_t, w_pad, kmask, hot, w_own, small_own, kmask_own, hot_own,
    small_s, small_r, mask_s, mask_r, wq_s, wq_r, x_s, x_r, relay_r, on_s, fwd_s, mix_s, mix_r, local,
    line_s, near_s, far_s, core_s, w_r,
):
    at = Place()
    heads = q_aug.shape[0]
    width = heads * HEAD_DIM
    share = frames.shape[0]
    step_rows = share // CHUNKS
    quarter = w_own.shape[0] // 4
    for i, w in enumerate((w_query, w_key, w_value)):
        w_own[i * width : (i + 1) * width] = w[...]
    small_own[...] = jnp.zeros_like(small_own)
    small_own[0:1, :] = row_of(b_up)
    small_own[1:2, 0:width] = row_of(b_query)
    values = row_of(b_value)
    small_own[1:2, 2 * width : 3 * width] = values
    for h in range(heads):
        small_own[2:3, h * 128 : h * 128 + HEAD_DIM] = values[:, h * HEAD_DIM : (h + 1) * HEAD_DIM]
        small_own[2:3, h * 128 + HEAD_DIM : h * 128 + HEAD_DIM + 3] = jnp.ones((1, 3), F32)
    at.barrier()
    primary = at.primary
    secondary = jnp.logical_not(primary)
    z = at.z

    def rows(ch):
        return pl.ds(ch * step_rows, step_rows)

    def piece(m, chip, core):
        if m == 2:
            n = w_out.shape[0] // 4
            half = w_out.shape[1] // 2
            return (pl.ds(pl.multiple_of(chip * n, 16), n), pl.ds(pl.multiple_of(core * half, 128), half))
        n = w_up.shape[0] // 8
        return (pl.ds(pl.multiple_of((2 * chip + core) * n, 16), n), slice(None))

    mats = ((w_up, up_all), (w_down, down_all), (w_out, out_all))

    for k in (1, 2, 3):
        at.send(small_own, small_all.at[z], small_s.at[k - 1], small_r.at[z], at.d, (z + k) % 4)
    wq_rows = pl.ds(pl.multiple_of(at.q * quarter, 16), quarter)
    first = jnp.where(at.p == 0, 1, at.p - 1)

    @pl.when(primary)
    def _():
        at.send(w_own.at[wq_rows], w_t.at[wq_rows], wq_s.at[0], wq_r.at[at.q], at.d, at.far)

    for ch in range(CHUNKS):
        @pl.when(at.p < 3)
        def _():
            at.send(frames.at[rows(ch)], x_all.at[z, rows(ch)], on_s.at[z, ch], x_r.at[z, ch], at.d, at.own_line(first))

        @pl.when(at.p == 3)
        def _():
            at.send(frames.at[rows(ch)], relay.at[rows(ch)], on_s.at[z, ch], relay_r.at[ch], at.d, at.own_line(2))

    @pl.when(primary)
    def _():
        for i in range(4):
            cols = slice(i * share, (i + 1) * share)
            seg, pad = segments[:, cols], padding[:, cols]
            row = lax.broadcasted_iota(jnp.int32, (128, share), 0)
            told = jnp.logical_and(row - HEAD_DIM == seg, pad == 1)
            mask = jnp.where(row < HEAD_DIM, 0.0, jnp.where(row < HEAD_DIM + 4, jnp.where(told, 0.0, -1e30), jnp.where(row < HEAD_DIM + 7, 1.0, 0.0)))
            kmask_own[cols, :] = mask.T.astype(BF16)
            hot_own[:, cols] = jnp.where(row[:16] == seg, 1.0, 0.0).astype(BF16)
        at.send(kmask_own, kmask, mask_s.at[0], mask_r.at[0], at.sib, z)
        at.send(hot_own, hot, mask_s.at[1], mask_r.at[1], at.sib, z)
        for ch in range(CHUNKS):
            at.send(frames.at[rows(ch)], x_all.at[z, rows(ch)], fwd_s.at[z, ch], x_r.at[z, ch], at.sib, z)
        pltpu.make_async_copy(w_own, w_t, local.at[2]).start()
        pltpu.make_async_copy(frames, x_all.at[z], local.at[3]).start()
        pltpu.make_async_copy(kmask_own, kmask, local.at[0]).start()
        pltpu.make_async_copy(hot_own, hot, local.at[1]).start()

    pltpu.make_async_copy(small_own, small_all.at[z], local.at[4]).start()

    def weights_first(m):
        src, dst = mats[m]
        r, c = piece(m, at.q, at.b)
        sem = w_r.at[m, z, 2 * at.q + at.b]

        @pl.when(z < 3)
        def _():
            at.send(src.at[r, c], dst.at[z, r, c], line_s.at[m, z, 0], sem, at.d, z + 1)

        @pl.when(z > 0)
        def _():
            at.send(src.at[r, c], dst.at[z, r, c], line_s.at[m, z, 1], sem, at.d, z - 1)

    def shard_at(n):
        low = z // 2
        near = z + low * (3 - 2 * z)
        s = jnp.where(near == 0, n + 1, 2 if n == 0 else (0 if n == 1 else 3))
        return s + low * (3 - 2 * s)

    def weights_line(m, n):
        dst = mats[m][1]
        s = shard_at(n)
        r, c = piece(m, at.q, at.b)
        block = dst.at[s, r, c]
        sem = w_r.at[m, s, 2 * at.q + at.b]
        at.got(block, sem)

        @pl.when(jnp.logical_and(s < z, z < 3))
        def _():
            at.send(block, block, line_s.at[m, s, 0], sem, at.d, z + 1)

        @pl.when(jnp.logical_and(s > z, z > 0))
        def _():
            at.send(block, block, line_s.at[m, s, 1], sem, at.d, z - 1)

        at.send(block, block, near_s.at[m, s], sem, at.near, z)
        at.send(block, block, far_s.at[m, s, 0], sem, at.across, z)
        at.send(block, block, core_s.at[m, s, 0], sem, at.sib, z)

    def weights_near(m, n):
        dst = mats[m][1]
        s = shard_at(n)
        r, c = piece(m, at.near_chip, at.b)
        block = dst.at[s, r, c]
        sem = w_r.at[m, s, 2 * at.near_chip + at.b]
        at.got(block, sem)
        at.send(block, block, far_s.at[m, s, 1], sem, at.across, z)
        at.send(block, block, core_s.at[m, s, 1], sem, at.sib, z)

    def weights_across(m, n):
        dst = mats[m][1]
        s = shard_at(n)
        for i, chip in ((2, at.across_chip), (3, at.opposite_chip)):
            r, c = piece(m, chip, at.b)
            block = dst.at[s, r, c]
            sem = w_r.at[m, s, 2 * chip + at.b]
            at.got(block, sem)
            at.send(block, block, core_s.at[m, s, i], sem, at.sib, z)

    for m in (2, 0, 1):
        weights_first(m)
    for m, (src, dst) in enumerate(mats):
        pltpu.make_async_copy(src, dst.at[z], local.at[5 + m]).start()

    def relay_job(ch):
        @pl.when(at.p == 2)
        def _():
            at.got(relay.at[rows(ch)], relay_r.at[ch])
            at.send(relay.at[rows(ch)], x_all.at[at.own_line(3), rows(ch)], x_s.at[ch], x_r.at[at.own_line(3), ch], at.d, at.own_line(1))

    relay_job(0)

    @pl.when(secondary)
    def _():
        at.got(w_t.at[wq_rows], wq_r.at[at.q])
        for k in (1, 2, 3):
            at.send(w_t.at[wq_rows], w_t.at[wq_rows], wq_s.at[k], wq_r.at[at.q], at.chip(k), z)

    for ch in range(1, CHUNKS):
        relay_job(ch)

    @pl.when(primary)
    def _():
        pltpu.make_async_copy(kmask_own, kmask, local.at[0]).wait()
        pltpu.make_async_copy(hot_own, hot, local.at[1]).wait()
        pltpu.make_async_copy(w_own, w_t, local.at[2]).wait()
        pltpu.make_async_copy(frames, x_all.at[z], local.at[3]).wait()

    pltpu.make_async_copy(small_own, small_all.at[z], local.at[4]).wait()
    for k in (1, 2, 3):
        at.got(small_all.at[(z + k) % 4], small_r.at[(z + k) % 4])

    @pl.when(secondary)
    def _():
        at.got(kmask, mask_r.at[0])
        at.got(hot, mask_r.at[1])
        for k in (1, 2, 3):
            other = (at.q + k) % 4
            at.got(w_t.at[pl.ds(pl.multiple_of(other * quarter, 16), quarter)], wq_r.at[other])

    w_pad[...] = jnp.zeros_like(w_pad)
    for i in range(2):
        for h in range(heads):
            w_pad[(i * heads + h) * 128 : (i * heads + h) * 128 + HEAD_DIM] = w_t[
                (i + 1) * width + h * HEAD_DIM : (i + 1) * width + (h + 1) * HEAD_DIM
            ]

    A, B, C = weights_line, weights_near, weights_across
    early = {1: ((A, 0, 0), (A, 0, 1), (A, 2, 0),), 2: ((A, 2, 1), (A, 1, 0), (A, 1, 1), (B, 0, 0), (B, 2, 0), (B, 1, 0),), 3: ((A, 0, 2), (C, 0, 0),)}
    jobs = {0: ((C, 1, 0), (B, 0, 1),), 1: ((B, 2, 1), (A, 2, 2),), 2: ((C, 2, 0),), 3: ((C, 0, 1), (B, 1, 1),), 4: ((A, 1, 2), (B, 0, 2),), 5: ((C, 2, 1), (B, 2, 2), (C, 1, 1),), 7: ((C, 0, 2), (C, 2, 2),), 9: ((B, 1, 2),)}

    def run_jobs(table, now):
        for when, todo in table.items():
            @pl.when(now == when)
            def _():
                for job, m, n in todo:
                    job(m, n)

    def gather_step(k, _):
        place = jnp.where(at.pp == 0, k, jnp.where(k == 0, 1, jnp.where(k == 1, 2, jnp.where(k == 2, 0, 3))))
        s = at.line(place)
        for ch in range(CHUNKS):
            block = x_all.at[s, rows(ch)]

            @pl.when(jnp.logical_or(k > 0, secondary))
            def _():
                at.got(block, x_r.at[s, ch])

            @pl.when(jnp.logical_and(k > 0, primary))
            def _():
                @pl.when(jnp.logical_and(at.p == 1, place >= 2))
                def _():
                    at.send(block, block, on_s.at[s, ch], x_r.at[s, ch], at.d, at.own_line(0))

                at.send(block, block, fwd_s.at[s, ch], x_r.at[s, ch], at.sib, z)

        run_jobs(early, k)
        cols = pl.ds(pl.multiple_of(s * share, share), share)
        biases = jnp.transpose(small_all[at.group])
        project(
            x_all[s], w_t[...], w_pad[...], biases[: 3 * width, 1:2], small_all[at.group, 2:3, : heads * 128], kmask[cols, :],
            hot[:, cols], cols, q_aug, k_aug, v_aug, k_t, v_t,
        )
        return 0

    lax.fori_loop(0, 4, gather_step, 0)

    def attend_step(t, _):
        turn, h = t // heads, t % heads
        i = (z + jnp.where(turn == 0, 2, jnp.where(turn == 1, 1, jnp.where(turn == 2, 3, 0)))) % 4
        cols = pl.ds(pl.multiple_of(i * share, share), share)
        mixed_heads[i, pl.ds(pl.multiple_of(h * HEAD_DIM, HEAD_DIM), HEAD_DIM), :] = attend(h, cols, q_aug, k_aug, v_t)
        mine = jnp.logical_and(primary, i == z)
        block = mixed_own.at[pl.ds(pl.multiple_of(at.group * width, 64), width)]

        @pl.when(jnp.logical_and(h == heads - 1, mine))
        def _():
            pltpu.make_async_copy(mixed_heads.at[i], block, mix_s.at[i]).start()

        @pl.when(jnp.logical_and(h == heads - 1, jnp.logical_not(mine)))
        def _():
            at.send(mixed_heads.at[i], block, mix_s.at[i], mix_r.at[at.group], at.row, i)

        run_jobs(jobs, t)
        return 0

    lax.fori_loop(0, 4 * heads, attend_step, 0)
    for job, m, n in jobs.get(99, ()):
        job(m, n)

    def leave(i, src, dst, part=None):
        if part is not None:
            src, dst, i = src.at[part], dst.at[part], i + part
        left.append((src, dst, out_sems.at[i]))
        pltpu.make_async_copy(src, dst, out_sems.at[i]).start()

    left = []
    for i, (src, dst) in enumerate((
        (x_all, x_all_h), (w_t, w_t_h), (mixed_heads, mixed_heads_h), (q_aug, q_aug_h), (k_aug, k_aug_h), (v_aug, v_aug_h), (k_t, k_t_h),
    )):
        leave(i, src, dst)

    def arrive(m):
        if m == 2:
            for g in range(4):
                mine = jnp.logical_and(primary, z == g)
                block = mixed_own.at[pl.ds(g * width, width)]

                @pl.when(mine)
                def _():
                    pltpu.make_async_copy(mixed_heads.at[g], block, mix_s.at[g]).wait()

                @pl.when(jnp.logical_not(mine))
                def _():
                    at.got(block, mix_r.at[g])

        for job, m2, n in {0: ((C, 1, 2),)}.get(m, ()):
            job(m2, n)
        src, dst = mats[m]
        pltpu.make_async_copy(src, dst.at[z], local.at[5 + m]).wait()
        for j in range(4):
            chip = (at.q + j) % 4
            r, c = piece(m, chip, 1 - at.b)
            for k in (1, 2, 3):
                s = (z + k) % 4
                at.got(dst.at[s, r, c], w_r.at[m, s, 2 * chip + 1 - at.b])

    feed_forward(
        skip, mixed_own, frames, cot, b_out, gain_one, shift_one, b_down, gain_two, shift_two, small_all,
        out_all, up_all, down_all, arrive, leave,
        (mixed_own_h, layer_h, gone_h, gmixed_h, normed_h, act_h, ginner_h, gbranch_h, gatt_h),
        layer, gone, gmixed, normed, act, ginner, gbranch, gatt, small_sums, slope,
    )
    for src, dst, sem in left:
        pltpu.make_async_copy(src, dst, sem).wait()

    for i in range(4):
        mine = jnp.logical_and(primary, z == i)

        @pl.when(jnp.logical_not(mine))
        def _():
            at.sent(mixed_heads.at[i], mix_s.at[i])

    for k in range(3):
        at.sent(small_own, small_s.at[k])
    for ch in range(CHUNKS):
        at.sent(frames.at[rows(ch)], on_s.at[z, ch])

        @pl.when(at.p == 2)
        def _():
            at.sent(relay.at[rows(ch)], x_s.at[ch])

        @pl.when(at.p == 1)
        def _():
            for place in (2, 3):
                at.sent(x_all.at[at.own_line(place), rows(ch)], on_s.at[at.own_line(place), ch])

        @pl.when(primary)
        def _():
            for s in range(4):
                at.sent(x_all.at[s, rows(ch)], fwd_s.at[s, ch])

    @pl.when(primary)
    def _():
        at.sent(kmask_own, mask_s.at[0])
        at.sent(hot_own, mask_s.at[1])
        at.sent(w_own.at[wq_rows], wq_s.at[0])

    @pl.when(secondary)
    def _():
        for k in (1, 2, 3):
            at.sent(w_t.at[wq_rows], wq_s.at[k])

    for m, (src, dst) in enumerate(mats):
        r, c = piece(m, at.q, at.b)
        block = src.at[r, c]
        for s in range(4):
            @pl.when(jnp.logical_and(s <= z, z < 3))
            def _():
                at.sent(block, line_s.at[m, s, 0])

            @pl.when(jnp.logical_and(s >= z, z > 0))
            def _():
                at.sent(block, line_s.at[m, s, 1])

            @pl.when(s != z)
            def _():
                at.sent(block, near_s.at[m, s])
                for i in range(2):
                    at.sent(block, far_s.at[m, s, i])
                for i in range(4):
                    at.sent(block, core_s.at[m, s, i])


def run_forward(
    skip, frames, cot, w_query, w_key, w_value, b_query, b_value, b_up, b_out, gain_one, shift_one, b_down, gain_two, shift_two,
    segments, padding, w_up, w_down, w_out,
):
    share, d = frames.shape
    length = segments.shape[1]
    width = w_query.shape[0]
    heads = width // HEAD_DIM
    f = w_up.shape[1]
    any_ = pl.BlockSpec(memory_space=pl.ANY)
    dma, V = pltpu.SemaphoreType.DMA, pltpu.VMEM
    return pl.pallas_call(
        forward_kernel,
        out_shape=(
            S((4, share, d)), S((3 * width, d)), S((4, width, share)), S((4 * width, share)),
            S((heads, 128, length)), S((heads, length, 128)), S((heads, length, 128)), S((heads, HEAD_DIM, length)),
            S((share, d)), S((share, d), F32), S((4 * width, share)), S((share, d)), S((4, share, f)),
            S((4, share, f)), S((share, d)), S((share, d)), S((16, d), F32),
        ),
        in_specs=[SMEM] + [VMEM] * 16 + [any_] * 3, out_specs=[any_] * 16 + [VMEM],
        scratch_shapes=[
            V((4, share, d), BF16), V((3 * width, d), BF16), V((4, width, share), BF16), V((4 * width, share), BF16),
            V((heads, 128, length), BF16), V((heads, length, 128), BF16), V((heads, length, 128), BF16), V((heads, HEAD_DIM, length), BF16),
            V((share, d), BF16), V((share, d), F32), V((4 * width, share), BF16), V((share, d), BF16), V((4, share, f), BF16),
            V((4, share, f), BF16), V((share, d), BF16), V((share, d), BF16), dma((22,)),
            V((4, 8, d), F32), V((4, d, f), BF16), V((4, f, d), BF16), V((4, width, d), BF16), V((4, share, f), F32),
            V((share, d), BF16), V((heads, HEAD_DIM, length), BF16), V((2 * heads * 128, d), BF16),
            V((length, 128), BF16), V((16, length), BF16),
            V((3 * width, d), BF16), V((8, d), F32), V((length, 128), BF16), V((16, length), BF16),
            dma((3,)), dma((4,)), dma((2,)), dma((2,)), dma((4,)), dma((4,)), dma((CHUNKS,)), dma((4, CHUNKS)), dma((CHUNKS,)),
            dma((4, CHUNKS)), dma((4, CHUNKS)), dma((4,)), dma((4,)), dma((8,)),
            dma((3, 4, 2)), dma((3, 4)), dma((3, 4, 2)), dma((3, 4, 4)), dma((3, 4, 8)),
        ],
        compiler_params=pltpu.CompilerParams(vmem_limit_bytes=LIMIT, collective_id=0, has_side_effects=True),
        name="forward",
    )(skip, frames, cot, w_query, w_key, w_value, b_query, b_value, b_up, b_out, gain_one, shift_one, b_down, gain_two, shift_two,
      segments, padding, w_up, w_down, w_out)


def attend_back(h, keys, queries, q_aug, k_aug, v_aug, k_t, do_aug, dk_acc, dv_acc):
    weights = jnp.exp(mm(k_aug[h, keys, :], q_aug[h, :, queries]))
    dv_acc[h, :, keys] += mm(do_aug[h, 0:HEAD_DIM, queries], weights.astype(BF16), 1, 1)
    grad = (weights * mm(v_aug[h, keys, :], do_aug[h, :, queries])).astype(BF16)
    dk_acc[h, :, keys] += mm(q_aug[h, 0:HEAD_DIM, queries], grad, 1, 1)
    return mm(k_t[h, :, keys], grad)


def total(first, *others):
    out = first.astype(F32)
    for other in others:
        out = out + other.astype(F32)
    return out


def backward_kernel(
    skip_ref, gmixed, mixed_own_h, normed_h, act_h, ginner_h, gbranch_h, gatt_h, small, gone_h, cot_h,
    x_all, w_t_h, mixed_heads_h, q_aug_h, k_aug_h, v_aug_h, k_t_h,
    frames_grad, dw_out, up_out, down_out, out_out, small_out,
    mixed_own, normed, act, ginner, gbranch, gatt, gone, cot, w_t, mixed_heads, q_aug, k_aug, v_aug, k_t, load_sems,
    do_in, do_aug, dk_acc, dv_acc, dq_acc, dq_keep, grads, x_sem,
    big, away, core_in, near_in, across_in, mid, z_in, bigo, core_ino, near_ino, across_ino, mido, z_ino,
    sib_in, line_in, dw_own, dw_in, dw_mid, dw_z, small_mine, small_plane, small_mid, small_z,
    gm_s, gm_r, ci_s, ci_r, nr_s, nr_r, ac_s, ac_r, z_s, z_r, ag_s, ag_r,
    part_s, part_r, line_s, line_r, dwp_s, dwp_r, dwz_s, dwz_r, dwo_s, dwo_r, dwf_s, sp_s, sp_r, sz_s, sz_r,
):
    at = Place()
    heads = q_aug.shape[0]
    width = heads * HEAD_DIM
    share = gatt.shape[0]
    length = q_aug.shape[2]
    step_rows = share // CHUNKS
    z, c, q = at.z, at.b, at.q
    primary = at.primary
    secondary = jnp.logical_not(primary)
    loads = []
    for src, dst in ((gbranch_h, gbranch), (act_h, act), (normed_h, normed), (ginner_h, ginner), (mixed_own_h, mixed_own), (gatt_h, gatt),
                     (mixed_heads_h, mixed_heads), (q_aug_h, q_aug), (k_aug_h, k_aug), (v_aug_h, v_aug), (k_t_h, k_t), (w_t_h, w_t),
                     (gone_h, gone), (cot_h, cot)):
        pltpu.make_async_copy(src, dst, load_sems.at[len(loads)]).start()
        loads.append((src, dst))

    def loaded(*numbers):
        for n in numbers:
            pltpu.make_async_copy(*loads[n], load_sems.at[n]).wait()

    at.barrier()

    for g in range(4):
        block = gmixed.at[pl.ds(g * width, width)]
        near = at.b == g // 2
        to_d = jnp.where(near, at.d, at.sib)
        to_z = jnp.where(near, g, (g + 2) % 4)
        mine = jnp.logical_and(near, z == g)

        @pl.when(mine)
        def _():
            pltpu.make_async_copy(block, do_in.at[z], gm_s.at[g]).start()

        @pl.when(jnp.logical_not(mine))
        def _():
            at.send(block, do_in.at[z], gm_s.at[g], gm_r.at[z], to_d, to_z)

    n_big = 8
    half = big.shape[1]
    quarter = half // 4
    halfo = bigo.shape[3]
    quartero = bigo.shape[2] // 4
    finals = (down_out, up_out, out_out)

    def big_rows(chip):
        return pl.ds(pl.multiple_of(chip * quarter, 16), quarter)

    def out_rows(chip):
        return pl.ds(pl.multiple_of(chip * quartero, 16), quartero)

    def weight_job(j):
        if j == 0:
            loaded(0, 1)
        if j == n_big // 2:
            loaded(2, 3)
        if j == n_big:
            loaded(4, 5)
        if j < n_big:
            kind, s = j // 4, j % 4
            made = mm(act[s], gbranch[...], 0, 0) if kind == 0 else mm(normed[...], ginner[s], 0, 0)
            made = made.astype(BF16)
            if j >= 4:
                at.sent(away.at[j % 4], ci_s.at[j - 4])

            @pl.when(c == 0)
            def _():
                big[j] = made[:half]
                away[j % 4] = made[half:]

            @pl.when(c == 1)
            def _():
                big[j] = made[half:]
                away[j % 4] = made[:half]

            at.send(away.at[j % 4], core_in.at[j], ci_s.at[j], ci_r.at[j], at.sib, z)
        else:
            for s in range(4):
                made = mm(mixed_own[s * width : (s + 1) * width, :], gatt[...])
                for i in range(2):
                    bigo[i, s] = made[:, i * halfo : (i + 1) * halfo].astype(BF16)
            at.send(bigo.at[1 - c], core_ino, ci_s.at[j], ci_r.at[j], at.sib, z)

    def core_job(j):
        at.got(core_in.at[j] if j < n_big else core_ino, ci_r.at[j])
        if j < n_big:
            big[j] = total(big[j], core_in[j]).astype(BF16)
        else:
            bigo[c] = total(bigo[c], core_ino[...]).astype(BF16)
        for i, chip in enumerate((at.near_chip, at.opposite_chip)):
            if j < n_big:
                at.send(big.at[j, big_rows(chip)], near_in.at[i, j], nr_s.at[j, i], nr_r.at[j, i], at.near, z)
            else:
                at.send(bigo.at[c, :, out_rows(chip)], near_ino.at[i], nr_s.at[j, i], nr_r.at[j, i], at.near, z)

    def near_job(j):
        if j < n_big:
            for i in range(2):
                at.got(near_in.at[i, j], nr_r.at[j, i])
            near_in[1, j] = total(big[j, big_rows(at.across_chip)], near_in[1, j]).astype(BF16)
            at.send(near_in.at[1, j], across_in.at[j], ac_s.at[j], ac_r.at[j], at.across, z)
        else:
            for i in range(2):
                at.got(near_ino.at[i], nr_r.at[j, i])
            near_ino[1] = total(bigo[c, :, out_rows(at.across_chip)], near_ino[1]).astype(BF16)
            at.send(near_ino.at[1], across_ino, ac_s.at[j], ac_r.at[j], at.across, z)

    def plane_job(j):
        if j < n_big:
            kind, s = j // 4, j % 4
            at.got(across_in.at[j], ac_r.at[j])
            mid[j] = total(big[j, big_rows(q)], near_in[0, j], across_in[j]).astype(BF16)

            @pl.when(z != s)
            def _():
                slot = 3 - (s - z + 4) % 4
                at.send(mid.at[j], z_in.at[slot, kind], z_s.at[j], z_r.at[kind, slot], at.d, s)
        else:
            at.got(across_ino, ac_r.at[j])
            mido[...] = total(bigo[c, :, out_rows(q)], near_ino[0], across_ino[...]).astype(BF16)
            for s in range(4):
                @pl.when(z != s)
                def _():
                    slot = 3 - (s - z + 4) % 4
                    at.send(mido.at[s], z_ino.at[slot], z_s.at[j + s], z_r.at[2, slot], at.d, s)

    def final_piece(kind, chip, core):
        if kind < 2:
            return finals[kind].at[pl.ds(pl.multiple_of(core * half + chip * quarter, 16), quarter)]
        return out_out.at[out_rows(chip), pl.ds(pl.multiple_of(core * halfo, 128), halfo)]

    def final_job(kind):
        for k in range(3):
            at.got(z_in.at[k, kind] if kind < 2 else z_ino.at[k], z_r.at[kind, k])
        piece = final_piece(kind, q, c)
        if kind < 2:
            piece[...] = total(mid[4 * kind + z], z_in[0, kind], z_in[1, kind], z_in[2, kind]).astype(BF16)
        else:
            piece[...] = total(mido[z], z_ino[0], z_ino[1], z_ino[2]).astype(BF16)
        sem = ag_r.at[kind, 2 * q + c]
        at.send(piece, piece, ag_s.at[kind, 0], sem, at.near, z)
        at.send(piece, piece, ag_s.at[kind, 1], sem, at.across, z)
        at.send(piece, piece, ag_s.at[kind, 2], sem, at.sib, z)

    def pass_job(kind):
        piece = final_piece(kind, at.near_chip, c)
        sem = ag_r.at[kind, 2 * at.near_chip + c]
        at.got(piece, sem)
        at.send(piece, piece, ag_s.at[kind, 3], sem, at.across, z)
        at.send(piece, piece, ag_s.at[kind, 4], sem, at.sib, z)

    def share_job(kind):
        for i, chip in enumerate((at.across_chip, at.opposite_chip)):
            piece = final_piece(kind, chip, c)
            sem = ag_r.at[kind, 2 * chip + c]
            at.got(piece, sem)
            at.send(piece, piece, ag_s.at[kind, 5 + i], sem, at.sib, z)

    def end_job(kind):
        for k in range(4):
            chip = (q + k) % 4
            at.got(final_piece(kind, chip, 1 - c), ag_r.at[kind, 2 * chip + 1 - c])

    for j in range(n_big + 1):
        weight_job(j)
        if j >= 2:
            core_job(j - 2)
    core_job(n_big - 1)
    core_job(n_big)
    x_here, part = core_in.at[0:4], core_in.at[4:8]
    pltpu.make_async_copy(x_all, x_here, x_sem.at[0]).start()

    late = at.rb
    side = length // 2

    def prepare(i):
        mine = jnp.logical_and(primary, z == i)

        @pl.when(mine)
        def _():
            pltpu.make_async_copy(gmixed.at[pl.ds(pl.multiple_of(i * width, 64), width)], do_in.at[i], gm_s.at[i]).wait()

        @pl.when(jnp.logical_not(mine))
        def _():
            at.got(do_in.at[i], gm_r.at[i])

        cols = pl.ds(pl.multiple_of(i * share, share), share)
        for h in range(heads):
            hs = slice(h * HEAD_DIM, (h + 1) * HEAD_DIM)
            do = do_in[i, hs, :]
            do_aug[h, 0:HEAD_DIM, cols] = do
            inner = jnp.sum(do.astype(F32) * mixed_heads[i, hs, :].astype(F32), 0, keepdims=True)
            do_aug[h, HEAD_DIM : HEAD_DIM + 16, cols] = pad_rows(split3(-inner), 16, share)
            do_aug[h, HEAD_DIM + 16 :, cols] = jnp.zeros((48, share), BF16)

    def half_row(n):
        return pl.ds(pl.multiple_of(n * side, side), side)

    dk_acc[...] = jnp.zeros_like(dk_acc)
    dv_acc[...] = jnp.zeros_like(dv_acc)

    N, M, Q, U, V = near_job, plane_job, final_job, pass_job, share_job
    jobs = {-1: ((N, 0), (N, 1),), 0: ((N, 2), (M, 0),), 1: ((M, 1),), 2: ((N, 3), (M, 2),), 4: ((N, 4), (M, 3),), 6: ((N, 5), (M, 4),), 8: ((N, 6), (M, 5),), 50: ((Q, 0),), 10: ((N, 7), (M, 6),)}

    def attention_step(t, _):
        last = t >= 3 * heads
        h = jnp.where(last, t - 3 * heads, t // 3)
        turn = jnp.where(last, 3, t % 3)
        keys = half_row(jnp.where(jnp.logical_or(turn == 0, last), late, 1 - late))
        queries = half_row(jnp.where(turn < 2, 1 - late, late))
        dq = attend_back(h, keys, queries, q_aug, k_aug, v_aug, k_t, do_aug, dk_acc, dv_acc)
        hs = pl.ds(pl.multiple_of(h * HEAD_DIM, HEAD_DIM), HEAD_DIM)

        @pl.when(turn == 0)
        def _():
            dq_acc[...] = dq

        @pl.when(turn == 1)
        def _():
            grads[hs, queries] = ((dq_acc[...] + dq).astype(BF16).astype(F32) * HEAD_DIM**-0.5).astype(BF16)

        @pl.when(turn == 2)
        def _():
            dq_keep[h] = dq

        @pl.when(turn == 3)
        def _():
            grads[hs, queries] = ((dq_keep[h] + dq).astype(BF16).astype(F32) * HEAD_DIM**-0.5).astype(BF16)

        for when, todo in jobs.items():
            if 0 <= when < 4 * heads:
                @pl.when(t == when)
                def _():
                    for job, j in todo:
                        job(j)

        return 0

    def rows(ch):
        return pl.ds(ch * step_rows, step_rows)

    def part_job(s):
        part[s] = mm(grads[:, pl.ds(pl.multiple_of(s * share, share), share)], w_t[...], 0, 0).astype(BF16)

        @pl.when(secondary)
        def _():
            for ch in range(CHUNKS):
                at.send(part.at[s, rows(ch)], sib_in.at[s, rows(ch)], part_s.at[s, ch], part_r.at[s, ch], at.sib, z)

    def line_job(place):
        s = at.line(place)
        for ch in range(CHUNKS):
            here = (s, rows(ch))

            @pl.when(jnp.logical_and(primary, place != at.p))
            def _():
                at.got(sib_in.at[here], part_r.at[s, ch])

                @pl.when(jnp.logical_and(at.p == 1, place >= 2))
                def _():
                    at.got(line_in.at[here], line_r.at[s, ch])
                    part[here] = total(part[here], sib_in[here], line_in[here]).astype(BF16)
                    at.send(part.at[here], line_in.at[here], line_s.at[s, ch], line_r.at[s, ch], at.d, at.own_line(2))

                @pl.when(jnp.logical_or(at.p == 0, place == 0))
                def _():
                    part[here] = total(part[here], sib_in[here]).astype(BF16)
                    at.send(part.at[here], line_in.at[here], line_s.at[s, ch], line_r.at[s, ch], at.d, at.own_line(1 - at.p))

    def finish(n):
        cols = half_row(n)
        for h in range(heads):
            grads[width + h * HEAD_DIM : width + (h + 1) * HEAD_DIM, cols] = dk_acc[h, :, cols].astype(BF16)
            grads[2 * width + h * HEAD_DIM : 2 * width + (h + 1) * HEAD_DIM, cols] = dv_acc[h, :, cols].astype(BF16)

    loaded(6, 7, 8, 9, 10, 11)
    for i in range(4):
        prepare(i)
    for job, j in jobs.get(-1, ()):
        job(j)
    lax.fori_loop(0, 3 * heads, attention_step, 0)
    finish(1 - late)
    for place in (3, 2):
        part_job(at.line(place))

    @pl.when(at.p == 0)
    def _():
        line_job(3)
        line_job(2)

    for job, j in jobs.get(50, ()):
        job(j)
    lax.fori_loop(3 * heads, 4 * heads, attention_step, 0)
    finish(late)
    for place in (0, 1):
        part_job(at.line(place))

    @pl.when(at.p == 0)
    def _():
        line_job(1)

    @pl.when(at.p == 1)
    def _():
        line_job(0)

    small_mine[...] = small[...]
    small_mine[pl.ds(10 + at.group, 1), 0 : 3 * width] = mm(jnp.ones((8, length), BF16), grads[...], 1, 1)[0:1]
    at.send(small_mine, small_plane.at[0], sp_s.at[0], sp_r.at[0], at.sib, z)
    for k in (1, 2, 3):
        at.send(small_mine, small_plane.at[4 - k], sp_s.at[k], sp_r.at[4 - k], at.chip(k), z)
        at.send(small_mine, small_plane.at[7 - k], sp_s.at[3 + k], sp_r.at[7 - k], at.other(k), z)

    pltpu.make_async_copy(x_all, x_here, x_sem.at[0]).wait()
    made = mm(grads[:, 0:share], x_here[0])
    for s in range(1, 4):
        made = made + mm(grads[:, s * share : (s + 1) * share], x_here[s])
    made = made.astype(BF16)
    fourth = made.shape[0] // 4
    for i in range(4):
        dw_own[i] = made[i * fourth : (i + 1) * fourth]
    at.send(dw_own.at[at.near_chip], dw_in.at[0], dwp_s.at[0], dwp_r.at[0], at.near, z)
    at.send(dw_own.at[at.opposite_chip], dw_in.at[1], dwp_s.at[1], dwp_r.at[1], at.near, z)

    def dw_rows(i):
        return pl.ds(pl.multiple_of(i * fourth, 16), fourth)

    def small_sum(_):
        for k in range(7):
            at.got(small_plane.at[k], sp_r.at[k])
        small_mid[...] = total(small_mine[...], *(small_plane[k] for k in range(7)))
        for k in (1, 2, 3):
            at.send(small_mid, small_z.at[3 - k], sz_s.at[k - 1], sz_r.at[3 - k], at.d, (z + k) % 4)

    def small_end(_):
        for k in range(3):
            at.got(small_z.at[k], sz_r.at[k])
        small_out[...] = total(small_mid[...], small_z[0], small_z[1], small_z[2])

    def onward(place):
        @pl.when(at.p == 1)
        def _():
            line_job(place)

        if place == 3:
            @pl.when(at.p == 2)
            def _():
                s = at.own_line(3)
                for ch in range(CHUNKS):
                    here = (s, rows(ch))
                    at.got(line_in.at[here], line_r.at[s, ch])
                    at.send(line_in.at[here], line_in.at[here], line_s.at[s, ch], line_r.at[s, ch], at.d, s)

    def dw_across(_):
        for k in range(2):
            at.got(dw_in.at[k], dwp_r.at[k])
        dw_in[1] = total(dw_own[at.across_chip], dw_in[1]).astype(BF16)
        at.send(dw_in.at[1], dw_in.at[2], dwp_s.at[2], dwp_r.at[2], at.across, z)

    def dw_plane(_):
        at.got(dw_in.at[2], dwp_r.at[2])
        dw_mid[...] = total(dw_own[q], dw_in[0], dw_in[2]).astype(BF16)

        @pl.when(secondary)
        def _():
            at.send(dw_mid, dw_z, dwz_s.at[0], dwz_r.at[0], at.d, at.far)

    def dw_final(_):
        @pl.when(primary)
        def _():
            at.got(dw_z, dwz_r.at[0])
            piece = dw_out.at[dw_rows(q)]
            piece[...] = total(dw_mid[...], dw_z[...]).astype(BF16)
            at.send(piece, piece, dwo_s.at[0], dwo_r.at[q], at.near, z)
            at.send(piece, piece, dwo_s.at[1], dwo_r.at[q], at.across, z)
            at.send(piece, piece, dwo_s.at[2], dwo_r.at[q], at.sib, z)

    def dw_pass(_):
        @pl.when(primary)
        def _():
            i = at.near_chip
            piece = dw_out.at[dw_rows(i)]
            at.got(piece, dwo_r.at[i])
            at.send(piece, piece, dwo_s.at[3], dwo_r.at[i], at.across, z)
            at.send(piece, piece, dwf_s.at[0], dwo_r.at[i], at.sib, z)

    for job, j in ((onward, 3), (M, 7), (small_sum, 0), (dw_across, 0), (N, 8), (dw_plane, 0), (M, 8), (onward, 2), (dw_final, 0), (U, 0), (Q, 1), (dw_pass, 0), (U, 1), (Q, 2), (V, 0), (small_end, 0), (U, 2), (V, 1), (V, 2)):
        job(j)

    skipped = skip_ref[0] == 1
    loaded(12, 13)
    for ch in range(CHUNKS):
        at.got(line_in.at[z, rows(ch)], line_r.at[z, ch])

    @pl.when(primary)
    def _():
        for ch in range(CHUNKS):
            at.got(sib_in.at[z, rows(ch)], part_r.at[z, ch])
        grad = gone[...] + total(part[z], sib_in[z], line_in[z])
        frames_grad[...] = jnp.where(skipped, cot[...].astype(F32), grad).astype(BF16)

    @pl.when(secondary)
    def _():
        grad = gone[...] + line_in[z].astype(F32)
        frames_grad[...] = jnp.where(skipped, cot[...].astype(F32), grad).astype(BF16)


    @pl.when(primary)
    def _():
        for k, i in ((1, at.across_chip), (2, at.opposite_chip)):
            piece = dw_out.at[dw_rows(i)]
            at.got(piece, dwo_r.at[i])
            at.send(piece, piece, dwf_s.at[k], dwo_r.at[i], at.sib, z)

    @pl.when(secondary)
    def _():
        for i in range(4):
            at.got(dw_out.at[dw_rows(i)], dwo_r.at[i])

    for kind in range(3):
        end_job(kind)

    for g in range(4):
        mine = jnp.logical_and(primary, z == g)

        @pl.when(jnp.logical_not(mine))
        def _():
            at.sent(gmixed.at[pl.ds(g * width, width)], gm_s.at[g])

    for j in range(n_big):
        if j >= 4:
            at.sent(core_in.at[j], ci_s.at[j])
        for k in range(2):
            at.sent(near_in.at[k, j], nr_s.at[j, k])
        at.sent(across_in.at[j], ac_s.at[j])

        @pl.when(z != j % 4)
        def _():
            at.sent(mid.at[j], z_s.at[j])

    at.sent(core_ino, ci_s.at[n_big])
    for k in range(2):
        at.sent(near_ino.at[k], nr_s.at[n_big, k])
    at.sent(across_ino, ac_s.at[n_big])
    for s in range(4):
        @pl.when(z != s)
        def _():
            at.sent(mido.at[s], z_s.at[n_big + s])

    for kind in range(3):
        for k in range(7):
            at.sent(final_piece(kind, q, c), ag_s.at[kind, k])
    for k in range(7):
        at.sent(small_mine, sp_s.at[k])
    for k in range(3):
        at.sent(small_mid, sz_s.at[k])
        at.sent(dw_mid, dwp_s.at[k])

    @pl.when(secondary)
    def _():
        at.sent(dw_mid, dwz_s.at[0])
        for s in range(4):
            for ch in range(CHUNKS):
                at.sent(part.at[s, rows(ch)], part_s.at[s, ch])

    @pl.when(primary)
    def _():
        for k in range(4):
            at.sent(dw_mid, dwo_s.at[k])
        for k in range(3):
            at.sent(dw_mid, dwf_s.at[k])
        for k in (1, 2, 3):
            for ch in range(CHUNKS):
                s = at.line((at.p + k) % 4)
                at.sent(part.at[s, rows(ch)], line_s.at[s, ch])

    @pl.when(at.p == 2)
    def _():
        for ch in range(CHUNKS):
            at.sent(line_in.at[at.own_line(3), rows(ch)], line_s.at[at.own_line(3), ch])


def run_backward(skip, gmixed, mixed_own, normed, act, ginner, gbranch, gatt, small, gone, cot,
                 x_all, w_t, mixed_heads, q_aug, k_aug, v_aug, k_t):
    share, d = gatt.shape
    any_ = pl.BlockSpec(memory_space=pl.ANY)
    f = act.shape[2]
    heads, _, length = q_aug.shape
    width = heads * HEAD_DIM
    dma, V = pltpu.SemaphoreType.DMA, pltpu.VMEM
    hd, hf, ho = d // 2, f // 2, d // 2
    return pl.pallas_call(
        backward_kernel,
        out_shape=(
            S((share, d)), S((3 * width, d)), S((d, f)), S((f, d)), S((width, d)), S((16, d), F32),
        ),
        in_specs=[SMEM] + [any_] * 7 + [VMEM] + [any_] * 9, out_specs=[VMEM] * 6,
        scratch_shapes=[
            V((4 * width, share), BF16), V((share, d), BF16), V((4, share, f), BF16), V((4, share, f), BF16), V((share, d), BF16),
            V((share, d), BF16), V((share, d), F32), V((share, d), BF16), V((3 * width, d), BF16), V((4, width, share), BF16),
            V((heads, 128, length), BF16), V((heads, length, 128), BF16), V((heads, length, 128), BF16),
            V((heads, HEAD_DIM, length), BF16), dma((14,)),
            V((4, width, share), BF16), V((heads, 128, length), BF16),
            V((heads, HEAD_DIM, length), F32), V((heads, HEAD_DIM, length), F32),
            V((HEAD_DIM, length // 2), F32), V((heads, HEAD_DIM, length // 2), F32), V((3 * width, length), BF16), dma((1,)),
            V((8, hd, d), BF16), V((4, hd, d), BF16), V((8, hd, d), BF16), V((2, 8, hd // 4, d), BF16), V((8, hd // 4, d), BF16), V((8, hd // 4, d), BF16),
            V((3, 2, hd // 4, d), BF16),
            V((2, 4, width, ho), BF16), V((4, width, ho), BF16), V((2, 4, width // 4, ho), BF16), V((4, width // 4, ho), BF16), V((4, width // 4, ho), BF16),
            V((3, width // 4, ho), BF16),
            V((4, share, d), BF16), V((4, share, d), BF16),
            V((4, 3 * width // 4, d), BF16), V((3, 3 * width // 4, d), BF16), V((3 * width // 4, d), BF16), V((3 * width // 4, d), BF16),
            V((16, d), F32), V((7, 16, d), F32), V((16, d), F32), V((3, 16, d), F32),
            dma((4,)), dma((4,)), dma((9,)), dma((9,)), dma((9, 2)), dma((9, 2)), dma((9,)), dma((9,)), dma((12,)), dma((3, 3)),
            dma((3, 7)), dma((3, 8)),
            dma((4, CHUNKS)), dma((4, CHUNKS)), dma((4, CHUNKS)), dma((4, CHUNKS)), dma((3,)), dma((3,)), dma((1,)), dma((1,)),
            dma((4,)), dma((4,)), dma((3,)), dma((7,)), dma((7,)), dma((3,)), dma((3,)),
        ],
        compiler_params=pltpu.CompilerParams(vmem_limit_bytes=LIMIT, collective_id=1, has_side_effects=True),
        name="attention_backward",
    )(skip, gmixed, mixed_own, normed, act, ginner, gbranch, gatt, small, gone, cot,
      x_all, w_t, mixed_heads, q_aug, k_aug, v_aug, k_t)


def last_kernel(dw, up, down, out, small, *outs):
    z = lax.axis_index("mp")
    d_query, d_key, d_value, d_up, d_down, d_out, b_query, b_value, b_up = outs[:9]
    width = d_out.shape[0]
    for i, target in enumerate((d_query, d_key, d_value)):
        target[...] = dw[i * width : (i + 1) * width].astype(F32)
    d_up[...] = up[...].astype(F32)
    d_down[...] = down[...].astype(F32)
    d_out[...] = out[...].astype(F32)
    bias = small[pl.ds(10 + z, 1), :]
    b_query[...] = bias[:, 0:width].reshape(width)
    b_value[...] = bias[:, 2 * width : 3 * width].reshape(width)
    b_up[...] = small[pl.ds(6 + z, 1), :].reshape(small.shape[1])
    for i, target in enumerate(outs[9:]):
        target[...] = small[i : i + 1, :].reshape(small.shape[1])


def S(shape, dtype=BF16):
    return jax.ShapeDtypeStruct(shape, dtype)


def shards(
    frames, cotangent, segments, padding, skip_flag, w_query, b_query, w_key, w_value, b_value,
    w_out, b_out, gain_one, shift_one, w_up, b_up, w_down, b_down, gain_two, shift_two,
):
    mp = lax.axis_size("mp")
    share, d = frames.shape[1:]
    length = segments.shape[1]
    width = w_query.shape[1]
    heads = width // HEAD_DIM
    params = pltpu.CompilerParams(vmem_limit_bytes=LIMIT)
    own = frames[0]
    f = w_up.shape[1]
    (
        x_all, w_t, mixed, mixed_own, q_aug, k_aug, v_aug, k_t,
        layer, gone, gmixed, normed, act, ginner, gbranch, gatt, small,
    ) = run_forward(
        skip_flag, own, cotangent[0], w_query.T, w_key.T, w_value.T, b_query, b_value, b_up,
        b_out, gain_one, shift_one, b_down, gain_two, shift_two, segments, padding, w_up, w_down, w_out,
    )
    frames_grad, wgrad, gup, gdown, gout, small = run_backward(
        skip_flag, gmixed, mixed_own, normed, act, ginner, gbranch, gatt, small, gone, cotangent[0],
        x_all, w_t, mixed, q_aug, k_aug, v_aug, k_t,
    )
    dp = lax.axis_size("dp")
    if dp > 8:
        groups = [list(range(i, dp, 8)) for i in range(8)]
        wgrad, gup, gdown, gout, small = (
            lax.psum(v.astype(F32), "dp", axis_index_groups=groups) for v in (wgrad, gup, gdown, gout, small)
        )
    d_query, d_key, d_value, d_up, d_down, d_out, b_q, b_v, b_u, *rest = pl.pallas_call(
        last_kernel,
        out_shape=tuple(
            S(s, F32) for s in [(width, d)] * 3 + [(d, f), (f, d), (width, d), (width,), (width,), (f,)] + [(d,)] * 6
        ),
        in_specs=[VMEM] * 5, out_specs=[VMEM] * 15, compiler_params=params, name="outputs",
    )(wgrad, gup, gdown, gout, small)
    b_down_grad, gain_two_grad, shift_two_grad, b_out_grad, gain_one_grad, shift_one_grad = rest
    return (
        layer[None], frames_grad[None], d_query.T, b_q, d_key.T, d_value.T, b_v,
        d_out, b_out_grad, gain_one_grad, shift_one_grad,
        d_up, b_u, d_down, b_down_grad, gain_two_grad, shift_two_grad,
    )


def solution(mesh):
    split = (P("dp", "mp", None), P(None, "mp"), P("mp"), P("mp", None), P())
    row, col, one, top, rep = split
    return jax.shard_map(
        shards,
        mesh=mesh,
        in_specs=(row, row, P("dp", None), P("dp", None), P("dp"), col, one, col, col, one, top, rep, rep, rep, col, one, top, rep, rep, rep),
        out_specs=(row, row, col, one, col, col, one, top, rep, rep, rep, col, one, top, rep, rep, rep),
        check_vma=False,
    )
```

```python
import functools

import jax
import jax.numpy as jnp
from jax import lax
from jax.experimental import pallas as pl
from jax.experimental.pallas import tpu as pltpu
from jax.sharding import PartitionSpec as P

HEAD_DIM = 64
F32, BF16 = jnp.float32, jnp.bfloat16
VMEM = pl.BlockSpec(memory_space=pltpu.VMEM)
SMEM = pl.BlockSpec(memory_space=pltpu.SMEM)
LIMIT = 60 << 20


def mm(a, b, ca=1, cb=0):
    return lax.dot_general(a, b, (((ca,), (cb,)), ((), ())), preferred_element_type=F32)


def row_of(ref):
    return ref[...].reshape(1, ref.shape[0])


def split3(v):
    hi = v.astype(BF16)
    rest = v - hi.astype(F32)
    mid = rest.astype(BF16)
    low = (rest - mid.astype(F32)).astype(BF16)
    return hi, mid, low


def pad_rows(parts, rows, width):
    parts = [p.astype(F32) for p in parts]
    have = sum(p.shape[0] for p in parts)
    return jnp.concatenate(parts + [jnp.zeros((rows - have, width), F32)], 0).astype(BF16)


def project(x, w_t, w_pad, bias_col, v_row, k_mask, one_hot, rows, q_aug, k_aug, v_aug, k_t, v_t):
    width = w_t.shape[0] // 3
    heads = width // HEAD_DIM
    every = mm(w_t, x, 1, 1) + bias_col
    every = jnp.concatenate([every[:width] * HEAD_DIM**-0.5, every[width:]], 0).astype(BF16)
    for h in range(heads):
        q_aug[h, 0:HEAD_DIM, rows] = every[h * HEAD_DIM : (h + 1) * HEAD_DIM]
        q_aug[h, HEAD_DIM : HEAD_DIM + 16, rows] = one_hot
        q_aug[h, HEAD_DIM + 16 :, rows] = jnp.zeros((48, x.shape[0]), BF16)
        k_t[h, :, rows] = every[width + h * HEAD_DIM : width + (h + 1) * HEAD_DIM]
        v_t[h, :, rows] = every[2 * width + h * HEAD_DIM : 2 * width + (h + 1) * HEAD_DIM]
    both = mm(x, w_pad, 1, 1)
    for h in range(heads):
        k_aug[h, rows, :] = both[:, h * 128 : (h + 1) * 128].astype(BF16) + k_mask
        at = (heads + h) * 128
        v_aug[h, rows, :] = (both[:, at : at + 128] + v_row[:, h * 128 : (h + 1) * 128]).astype(BF16)


def attend(h, cols, q_aug, k_aug, v_t):
    scores = mm(k_aug[h], q_aug[h, :, cols])
    peak = jnp.max(scores, 0, keepdims=True)
    raised = jnp.exp(scores - peak)
    summed = jnp.sum(raised, 0, keepdims=True)
    mixed = mm(v_t[h], raised.astype(BF16)) / summed
    one_hot = q_aug[h, HEAD_DIM : HEAD_DIM + 16, cols].astype(F32)[0:4]
    q_aug[h, HEAD_DIM : HEAD_DIM + 16, cols] = pad_rows((one_hot,) + split3(-(peak + jnp.log(summed))), 16, mixed.shape[1])
    return mixed.astype(BF16)


def norm_stats(v):
    centered = v - jnp.mean(v, -1, keepdims=True)
    r = lax.rsqrt(jnp.mean(centered * centered, -1, keepdims=True) + 1e-05)
    return centered * r, r


def norm_back(c, gain, hat, r):
    e = c * gain
    return r * (e - jnp.mean(e, -1, keepdims=True) - hat * jnp.mean(e * hat, -1, keepdims=True))


def feed_forward(
    skip_ref, mixed_ref, frames_ref, cot_ref, b_out, gain_one, shift_one, b_down, gain_two, shift_two, small_all,
    wout_ref, wup_ref, wdown_ref, arrive, leave, outside,
    layer_ref, gone_ref, gmixed_ref, normed_ref, act_ref, ginner_ref, gbranch_ref, gatt_ref, small_ref, slope_ref,
):
    skipped = skip_ref[0] == 1
    mixed_h, layer_h, gone_h, gmixed_h, normed_h, act_h, ginner_h, gbranch_h, gatt_h = outside
    b_out, gain_one, shift_one, b_down, gain_two, shift_two = (row_of(v) for v in (b_out, gain_one, shift_one, b_down, gain_two, shift_two))
    frames = frames_ref[...].astype(F32)
    arrive(2)
    all_out = wout_ref[...].reshape(mixed_ref.shape[0], frames.shape[1])
    attended = mm(mixed_ref[...], all_out, 0, 0) + b_out
    hat_one, r_one = norm_stats(frames + attended)
    normed = hat_one * gain_one + shift_one
    normed_ref[...] = normed.astype(BF16)
    leave(7, mixed_ref, mixed_h)
    leave(8, normed_ref, normed_h)
    parts = wup_ref.shape[0]
    arrive(0)
    for s in range(parts):
        inner = mm(normed_ref[...], wup_ref[s]) + small_all[s, 0:1, :]
        cdf = 0.5 * (1.0 + lax.erf(inner * (0.5**0.5)))
        slope_ref[s] = cdf + inner * (jnp.exp(-0.5 * inner * inner) * 0.3989422804014327)
        act_ref[s] = (inner * cdf).astype(BF16)
        leave(9, act_ref, act_h, s)
    arrive(1)
    branch = mm(act_ref[0], wdown_ref[0])
    for s in range(1, parts):
        branch = branch + mm(act_ref[s], wdown_ref[s])
    hat_two, r_two = norm_stats(normed + (branch + b_down))
    result = hat_two * gain_two + shift_two
    cot = cot_ref[...].astype(F32)
    layer_ref[...] = jnp.where(skipped, frames, result).astype(BF16)
    grad_out = jnp.where(skipped, 0.0, cot)
    grad_two = norm_back(grad_out, gain_two, hat_two, r_two)
    gbranch = grad_two.astype(BF16)
    gbranch_ref[...] = gbranch
    leave(13, layer_ref, layer_h)
    leave(14, gbranch_ref, gbranch_h)
    small_ref[10:16, :] = jnp.zeros_like(small_ref[10:16, :])
    small_ref[0:1, :] = jnp.sum(gbranch.astype(F32), 0, keepdims=True)
    small_ref[1:2, :] = jnp.sum(grad_out * hat_two, 0, keepdims=True)
    small_ref[2:3, :] = jnp.sum(grad_out, 0, keepdims=True)
    grad_normed = grad_two
    for s in range(parts):
        gact = mm(gbranch_ref[...], wdown_ref[s], 1, 1)
        ginner = (gact * slope_ref[s]).astype(BF16)
        ginner_ref[s] = ginner
        leave(15, ginner_ref, ginner_h, s)
        small_ref[6 + s : 7 + s, :] = jnp.sum(ginner.astype(F32), 0, keepdims=True)
        grad_normed = grad_normed + mm(ginner, wup_ref[s], 1, 1)
    grad_one = norm_back(grad_normed, gain_one, hat_one, r_one)
    gone_ref[...] = grad_one
    gatt = grad_one.astype(BF16)
    gatt_ref[...] = gatt
    leave(19, gone_ref, gone_h)
    leave(20, gatt_ref, gatt_h)
    small_ref[3:4, :] = jnp.sum(gatt.astype(F32), 0, keepdims=True)
    small_ref[4:5, :] = jnp.sum(grad_normed * hat_one, 0, keepdims=True)
    small_ref[5:6, :] = jnp.sum(grad_normed, 0, keepdims=True)
    gmixed_ref[...] = mm(all_out, gatt, 1, 1).astype(BF16)
    leave(21, gmixed_ref, gmixed_h)


MESH = pl.DeviceIdType.MESH
CHUNKS = 3


class Place:
    def __init__(self):
        self.d, self.z = lax.axis_index("dp"), lax.axis_index("mp")
        d, z = self.d, self.z
        self.b = d % 2
        self.p = z + self.b * (3 - 2 * z)
        self.sib = d + 1 - 2 * self.b
        self.q = (d // 2) % 4
        self.base = d - d % 8
        q = self.q
        turn, over = q + 1 - 2 * (q % 2), (q + 2) % 4
        self.near_chip = turn + self.b * (over - turn)
        self.across_chip = over + self.b * (turn - over)
        self.opposite_chip = 3 - q
        self.near = self.base + 2 * self.near_chip + self.b
        self.across = self.base + 2 * self.across_chip + self.b
        self.primary = self.p < 2
        self.rb = z // 2
        self.row = d - self.b + self.rb
        self.pp = z + self.rb * (3 - 2 * z)
        self.far = (z + 2) % 4
        self.group = jnp.where(self.primary, z, self.far)

    def own_line(self, place):
        return place + self.b * (3 - 2 * place)

    def line(self, place):
        return place + self.rb * (3 - 2 * place)

    def chip(self, k):
        return self.base + 2 * ((self.q + k) % 4) + self.b

    def other(self, k):
        return self.base + 2 * ((self.q + k) % 4) + 1 - self.b

    def barrier(self):
        sem = pltpu.get_barrier_semaphore()
        others = [((self.d), (self.z + k) % 4) for k in (1, 2, 3)]
        others += [(self.sib, (self.z + k) % 4) for k in range(4)]
        others += [(self.chip(k), self.z) for k in (1, 2, 3)]
        others += [(self.other(k), self.z) for k in (1, 2, 3)]
        for dp, mp in others:
            pl.semaphore_signal(sem, inc=1, device_id=(dp, mp), device_id_type=MESH)
        pl.semaphore_wait(sem, len(others))

    def send(self, src, dst, send_sem, recv_sem, dp, mp):
        pltpu.make_async_remote_copy(
            src_ref=src, dst_ref=dst, send_sem=send_sem, recv_sem=recv_sem, device_id=(dp, mp), device_id_type=MESH
        ).start()

    def sent(self, src, send_sem):
        pltpu.make_async_remote_copy(
            src_ref=src, dst_ref=src, send_sem=send_sem, recv_sem=send_sem, device_id=(self.sib, self.z), device_id_type=MESH
        ).wait_send()

    def got(self, dst, recv_sem):
        pltpu.make_async_remote_copy(
            src_ref=dst, dst_ref=dst, send_sem=recv_sem, recv_sem=recv_sem, device_id=(self.sib, self.z), device_id_type=MESH
        ).wait_recv()


def forward_kernel(
    skip, frames, cot, w_query, w_key, w_value, b_query, b_value, b_up, b_out, gain_one, shift_one, b_down, gain_two, shift_two,
    segments, padding, w_up, w_down, w_out,
    x_all_h, w_t_h, mixed_heads_h, mixed_own_h, q_aug_h, k_aug_h, v_aug_h, k_t_h,
    layer_h, gone_h, gmixed_h, normed_h, act_h, ginner_h, gbranch_h, gatt_h, small_sums,
    x_all, w_t, mixed_heads, mixed_own, q_aug, k_aug, v_aug, k_t,
    layer, gone, gmixed, normed, act, ginner, gbranch, gatt, out_sems,
    small_all, up_all, down_all, out_all, slope,
    relay, v_t, w_pad, kmask, hot, w_own, small_own, kmask_own, hot_own,
    small_s, small_r, mask_s, mask_r, wq_s, wq_r, x_s, x_r, relay_r, on_s, fwd_s, mix_s, mix_r, local,
    line_s, near_s, far_s, core_s, w_r,
):
    at = Place()
    heads = q_aug.shape[0]
    width = heads * HEAD_DIM
    share = frames.shape[0]
    step_rows = share // CHUNKS
    quarter = w_own.shape[0] // 4
    for i, w in enumerate((w_query, w_key, w_value)):
        w_own[i * width : (i + 1) * width] = w[...]
    small_own[...] = jnp.zeros_like(small_own)
    small_own[0:1, :] = row_of(b_up)
    small_own[1:2, 0:width] = row_of(b_query)
    values = row_of(b_value)
    small_own[1:2, 2 * width : 3 * width] = values
    for h in range(heads):
        small_own[2:3, h * 128 : h * 128 + HEAD_DIM] = values[:, h * HEAD_DIM : (h + 1) * HEAD_DIM]
        small_own[2:3, h * 128 + HEAD_DIM : h * 128 + HEAD_DIM + 3] = jnp.ones((1, 3), F32)
    at.barrier()
    primary = at.primary
    secondary = jnp.logical_not(primary)
    z = at.z

    def rows(ch):
        return pl.ds(ch * step_rows, step_rows)

    def piece(m, chip, core):
        if m == 2:
            n = w_out.shape[0] // 4
            half = w_out.shape[1] // 2
            return (pl.ds(pl.multiple_of(chip * n, 16), n), pl.ds(pl.multiple_of(core * half, 128), half))
        n = w_up.shape[0] // 8
        return (pl.ds(pl.multiple_of((2 * chip + core) * n, 16), n), slice(None))

    mats = ((w_up, up_all), (w_down, down_all), (w_out, out_all))

    for k in (1, 2, 3):
        at.send(small_own, small_all.at[z], small_s.at[k - 1], small_r.at[z], at.d, (z + k) % 4)
    wq_rows = pl.ds(pl.multiple_of(at.q * quarter, 16), quarter)
    first = jnp.where(at.p == 0, 1, at.p - 1)

    @pl.when(primary)
    def _():
        at.send(w_own.at[wq_rows], w_t.at[wq_rows], wq_s.at[0], wq_r.at[at.q], at.d, at.far)

    for ch in range(CHUNKS):
        @pl.when(at.p < 3)
        def _():
            at.send(frames.at[rows(ch)], x_all.at[z, rows(ch)], on_s.at[z, ch], x_r.at[z, ch], at.d, at.own_line(first))

        @pl.when(at.p == 3)
        def _():
            at.send(frames.at[rows(ch)], relay.at[rows(ch)], on_s.at[z, ch], relay_r.at[ch], at.d, at.own_line(2))

    @pl.when(primary)
    def _():
        for i in range(4):
            cols = slice(i * share, (i + 1) * share)
            seg, pad = segments[:, cols], padding[:, cols]
            row = lax.broadcasted_iota(jnp.int32, (128, share), 0)
            told = jnp.logical_and(row - HEAD_DIM == seg, pad == 1)
            mask = jnp.where(row < HEAD_DIM, 0.0, jnp.where(row < HEAD_DIM + 4, jnp.where(told, 0.0, -1e30), jnp.where(row < HEAD_DIM + 7, 1.0, 0.0)))
            kmask_own[cols, :] = mask.T.astype(BF16)
            hot_own[:, cols] = jnp.where(row[:16] == seg, 1.0, 0.0).astype(BF16)
        at.send(kmask_own, kmask, mask_s.at[0], mask_r.at[0], at.sib, z)
        at.send(hot_own, hot, mask_s.at[1], mask_r.at[1], at.sib, z)
        for ch in range(CHUNKS):
            at.send(frames.at[rows(ch)], x_all.at[z, rows(ch)], fwd_s.at[z, ch], x_r.at[z, ch], at.sib, z)
        pltpu.make_async_copy(w_own, w_t, local.at[2]).start()
        pltpu.make_async_copy(frames, x_all.at[z], local.at[3]).start()
        pltpu.make_async_copy(kmask_own, kmask, local.at[0]).start()
        pltpu.make_async_copy(hot_own, hot, local.at[1]).start()

    pltpu.make_async_copy(small_own, small_all.at[z], local.at[4]).start()

    def weights_first(m):
        src, dst = mats[m]
        r, c = piece(m, at.q, at.b)
        sem = w_r.at[m, z, 2 * at.q + at.b]

        @pl.when(z < 3)
        def _():
            at.send(src.at[r, c], dst.at[z, r, c], line_s.at[m, z, 0], sem, at.d, z + 1)

        @pl.when(z > 0)
        def _():
            at.send(src.at[r, c], dst.at[z, r, c], line_s.at[m, z, 1], sem, at.d, z - 1)

    def shard_at(n):
        low = z // 2
        near = z + low * (3 - 2 * z)
        s = jnp.where(near == 0, n + 1, 2 if n == 0 else (0 if n == 1 else 3))
        return s + low * (3 - 2 * s)

    def weights_line(m, n):
        dst = mats[m][1]
        s = shard_at(n)
        r, c = piece(m, at.q, at.b)
        block = dst.at[s, r, c]
        sem = w_r.at[m, s, 2 * at.q + at.b]
        at.got(block, sem)

        @pl.when(jnp.logical_and(s < z, z < 3))
        def _():
            at.send(block, block, line_s.at[m, s, 0], sem, at.d, z + 1)

        @pl.when(jnp.logical_and(s > z, z > 0))
        def _():
            at.send(block, block, line_s.at[m, s, 1], sem, at.d, z - 1)

        at.send(block, block, near_s.at[m, s], sem, at.near, z)
        at.send(block, block, far_s.at[m, s, 0], sem, at.across, z)
        at.send(block, block, core_s.at[m, s, 0], sem, at.sib, z)

    def weights_near(m, n):
        dst = mats[m][1]
        s = shard_at(n)
        r, c = piece(m, at.near_chip, at.b)
        block = dst.at[s, r, c]
        sem = w_r.at[m, s, 2 * at.near_chip + at.b]
        at.got(block, sem)
        at.send(block, block, far_s.at[m, s, 1], sem, at.across, z)
        at.send(block, block, core_s.at[m, s, 1], sem, at.sib, z)

    def weights_across(m, n):
        dst = mats[m][1]
        s = shard_at(n)
        for i, chip in ((2, at.across_chip), (3, at.opposite_chip)):
            r, c = piece(m, chip, at.b)
            block = dst.at[s, r, c]
            sem = w_r.at[m, s, 2 * chip + at.b]
            at.got(block, sem)
            at.send(block, block, core_s.at[m, s, i], sem, at.sib, z)

    for m in (2, 0, 1):
        weights_first(m)
    for m, (src, dst) in enumerate(mats):
        pltpu.make_async_copy(src, dst.at[z], local.at[5 + m]).start()

    def relay_job(ch):
        @pl.when(at.p == 2)
        def _():
            at.got(relay.at[rows(ch)], relay_r.at[ch])
            at.send(relay.at[rows(ch)], x_all.at[at.own_line(3), rows(ch)], x_s.at[ch], x_r.at[at.own_line(3), ch], at.d, at.own_line(1))

    relay_job(0)

    @pl.when(secondary)
    def _():
        at.got(w_t.at[wq_rows], wq_r.at[at.q])
        for k in (1, 2, 3):
            at.send(w_t.at[wq_rows], w_t.at[wq_rows], wq_s.at[k], wq_r.at[at.q], at.chip(k), z)

    for ch in range(1, CHUNKS):
        relay_job(ch)

    @pl.when(primary)
    def _():
        pltpu.make_async_copy(kmask_own, kmask, local.at[0]).wait()
        pltpu.make_async_copy(hot_own, hot, local.at[1]).wait()
        pltpu.make_async_copy(w_own, w_t, local.at[2]).wait()
        pltpu.make_async_copy(frames, x_all.at[z], local.at[3]).wait()

    pltpu.make_async_copy(small_own, small_all.at[z], local.at[4]).wait()
    for k in (1, 2, 3):
        at.got(small_all.at[(z + k) % 4], small_r.at[(z + k) % 4])

    @pl.when(secondary)
    def _():
        at.got(kmask, mask_r.at[0])
        at.got(hot, mask_r.at[1])
        for k in (1, 2, 3):
            other = (at.q + k) % 4
            at.got(w_t.at[pl.ds(pl.multiple_of(other * quarter, 16), quarter)], wq_r.at[other])

    w_pad[...] = jnp.zeros_like(w_pad)
    for i in range(2):
        for h in range(heads):
            w_pad[(i * heads + h) * 128 : (i * heads + h) * 128 + HEAD_DIM] = w_t[
                (i + 1) * width + h * HEAD_DIM : (i + 1) * width + (h + 1) * HEAD_DIM
            ]

    A, B, C = weights_line, weights_near, weights_across
    early = {1: ((A, 0, 0), (A, 0, 1), (A, 2, 0),), 2: ((A, 2, 1), (A, 1, 0), (A, 1, 1), (B, 0, 0), (B, 2, 0), (B, 1, 0),), 3: ((A, 0, 2), (C, 0, 0),)}
    jobs = {0: ((C, 1, 0), (B, 0, 1),), 1: ((B, 2, 1), (A, 2, 2),), 2: ((C, 2, 0),), 3: ((C, 0, 1), (B, 1, 1),), 4: ((A, 1, 2), (B, 0, 2),), 5: ((C, 2, 1), (B, 2, 2), (C, 1, 1),), 7: ((C, 0, 2), (C, 2, 2),), 9: ((B, 1, 2),)}

    def run_jobs(table, now):
        for when, todo in table.items():
            @pl.when(now == when)
            def _():
                for job, m, n in todo:
                    job(m, n)

    def gather_step(k, _):
        place = jnp.where(at.pp == 0, k, jnp.where(k == 0, 1, jnp.where(k == 1, 2, jnp.where(k == 2, 0, 3))))
        s = at.line(place)
        for ch in range(CHUNKS):
            block = x_all.at[s, rows(ch)]

            @pl.when(jnp.logical_or(k > 0, secondary))
            def _():
                at.got(block, x_r.at[s, ch])

            @pl.when(jnp.logical_and(k > 0, primary))
            def _():
                @pl.when(jnp.logical_and(at.p == 1, place >= 2))
                def _():
                    at.send(block, block, on_s.at[s, ch], x_r.at[s, ch], at.d, at.own_line(0))

                at.send(block, block, fwd_s.at[s, ch], x_r.at[s, ch], at.sib, z)

        run_jobs(early, k)
        cols = pl.ds(pl.multiple_of(s * share, share), share)
        biases = jnp.transpose(small_all[at.group])
        project(
            x_all[s], w_t[...], w_pad[...], biases[: 3 * width, 1:2], small_all[at.group, 2:3, : heads * 128], kmask[cols, :],
            hot[:, cols], cols, q_aug, k_aug, v_aug, k_t, v_t,
        )
        return 0

    lax.fori_loop(0, 4, gather_step, 0)

    def attend_step(t, _):
        turn, h = t // heads, t % heads
        i = (z + jnp.where(turn == 0, 2, jnp.where(turn == 1, 1, jnp.where(turn == 2, 3, 0)))) % 4
        cols = pl.ds(pl.multiple_of(i * share, share), share)
        mixed_heads[i, pl.ds(pl.multiple_of(h * HEAD_DIM, HEAD_DIM), HEAD_DIM), :] = attend(h, cols, q_aug, k_aug, v_t)
        mine = jnp.logical_and(primary, i == z)
        block = mixed_own.at[pl.ds(pl.multiple_of(at.group * width, 64), width)]

        @pl.when(jnp.logical_and(h == heads - 1, mine))
        def _():
            pltpu.make_async_copy(mixed_heads.at[i], block, mix_s.at[i]).start()

        @pl.when(jnp.logical_and(h == heads - 1, jnp.logical_not(mine)))
        def _():
            at.send(mixed_heads.at[i], block, mix_s.at[i], mix_r.at[at.group], at.row, i)

        run_jobs(jobs, t)
        return 0

    lax.fori_loop(0, 4 * heads, attend_step, 0)
    for job, m, n in jobs.get(99, ()):
        job(m, n)

    def leave(i, src, dst, part=None):
        if part is not None:
            src, dst, i = src.at[part], dst.at[part], i + part
        left.append((src, dst, out_sems.at[i]))
        pltpu.make_async_copy(src, dst, out_sems.at[i]).start()

    left = []
    for i, (src, dst) in enumerate((
        (x_all, x_all_h), (w_t, w_t_h), (mixed_heads, mixed_heads_h), (q_aug, q_aug_h), (k_aug, k_aug_h), (v_aug, v_aug_h), (k_t, k_t_h),
    )):
        leave(i, src, dst)

    def arrive(m):
        if m == 2:
            for g in range(4):
                mine = jnp.logical_and(primary, z == g)
                block = mixed_own.at[pl.ds(g * width, width)]

                @pl.when(mine)
                def _():
                    pltpu.make_async_copy(mixed_heads.at[g], block, mix_s.at[g]).wait()

                @pl.when(jnp.logical_not(mine))
                def _():
                    at.got(block, mix_r.at[g])

        for job, m2, n in {0: ((C, 1, 2),)}.get(m, ()):
            job(m2, n)
        src, dst = mats[m]
        pltpu.make_async_copy(src, dst.at[z], local.at[5 + m]).wait()
        for j in range(4):
            chip = (at.q + j) % 4
            r, c = piece(m, chip, 1 - at.b)
            for k in (1, 2, 3):
                s = (z + k) % 4
                at.got(dst.at[s, r, c], w_r.at[m, s, 2 * chip + 1 - at.b])

    feed_forward(
        skip, mixed_own, frames, cot, b_out, gain_one, shift_one, b_down, gain_two, shift_two, small_all,
        out_all, up_all, down_all, arrive, leave,
        (mixed_own_h, layer_h, gone_h, gmixed_h, normed_h, act_h, ginner_h, gbranch_h, gatt_h),
        layer, gone, gmixed, normed, act, ginner, gbranch, gatt, small_sums, slope,
    )
    for src, dst, sem in left:
        pltpu.make_async_copy(src, dst, sem).wait()

    for i in range(4):
        mine = jnp.logical_and(primary, z == i)

        @pl.when(jnp.logical_not(mine))
        def _():
            at.sent(mixed_heads.at[i], mix_s.at[i])

    for k in range(3):
        at.sent(small_own, small_s.at[k])
    for ch in range(CHUNKS):
        at.sent(frames.at[rows(ch)], on_s.at[z, ch])

        @pl.when(at.p == 2)
        def _():
            at.sent(relay.at[rows(ch)], x_s.at[ch])

        @pl.when(at.p == 1)
        def _():
            for place in (2, 3):
                at.sent(x_all.at[at.own_line(place), rows(ch)], on_s.at[at.own_line(place), ch])

        @pl.when(primary)
        def _():
            for s in range(4):
                at.sent(x_all.at[s, rows(ch)], fwd_s.at[s, ch])

    @pl.when(primary)
    def _():
        at.sent(kmask_own, mask_s.at[0])
        at.sent(hot_own, mask_s.at[1])
        at.sent(w_own.at[wq_rows], wq_s.at[0])

    @pl.when(secondary)
    def _():
        for k in (1, 2, 3):
            at.sent(w_t.at[wq_rows], wq_s.at[k])

    for m, (src, dst) in enumerate(mats):
        r, c = piece(m, at.q, at.b)
        block = src.at[r, c]
        for s in range(4):
            @pl.when(jnp.logical_and(s <= z, z < 3))
            def _():
                at.sent(block, line_s.at[m, s, 0])

            @pl.when(jnp.logical_and(s >= z, z > 0))
            def _():
                at.sent(block, line_s.at[m, s, 1])

            @pl.when(s != z)
            def _():
                at.sent(block, near_s.at[m, s])
                for i in range(2):
                    at.sent(block, far_s.at[m, s, i])
                for i in range(4):
                    at.sent(block, core_s.at[m, s, i])


def run_forward(
    skip, frames, cot, w_query, w_key, w_value, b_query, b_value, b_up, b_out, gain_one, shift_one, b_down, gain_two, shift_two,
    segments, padding, w_up, w_down, w_out,
):
    share, d = frames.shape
    length = segments.shape[1]
    width = w_query.shape[0]
    heads = width // HEAD_DIM
    f = w_up.shape[1]
    any_ = pl.BlockSpec(memory_space=pl.ANY)
    dma, V = pltpu.SemaphoreType.DMA, pltpu.VMEM
    return pl.pallas_call(
        forward_kernel,
        out_shape=(
            S((4, share, d)), S((3 * width, d)), S((4, width, share)), S((4 * width, share)),
            S((heads, 128, length)), S((heads, length, 128)), S((heads, length, 128)), S((heads, HEAD_DIM, length)),
            S((share, d)), S((share, d), F32), S((4 * width, share)), S((share, d)), S((4, share, f)),
            S((4, share, f)), S((share, d)), S((share, d)), S((16, d), F32),
        ),
        in_specs=[SMEM] + [VMEM] * 16 + [any_] * 3, out_specs=[any_] * 16 + [VMEM],
        scratch_shapes=[
            V((4, share, d), BF16), V((3 * width, d), BF16), V((4, width, share), BF16), V((4 * width, share), BF16),
            V((heads, 128, length), BF16), V((heads, length, 128), BF16), V((heads, length, 128), BF16), V((heads, HEAD_DIM, length), BF16),
            V((share, d), BF16), V((share, d), F32), V((4 * width, share), BF16), V((share, d), BF16), V((4, share, f), BF16),
            V((4, share, f), BF16), V((share, d), BF16), V((share, d), BF16), dma((22,)),
            V((4, 8, d), F32), V((4, d, f), BF16), V((4, f, d), BF16), V((4, width, d), BF16), V((4, share, f), F32),
            V((share, d), BF16), V((heads, HEAD_DIM, length), BF16), V((2 * heads * 128, d), BF16),
            V((length, 128), BF16), V((16, length), BF16),
            V((3 * width, d), BF16), V((8, d), F32), V((length, 128), BF16), V((16, length), BF16),
            dma((3,)), dma((4,)), dma((2,)), dma((2,)), dma((4,)), dma((4,)), dma((CHUNKS,)), dma((4, CHUNKS)), dma((CHUNKS,)),
            dma((4, CHUNKS)), dma((4, CHUNKS)), dma((4,)), dma((4,)), dma((8,)),
            dma((3, 4, 2)), dma((3, 4)), dma((3, 4, 2)), dma((3, 4, 4)), dma((3, 4, 8)),
        ],
        compiler_params=pltpu.CompilerParams(vmem_limit_bytes=LIMIT, collective_id=0, has_side_effects=True),
        name="forward",
    )(skip, frames, cot, w_query, w_key, w_value, b_query, b_value, b_up, b_out, gain_one, shift_one, b_down, gain_two, shift_two,
      segments, padding, w_up, w_down, w_out)


def attend_back(h, keys, queries, q_aug, k_aug, v_aug, k_t, do_aug, dk_acc, dv_acc):
    weights = jnp.exp(mm(k_aug[h, keys, :], q_aug[h, :, queries]))
    dv_acc[h, :, keys] += mm(do_aug[h, 0:HEAD_DIM, queries], weights.astype(BF16), 1, 1)
    grad = (weights * mm(v_aug[h, keys, :], do_aug[h, :, queries])).astype(BF16)
    dk_acc[h, :, keys] += mm(q_aug[h, 0:HEAD_DIM, queries], grad, 1, 1)
    return mm(k_t[h, :, keys], grad)


def total(first, *others):
    out = first.astype(F32)
    for other in others:
        out = out + other.astype(F32)
    return out


def backward_kernel(
    skip_ref, gmixed, mixed_own_h, normed_h, act_h, ginner_h, gbranch_h, gatt_h, small, gone_h, cot_h,
    x_all, w_t_h, mixed_heads_h, q_aug_h, k_aug_h, v_aug_h, k_t_h,
    frames_grad, dw_out, up_out, down_out, out_out, small_out,
    mixed_own, normed, act, ginner, gbranch, gatt, gone, cot, w_t, mixed_heads, q_aug, k_aug, v_aug, k_t, load_sems,
    do_in, do_aug, dk_acc, dv_acc, dq_acc, dq_keep, grads, x_sem,
    big, away, core_in, near_in, across_in, mid, z_in, bigo, core_ino, near_ino, across_ino, mido, z_ino,
    sib_in, line_in, dw_own, dw_in, dw_mid, dw_z, small_mine, small_plane, small_mid, small_z,
    gm_s, gm_r, ci_s, ci_r, nr_s, nr_r, ac_s, ac_r, z_s, z_r, ag_s, ag_r,
    part_s, part_r, line_s, line_r, dwp_s, dwp_r, dwz_s, dwz_r, dwo_s, dwo_r, dwf_s, sp_s, sp_r, sz_s, sz_r,
):
    at = Place()
    heads = q_aug.shape[0]
    width = heads * HEAD_DIM
    share = gatt.shape[0]
    length = q_aug.shape[2]
    step_rows = share // CHUNKS
    z, c, q = at.z, at.b, at.q
    primary = at.primary
    secondary = jnp.logical_not(primary)
    loads = []
    for src, dst in ((gbranch_h, gbranch), (act_h, act), (normed_h, normed), (ginner_h, ginner), (mixed_own_h, mixed_own), (gatt_h, gatt),
                     (mixed_heads_h, mixed_heads), (q_aug_h, q_aug), (k_aug_h, k_aug), (v_aug_h, v_aug), (k_t_h, k_t), (w_t_h, w_t),
                     (gone_h, gone), (cot_h, cot)):
        pltpu.make_async_copy(src, dst, load_sems.at[len(loads)]).start()
        loads.append((src, dst))

    def loaded(*numbers):
        for n in numbers:
            pltpu.make_async_copy(*loads[n], load_sems.at[n]).wait()

    at.barrier()

    for g in range(4):
        block = gmixed.at[pl.ds(g * width, width)]
        near = at.b == g // 2
        to_d = jnp.where(near, at.d, at.sib)
        to_z = jnp.where(near, g, (g + 2) % 4)
        mine = jnp.logical_and(near, z == g)

        @pl.when(mine)
        def _():
            pltpu.make_async_copy(block, do_in.at[z], gm_s.at[g]).start()

        @pl.when(jnp.logical_not(mine))
        def _():
            at.send(block, do_in.at[z], gm_s.at[g], gm_r.at[z], to_d, to_z)

    n_big = 8
    half = big.shape[1]
    quarter = half // 4
    halfo = bigo.shape[3]
    quartero = bigo.shape[2] // 4
    finals = (down_out, up_out, out_out)

    def big_rows(chip):
        return pl.ds(pl.multiple_of(chip * quarter, 16), quarter)

    def out_rows(chip):
        return pl.ds(pl.multiple_of(chip * quartero, 16), quartero)

    def weight_job(j):
        if j == 0:
            loaded(0, 1)
        if j == n_big // 2:
            loaded(2, 3)
        if j == n_big:
            loaded(4, 5)
        if j < n_big:
            kind, s = j // 4, j % 4
            made = mm(act[s], gbranch[...], 0, 0) if kind == 0 else mm(normed[...], ginner[s], 0, 0)
            made = made.astype(BF16)
            if j >= 4:
                at.sent(away.at[j % 4], ci_s.at[j - 4])

            @pl.when(c == 0)
            def _():
                big[j] = made[:half]
                away[j % 4] = made[half:]

            @pl.when(c == 1)
            def _():
                big[j] = made[half:]
                away[j % 4] = made[:half]

            at.send(away.at[j % 4], core_in.at[j], ci_s.at[j], ci_r.at[j], at.sib, z)
        else:
            for s in range(4):
                made = mm(mixed_own[s * width : (s + 1) * width, :], gatt[...])
                for i in range(2):
                    bigo[i, s] = made[:, i * halfo : (i + 1) * halfo].astype(BF16)
            at.send(bigo.at[1 - c], core_ino, ci_s.at[j], ci_r.at[j], at.sib, z)

    def core_job(j):
        at.got(core_in.at[j] if j < n_big else core_ino, ci_r.at[j])
        if j < n_big:
            big[j] = total(big[j], core_in[j]).astype(BF16)
        else:
            bigo[c] = total(bigo[c], core_ino[...]).astype(BF16)
        for i, chip in enumerate((at.near_chip, at.opposite_chip)):
            if j < n_big:
                at.send(big.at[j, big_rows(chip)], near_in.at[i, j], nr_s.at[j, i], nr_r.at[j, i], at.near, z)
            else:
                at.send(bigo.at[c, :, out_rows(chip)], near_ino.at[i], nr_s.at[j, i], nr_r.at[j, i], at.near, z)

    def near_job(j):
        if j < n_big:
            for i in range(2):
                at.got(near_in.at[i, j], nr_r.at[j, i])
            near_in[1, j] = total(big[j, big_rows(at.across_chip)], near_in[1, j]).astype(BF16)
            at.send(near_in.at[1, j], across_in.at[j], ac_s.at[j], ac_r.at[j], at.across, z)
        else:
            for i in range(2):
                at.got(near_ino.at[i], nr_r.at[j, i])
            near_ino[1] = total(bigo[c, :, out_rows(at.across_chip)], near_ino[1]).astype(BF16)
            at.send(near_ino.at[1], across_ino, ac_s.at[j], ac_r.at[j], at.across, z)

    def plane_job(j):
        if j < n_big:
            kind, s = j // 4, j % 4
            at.got(across_in.at[j], ac_r.at[j])
            mid[j] = total(big[j, big_rows(q)], near_in[0, j], across_in[j]).astype(BF16)

            @pl.when(z != s)
            def _():
                slot = 3 - (s - z + 4) % 4
                at.send(mid.at[j], z_in.at[slot, kind], z_s.at[j], z_r.at[kind, slot], at.d, s)
        else:
            at.got(across_ino, ac_r.at[j])
            mido[...] = total(bigo[c, :, out_rows(q)], near_ino[0], across_ino[...]).astype(BF16)
            for s in range(4):
                @pl.when(z != s)
                def _():
                    slot = 3 - (s - z + 4) % 4
                    at.send(mido.at[s], z_ino.at[slot], z_s.at[j + s], z_r.at[2, slot], at.d, s)

    def final_piece(kind, chip, core):
        if kind < 2:
            return finals[kind].at[pl.ds(pl.multiple_of(core * half + chip * quarter, 16), quarter)]
        return out_out.at[out_rows(chip), pl.ds(pl.multiple_of(core * halfo, 128), halfo)]

    def final_job(kind):
        for k in range(3):
            at.got(z_in.at[k, kind] if kind < 2 else z_ino.at[k], z_r.at[kind, k])
        piece = final_piece(kind, q, c)
        if kind < 2:
            piece[...] = total(mid[4 * kind + z], z_in[0, kind], z_in[1, kind], z_in[2, kind]).astype(BF16)
        else:
            piece[...] = total(mido[z], z_ino[0], z_ino[1], z_ino[2]).astype(BF16)
        sem = ag_r.at[kind, 2 * q + c]
        at.send(piece, piece, ag_s.at[kind, 0], sem, at.near, z)
        at.send(piece, piece, ag_s.at[kind, 1], sem, at.across, z)
        at.send(piece, piece, ag_s.at[kind, 2], sem, at.sib, z)

    def pass_job(kind):
        piece = final_piece(kind, at.near_chip, c)
        sem = ag_r.at[kind, 2 * at.near_chip + c]
        at.got(piece, sem)
        at.send(piece, piece, ag_s.at[kind, 3], sem, at.across, z)
        at.send(piece, piece, ag_s.at[kind, 4], sem, at.sib, z)

    def share_job(kind):
        for i, chip in enumerate((at.across_chip, at.opposite_chip)):
            piece = final_piece(kind, chip, c)
            sem = ag_r.at[kind, 2 * chip + c]
            at.got(piece, sem)
            at.send(piece, piece, ag_s.at[kind, 5 + i], sem, at.sib, z)

    def end_job(kind):
        for k in range(4):
            chip = (q + k) % 4
            at.got(final_piece(kind, chip, 1 - c), ag_r.at[kind, 2 * chip + 1 - c])

    for j in range(n_big + 1):
        weight_job(j)
        if j >= 2:
            core_job(j - 2)
    core_job(n_big - 1)
    core_job(n_big)
    x_here, part = core_in.at[0:4], core_in.at[4:8]
    pltpu.make_async_copy(x_all, x_here, x_sem.at[0]).start()

    late = at.rb
    side = length // 2

    def prepare(i):
        mine = jnp.logical_and(primary, z == i)

        @pl.when(mine)
        def _():
            pltpu.make_async_copy(gmixed.at[pl.ds(pl.multiple_of(i * width, 64), width)], do_in.at[i], gm_s.at[i]).wait()

        @pl.when(jnp.logical_not(mine))
        def _():
            at.got(do_in.at[i], gm_r.at[i])

        cols = pl.ds(pl.multiple_of(i * share, share), share)
        for h in range(heads):
            hs = slice(h * HEAD_DIM, (h + 1) * HEAD_DIM)
            do = do_in[i, hs, :]
            do_aug[h, 0:HEAD_DIM, cols] = do
            inner = jnp.sum(do.astype(F32) * mixed_heads[i, hs, :].astype(F32), 0, keepdims=True)
            do_aug[h, HEAD_DIM : HEAD_DIM + 16, cols] = pad_rows(split3(-inner), 16, share)
            do_aug[h, HEAD_DIM + 16 :, cols] = jnp.zeros((48, share), BF16)

    def half_row(n):
        return pl.ds(pl.multiple_of(n * side, side), side)

    dk_acc[...] = jnp.zeros_like(dk_acc)
    dv_acc[...] = jnp.zeros_like(dv_acc)

    N, M, Q, U, V = near_job, plane_job, final_job, pass_job, share_job
    jobs = {-1: ((N, 0), (N, 1),), 0: ((N, 2), (M, 0),), 1: ((M, 1),), 2: ((N, 3), (M, 2),), 4: ((N, 4), (M, 3),), 6: ((N, 5), (M, 4),), 8: ((N, 6), (M, 5),), 50: ((Q, 0),), 10: ((N, 7), (M, 6),)}

    def attention_step(t, _):
        last = t >= 3 * heads
        h = jnp.where(last, t - 3 * heads, t // 3)
        turn = jnp.where(last, 3, t % 3)
        keys = half_row(jnp.where(jnp.logical_or(turn == 0, last), late, 1 - late))
        queries = half_row(jnp.where(turn < 2, 1 - late, late))
        dq = attend_back(h, keys, queries, q_aug, k_aug, v_aug, k_t, do_aug, dk_acc, dv_acc)
        hs = pl.ds(pl.multiple_of(h * HEAD_DIM, HEAD_DIM), HEAD_DIM)

        @pl.when(turn == 0)
        def _():
            dq_acc[...] = dq

        @pl.when(turn == 1)
        def _():
            grads[hs, queries] = ((dq_acc[...] + dq).astype(BF16).astype(F32) * HEAD_DIM**-0.5).astype(BF16)

        @pl.when(turn == 2)
        def _():
            dq_keep[h] = dq

        @pl.when(turn == 3)
        def _():
            grads[hs, queries] = ((dq_keep[h] + dq).astype(BF16).astype(F32) * HEAD_DIM**-0.5).astype(BF16)

        for when, todo in jobs.items():
            if 0 <= when < 4 * heads:
                @pl.when(t == when)
                def _():
                    for job, j in todo:
                        job(j)

        return 0

    def rows(ch):
        return pl.ds(ch * step_rows, step_rows)

    def part_job(s):
        part[s] = mm(grads[:, pl.ds(pl.multiple_of(s * share, share), share)], w_t[...], 0, 0).astype(BF16)

        @pl.when(secondary)
        def _():
            for ch in range(CHUNKS):
                at.send(part.at[s, rows(ch)], sib_in.at[s, rows(ch)], part_s.at[s, ch], part_r.at[s, ch], at.sib, z)

    def line_job(place):
        s = at.line(place)
        for ch in range(CHUNKS):
            here = (s, rows(ch))

            @pl.when(jnp.logical_and(primary, place != at.p))
            def _():
                at.got(sib_in.at[here], part_r.at[s, ch])

                @pl.when(jnp.logical_and(at.p == 1, place >= 2))
                def _():
                    at.got(line_in.at[here], line_r.at[s, ch])
                    part[here] = total(part[here], sib_in[here], line_in[here]).astype(BF16)
                    at.send(part.at[here], line_in.at[here], line_s.at[s, ch], line_r.at[s, ch], at.d, at.own_line(2))

                @pl.when(jnp.logical_or(at.p == 0, place == 0))
                def _():
                    part[here] = total(part[here], sib_in[here]).astype(BF16)
                    at.send(part.at[here], line_in.at[here], line_s.at[s, ch], line_r.at[s, ch], at.d, at.own_line(1 - at.p))

    def finish(n):
        cols = half_row(n)
        for h in range(heads):
            grads[width + h * HEAD_DIM : width + (h + 1) * HEAD_DIM, cols] = dk_acc[h, :, cols].astype(BF16)
            grads[2 * width + h * HEAD_DIM : 2 * width + (h + 1) * HEAD_DIM, cols] = dv_acc[h, :, cols].astype(BF16)

    loaded(6, 7, 8, 9, 10, 11)
    for i in range(4):
        prepare(i)
    for job, j in jobs.get(-1, ()):
        job(j)
    lax.fori_loop(0, 3 * heads, attention_step, 0)
    finish(1 - late)
    for place in (3, 2):
        part_job(at.line(place))

    @pl.when(at.p == 0)
    def _():
        line_job(3)
        line_job(2)

    for job, j in jobs.get(50, ()):
        job(j)
    lax.fori_loop(3 * heads, 4 * heads, attention_step, 0)
    finish(late)
    for place in (0, 1):
        part_job(at.line(place))

    @pl.when(at.p == 0)
    def _():
        line_job(1)

    @pl.when(at.p == 1)
    def _():
        line_job(0)

    small_mine[...] = small[...]
    small_mine[pl.ds(10 + at.group, 1), 0 : 3 * width] = mm(jnp.ones((8, length), BF16), grads[...], 1, 1)[0:1]
    at.send(small_mine, small_plane.at[0], sp_s.at[0], sp_r.at[0], at.sib, z)
    for k in (1, 2, 3):
        at.send(small_mine, small_plane.at[4 - k], sp_s.at[k], sp_r.at[4 - k], at.chip(k), z)
        at.send(small_mine, small_plane.at[7 - k], sp_s.at[3 + k], sp_r.at[7 - k], at.other(k), z)

    pltpu.make_async_copy(x_all, x_here, x_sem.at[0]).wait()
    made = mm(grads[:, 0:share], x_here[0])
    for s in range(1, 4):
        made = made + mm(grads[:, s * share : (s + 1) * share], x_here[s])
    made = made.astype(BF16)
    fourth = made.shape[0] // 4
    for i in range(4):
        dw_own[i] = made[i * fourth : (i + 1) * fourth]
    at.send(dw_own.at[at.near_chip], dw_in.at[0], dwp_s.at[0], dwp_r.at[0], at.near, z)
    at.send(dw_own.at[at.opposite_chip], dw_in.at[1], dwp_s.at[1], dwp_r.at[1], at.near, z)

    def dw_rows(i):
        return pl.ds(pl.multiple_of(i * fourth, 16), fourth)

    def small_sum(_):
        for k in range(7):
            at.got(small_plane.at[k], sp_r.at[k])
        small_mid[...] = total(small_mine[...], *(small_plane[k] for k in range(7)))
        for k in (1, 2, 3):
            at.send(small_mid, small_z.at[3 - k], sz_s.at[k - 1], sz_r.at[3 - k], at.d, (z + k) % 4)

    def small_end(_):
        for k in range(3):
            at.got(small_z.at[k], sz_r.at[k])
        small_out[...] = total(small_mid[...], small_z[0], small_z[1], small_z[2])

    def onward(place):
        @pl.when(at.p == 1)
        def _():
            line_job(place)

        if place == 3:
            @pl.when(at.p == 2)
            def _():
                s = at.own_line(3)
                for ch in range(CHUNKS):
                    here = (s, rows(ch))
                    at.got(line_in.at[here], line_r.at[s, ch])
                    at.send(line_in.at[here], line_in.at[here], line_s.at[s, ch], line_r.at[s, ch], at.d, s)

    def dw_across(_):
        for k in range(2):
            at.got(dw_in.at[k], dwp_r.at[k])
        dw_in[1] = total(dw_own[at.across_chip], dw_in[1]).astype(BF16)
        at.send(dw_in.at[1], dw_in.at[2], dwp_s.at[2], dwp_r.at[2], at.across, z)

    def dw_plane(_):
        at.got(dw_in.at[2], dwp_r.at[2])
        dw_mid[...] = total(dw_own[q], dw_in[0], dw_in[2]).astype(BF16)

        @pl.when(secondary)
        def _():
            at.send(dw_mid, dw_z, dwz_s.at[0], dwz_r.at[0], at.d, at.far)

    def dw_final(_):
        @pl.when(primary)
        def _():
            at.got(dw_z, dwz_r.at[0])
            piece = dw_out.at[dw_rows(q)]
            piece[...] = total(dw_mid[...], dw_z[...]).astype(BF16)
            at.send(piece, piece, dwo_s.at[0], dwo_r.at[q], at.near, z)
            at.send(piece, piece, dwo_s.at[1], dwo_r.at[q], at.across, z)
            at.send(piece, piece, dwo_s.at[2], dwo_r.at[q], at.sib, z)

    def dw_pass(_):
        @pl.when(primary)
        def _():
            i = at.near_chip
            piece = dw_out.at[dw_rows(i)]
            at.got(piece, dwo_r.at[i])
            at.send(piece, piece, dwo_s.at[3], dwo_r.at[i], at.across, z)
            at.send(piece, piece, dwf_s.at[0], dwo_r.at[i], at.sib, z)

    for job, j in ((onward, 3), (M, 7), (dw_across, 0), (small_sum, 0), (N, 8), (dw_plane, 0), (M, 8), (onward, 2), (U, 0), (dw_final, 0), (Q, 1), (dw_pass, 0), (U, 1), (Q, 2), (V, 0), (small_end, 0), (U, 2), (V, 1), (V, 2)):
        job(j)

    skipped = skip_ref[0] == 1
    loaded(12, 13)
    for ch in range(CHUNKS):
        at.got(line_in.at[z, rows(ch)], line_r.at[z, ch])

    @pl.when(primary)
    def _():
        for ch in range(CHUNKS):
            at.got(sib_in.at[z, rows(ch)], part_r.at[z, ch])
        grad = gone[...] + total(part[z], sib_in[z], line_in[z])
        frames_grad[...] = jnp.where(skipped, cot[...].astype(F32), grad).astype(BF16)

    @pl.when(secondary)
    def _():
        grad = gone[...] + line_in[z].astype(F32)
        frames_grad[...] = jnp.where(skipped, cot[...].astype(F32), grad).astype(BF16)


    @pl.when(primary)
    def _():
        for k, i in ((1, at.across_chip), (2, at.opposite_chip)):
            piece = dw_out.at[dw_rows(i)]
            at.got(piece, dwo_r.at[i])
            at.send(piece, piece, dwf_s.at[k], dwo_r.at[i], at.sib, z)

    @pl.when(secondary)
    def _():
        for i in range(4):
            at.got(dw_out.at[dw_rows(i)], dwo_r.at[i])

    for kind in range(3):
        end_job(kind)

    for g in range(4):
        mine = jnp.logical_and(primary, z == g)

        @pl.when(jnp.logical_not(mine))
        def _():
            at.sent(gmixed.at[pl.ds(g * width, width)], gm_s.at[g])

    for j in range(n_big):
        if j >= 4:
            at.sent(core_in.at[j], ci_s.at[j])
        for k in range(2):
            at.sent(near_in.at[k, j], nr_s.at[j, k])
        at.sent(across_in.at[j], ac_s.at[j])

        @pl.when(z != j % 4)
        def _():
            at.sent(mid.at[j], z_s.at[j])

    at.sent(core_ino, ci_s.at[n_big])
    for k in range(2):
        at.sent(near_ino.at[k], nr_s.at[n_big, k])
    at.sent(across_ino, ac_s.at[n_big])
    for s in range(4):
        @pl.when(z != s)
        def _():
            at.sent(mido.at[s], z_s.at[n_big + s])

    for kind in range(3):
        for k in range(7):
            at.sent(final_piece(kind, q, c), ag_s.at[kind, k])
    for k in range(7):
        at.sent(small_mine, sp_s.at[k])
    for k in range(3):
        at.sent(small_mid, sz_s.at[k])
        at.sent(dw_mid, dwp_s.at[k])

    @pl.when(secondary)
    def _():
        at.sent(dw_mid, dwz_s.at[0])
        for s in range(4):
            for ch in range(CHUNKS):
                at.sent(part.at[s, rows(ch)], part_s.at[s, ch])

    @pl.when(primary)
    def _():
        for k in range(4):
            at.sent(dw_mid, dwo_s.at[k])
        for k in range(3):
            at.sent(dw_mid, dwf_s.at[k])
        for k in (1, 2, 3):
            for ch in range(CHUNKS):
                s = at.line((at.p + k) % 4)
                at.sent(part.at[s, rows(ch)], line_s.at[s, ch])

    @pl.when(at.p == 2)
    def _():
        for ch in range(CHUNKS):
            at.sent(line_in.at[at.own_line(3), rows(ch)], line_s.at[at.own_line(3), ch])


def run_backward(skip, gmixed, mixed_own, normed, act, ginner, gbranch, gatt, small, gone, cot,
                 x_all, w_t, mixed_heads, q_aug, k_aug, v_aug, k_t):
    share, d = gatt.shape
    any_ = pl.BlockSpec(memory_space=pl.ANY)
    f = act.shape[2]
    heads, _, length = q_aug.shape
    width = heads * HEAD_DIM
    dma, V = pltpu.SemaphoreType.DMA, pltpu.VMEM
    hd, hf, ho = d // 2, f // 2, d // 2
    return pl.pallas_call(
        backward_kernel,
        out_shape=(
            S((share, d)), S((3 * width, d)), S((d, f)), S((f, d)), S((width, d)), S((16, d), F32),
        ),
        in_specs=[SMEM] + [any_] * 7 + [VMEM] + [any_] * 9, out_specs=[VMEM] * 6,
        scratch_shapes=[
            V((4 * width, share), BF16), V((share, d), BF16), V((4, share, f), BF16), V((4, share, f), BF16), V((share, d), BF16),
            V((share, d), BF16), V((share, d), F32), V((share, d), BF16), V((3 * width, d), BF16), V((4, width, share), BF16),
            V((heads, 128, length), BF16), V((heads, length, 128), BF16), V((heads, length, 128), BF16),
            V((heads, HEAD_DIM, length), BF16), dma((14,)),
            V((4, width, share), BF16), V((heads, 128, length), BF16),
            V((heads, HEAD_DIM, length), F32), V((heads, HEAD_DIM, length), F32),
            V((HEAD_DIM, length // 2), F32), V((heads, HEAD_DIM, length // 2), F32), V((3 * width, length), BF16), dma((1,)),
            V((8, hd, d), BF16), V((4, hd, d), BF16), V((8, hd, d), BF16), V((2, 8, hd // 4, d), BF16), V((8, hd // 4, d), BF16), V((8, hd // 4, d), BF16),
            V((3, 2, hd // 4, d), BF16),
            V((2, 4, width, ho), BF16), V((4, width, ho), BF16), V((2, 4, width // 4, ho), BF16), V((4, width // 4, ho), BF16), V((4, width // 4, ho), BF16),
            V((3, width // 4, ho), BF16),
            V((4, share, d), BF16), V((4, share, d), BF16),
            V((4, 3 * width // 4, d), BF16), V((3, 3 * width // 4, d), BF16), V((3 * width // 4, d), BF16), V((3 * width // 4, d), BF16),
            V((16, d), F32), V((7, 16, d), F32), V((16, d), F32), V((3, 16, d), F32),
            dma((4,)), dma((4,)), dma((9,)), dma((9,)), dma((9, 2)), dma((9, 2)), dma((9,)), dma((9,)), dma((12,)), dma((3, 3)),
            dma((3, 7)), dma((3, 8)),
            dma((4, CHUNKS)), dma((4, CHUNKS)), dma((4, CHUNKS)), dma((4, CHUNKS)), dma((3,)), dma((3,)), dma((1,)), dma((1,)),
            dma((4,)), dma((4,)), dma((3,)), dma((7,)), dma((7,)), dma((3,)), dma((3,)),
        ],
        compiler_params=pltpu.CompilerParams(vmem_limit_bytes=LIMIT, collective_id=1, has_side_effects=True),
        name="attention_backward",
    )(skip, gmixed, mixed_own, normed, act, ginner, gbranch, gatt, small, gone, cot,
      x_all, w_t, mixed_heads, q_aug, k_aug, v_aug, k_t)


def last_kernel(dw, up, down, out, small, layer, frames, layer_out, frames_out, *outs):
    layer_out[...] = layer[...]
    frames_out[...] = frames[...]
    z = lax.axis_index("mp")
    d_query, d_key, d_value, d_up, d_down, d_out, b_query, b_value, b_up = outs[:9]
    width = d_out.shape[0]
    for i, target in enumerate((d_query, d_key, d_value)):
        target[...] = dw[i * width : (i + 1) * width].astype(F32)
    d_up[...] = up[...].astype(F32)
    d_down[...] = down[...].astype(F32)
    d_out[...] = out[...].astype(F32)
    bias = small[pl.ds(10 + z, 1), :]
    b_query[...] = bias[:, 0:width].reshape(width)
    b_value[...] = bias[:, 2 * width : 3 * width].reshape(width)
    b_up[...] = small[pl.ds(6 + z, 1), :].reshape(small.shape[1])
    for i, target in enumerate(outs[9:]):
        target[...] = small[i : i + 1, :].reshape(small.shape[1])


def S(shape, dtype=BF16):
    return jax.ShapeDtypeStruct(shape, dtype)


def shards(
    frames, cotangent, segments, padding, skip_flag, w_query, b_query, w_key, w_value, b_value,
    w_out, b_out, gain_one, shift_one, w_up, b_up, w_down, b_down, gain_two, shift_two,
):
    mp = lax.axis_size("mp")
    share, d = frames.shape[1:]
    length = segments.shape[1]
    width = w_query.shape[1]
    heads = width // HEAD_DIM
    params = pltpu.CompilerParams(vmem_limit_bytes=LIMIT)
    own = frames[0]
    f = w_up.shape[1]
    (
        x_all, w_t, mixed, mixed_own, q_aug, k_aug, v_aug, k_t,
        layer, gone, gmixed, normed, act, ginner, gbranch, gatt, small,
    ) = run_forward(
        skip_flag, own, cotangent[0], w_query.T, w_key.T, w_value.T, b_query, b_value, b_up,
        b_out, gain_one, shift_one, b_down, gain_two, shift_two, segments, padding, w_up, w_down, w_out,
    )
    frames_grad, wgrad, gup, gdown, gout, small = run_backward(
        skip_flag, gmixed, mixed_own, normed, act, ginner, gbranch, gatt, small, gone, cotangent[0],
        x_all, w_t, mixed, q_aug, k_aug, v_aug, k_t,
    )
    dp = lax.axis_size("dp")
    if dp > 8:
        groups = [list(range(i, dp, 8)) for i in range(8)]
        wgrad, gup, gdown, gout, small = (
            lax.psum(v.astype(F32), "dp", axis_index_groups=groups) for v in (wgrad, gup, gdown, gout, small)
        )
    layer, frames_grad, d_query, d_key, d_value, d_up, d_down, d_out, b_q, b_v, b_u, *rest = pl.pallas_call(
        last_kernel,
        out_shape=(S((share, d)), S((share, d))) + tuple(
            S(s, F32) for s in [(width, d)] * 3 + [(d, f), (f, d), (width, d), (width,), (width,), (f,)] + [(d,)] * 6
        ),
        in_specs=[VMEM] * 7, out_specs=[VMEM] * 17, compiler_params=params, name="outputs",
    )(wgrad, gup, gdown, gout, small, layer, frames_grad)
    b_down_grad, gain_two_grad, shift_two_grad, b_out_grad, gain_one_grad, shift_one_grad = rest
    return (
        layer[None], frames_grad[None], d_query.T, b_q, d_key.T, d_value.T, b_v,
        d_out, b_out_grad, gain_one_grad, shift_one_grad,
        d_up, b_u, d_down, b_down_grad, gain_two_grad, shift_two_grad,
    )


def solution(mesh):
    split = (P("dp", "mp", None), P(None, "mp"), P("mp"), P("mp", None), P())
    row, col, one, top, rep = split
    return jax.shard_map(
        shards,
        mesh=mesh,
        in_specs=(row, row, P("dp", None), P("dp", None), P("dp"), col, one, col, col, one, top, rep, rep, rep, col, one, top, rep, rep, rep),
        out_specs=(row, row, col, one, col, col, one, top, rep, rep, rep, col, one, top, rep, rep, rep),
        check_vma=False,
    )
```
